32 devices in a mesh: dp: 8 (over y, x, core), mp: 4 (over z).
Axes of the slice: x: 2, y: 2, z: 4, core: 2. Of those that a mesh axis runs over, the one named last changes fastest.
Arguments:
- query_states: bfloat16 [64, 128, 768], P(('dp', 'mp'))
- passage_states: bfloat16 [32, 512, 768], P(('dp', 'mp'))
- query_lengths: int32 [64], P('dp'), may hold values from 16 to 128, as said below
- passage_lengths: int32 [32], P('dp'), may hold values from 64 to 512, as said below
- query_count: int32 [32], replicated, may hold values from 0 to 2, as said below
- passage_count: int32 [32], replicated, may hold values from 0 to 1, as said below
- positive: int32 [64], P(('dp', 'mp')), may hold values from 0 to 31, as said below
- query_key_value_matrix: bfloat16 [2, 3, 768, 768], P(None, None, None, 'mp'), may hold values from -0.21875 to 0.21875
- qv_bias: bfloat16 [2, 2, 768], P(None, None, 'mp'), may hold values from -4 to 4
- out_weight: bfloat16 [2, 768, 768], P(None, 'mp'), may hold values from -0.4375 to 0.4375
- out_bias: bfloat16 [2, 768], replicated, may hold values from -1.5 to 1.5
- norm_gain: bfloat16 [2, 2, 768], replicated, may hold values from 0.5 to 1.5
- norm_bias: bfloat16 [2, 2, 768], replicated, may hold values from -1.5 to 1.5
- up_matrix: bfloat16 [2, 768, 3072], P(None, None, 'mp'), may hold values from -0.21875 to 0.21875
- up_bias: bfloat16 [2, 3072], P(None, 'mp'), may hold values from -4 to 4
- down_matrix: bfloat16 [2, 3072, 768], P(None, 'mp'), may hold values from -0.109375 to 0.109375
- down_bias: bfloat16 [2, 768], replicated, may hold values from -1.5 to 1.5
Outputs:
- loss: float32 [], replicated
- query_grad: float32 [64, 128, 768], P(('dp', 'mp'))
- passage_grad: float32 [32, 512, 768], P(('dp', 'mp'))
- qkv_weight_grad: float32 [2, 3, 768, 768], P(None, None, None, 'mp')
- qv_bias_grad: float32 [2, 2, 768], P(None, None, 'mp')
- out_weight_grad: float32 [2, 768, 768], P(None, 'mp')
- out_bias_grad: float32 [2, 768], replicated
- norm_gain_grad: float32 [2, 2, 768], replicated
- norm_bias_grad: float32 [2, 2, 768], replicated
- up_weight_grad: float32 [2, 768, 3072], P(None, None, 'mp')
- up_bias_grad: float32 [2, 3072], P(None, 'mp')
- down_weight_grad: float32 [2, 3072, 768], P(None, 'mp')
- down_bias_grad: float32 [2, 768], replicated
The draws below stay inside these ranges and needn't reach their ends.
Inputs may be any that keep to these rules, and one draw needn't show every extreme that they name: `query_count`: live queries of each device are its first slots; some device has 2. `passage_count`: live passages of each device are its first slots; the last device has 1. Each index names a live passage; some query's positive is the last passage. `query_lengths`: valid tokens come first; some query has all 128. `passage_lengths`: valid tokens come first; some passage has all 512.
All inputs are finite; a program needn't handle non-finite values.
Results may differ from the reference program's by a relative error of at most 0.017.
Values may be sent and summed in bfloat16 or wider, within the bound.
A program may use at most 256 MiB of HBM per device.

```python
import math
from functools import partial
import jax
import jax.numpy as jnp
from jax import lax

D = 768
HEADS = 12
HEAD_DIM = 64
FF = 3072
LAYERS = 2
LQ = 128
LP = 512
Q_DEV = 2
P_DEV = 1
QUERIES = 64
PASSAGES = 32
GRAD_SCALE = 8192


def passage_live(key):
    key = jax.random.fold_in(key, 101)
    first_key, second_key = jax.random.split(key)
    devices_all = PASSAGES // P_DEV
    counts = jax.random.randint(first_key, (devices_all,), 0, P_DEV + 1)
    chosen = jax.random.randint(second_key, (), 0, devices_all)
    device_ids = jnp.arange(devices_all)
    full = (device_ids == chosen) | (device_ids == devices_all - 1)
    return jnp.where(full, P_DEV, counts).astype(jnp.int32)


def draw_passage_count(key, part):
    return passage_live(key)


def draw_positive(key, part):
    counts = passage_live(key)
    key = jax.random.fold_in(key, 7)
    first_key, second_key = jax.random.split(key)
    pass_ids = jnp.arange(PASSAGES, dtype=jnp.int32)
    live_pass = (pass_ids % P_DEV < counts[pass_ids // P_DEV]).astype(jnp.int32)
    live_total = jnp.sum(live_pass)
    picks = jax.random.randint(first_key, (QUERIES,), 0, live_total)
    running = jnp.cumsum(live_pass)
    indices = jnp.sum((running[None, :] <= picks[:, None]).astype(jnp.int32), axis=1).astype(jnp.int32)
    chosen = jax.random.randint(second_key, (), 0, QUERIES)
    return jnp.where(jnp.arange(QUERIES) == chosen, PASSAGES - 1, indices).astype(jnp.int32)


def draw_query_count(key, part):
    key = jax.random.fold_in(key, 5)
    first_key, second_key = jax.random.split(key)
    devices_all = QUERIES // Q_DEV
    counts = jax.random.randint(first_key, (devices_all,), 0, Q_DEV + 1)
    chosen = jax.random.randint(second_key, (), 0, devices_all)
    return jnp.where(jnp.arange(devices_all) == chosen, Q_DEV, counts).astype(jnp.int32)


def ragged_lengths(key, num_seqs, seq_len):
    first_key, second_key = jax.random.split(key)
    lengths = jax.random.randint(first_key, (num_seqs,), max(1, seq_len // 8), seq_len + 1)
    chosen = jax.random.randint(second_key, (), 0, num_seqs)
    return jnp.where(jnp.arange(num_seqs) == chosen, seq_len, lengths).astype(jnp.int32)


def draw_query_lengths(key, part):
    key = jax.random.fold_in(key, 9)
    return ragged_lengths(key, QUERIES, LQ)


def draw_passage_lengths(key, part):
    key = jax.random.fold_in(key, 13)
    return ragged_lengths(key, PASSAGES, LP)


def token_states_normal(key, num_seqs, seq_len):
    first_key, second_key = jax.random.split(key)
    common = jax.random.normal(first_key, (num_seqs, 1, D), jnp.float32)
    noise = jax.random.normal(second_key, (num_seqs, seq_len, D), jnp.float32)
    return 0.8 * common + 0.6 * noise


def draw_query_states(key, part):
    key = jax.random.fold_in(key, 21)
    values = token_states_normal(key, QUERIES, LQ)
    return values.astype(jnp.bfloat16)


def draw_passage_states(key, part):
    key = jax.random.fold_in(key, 23)
    values = token_states_normal(key, PASSAGES, LP)
    return values.astype(jnp.bfloat16)


def level_of(own_key, extent, cuts, low, top_value):
    loudness = 1.0
    for axis_at, shards_of in cuts:
        steps = jax.random.uniform(jax.random.fold_in(jax.random.fold_in(own_key, 6), axis_at), (shards_of,), jnp.float32, low / len(cuts), top_value / len(cuts))
        loudness = loudness * jnp.repeat(jnp.exp(steps), extent[axis_at] // shards_of).reshape((-1,) + (1,) * (len(extent) - 1 - axis_at))
    return loudness


def bell_draw(rng, dims, scale, most, shards=(), held_as=jnp.bfloat16):
    level = level_of(rng, dims, shards, -0.22, 0.18) if shards else 1.0
    array = jax.random.normal(rng, dims, jnp.float32) * scale * level
    return jnp.minimum(jnp.maximum(array, -most), most).astype(held_as)


def setup_inputs(seed: int = 0) -> dict:
    arg_keys = jax.random.split(jax.random.key(seed), 18)
    query_states = draw_query_states(jax.random.fold_in(arg_keys[17], 71), 0)
    passage_states = draw_passage_states(jax.random.fold_in(arg_keys[17], 71), 0)
    query_lengths = draw_query_lengths(jax.random.fold_in(arg_keys[17], 71), 0)
    passage_lengths = draw_passage_lengths(jax.random.fold_in(arg_keys[17], 71), 0)
    query_count = draw_query_count(jax.random.fold_in(arg_keys[17], 71), 0)
    passage_count = draw_passage_count(jax.random.fold_in(arg_keys[17], 71), 0)
    positive = draw_positive(jax.random.fold_in(arg_keys[17], 71), 0)
    query_key_value_matrix = bell_draw(arg_keys[7], (LAYERS, 3, D, D), D ** -0.5, 0.21875, ((3, 4),))
    qv_bias = bell_draw(arg_keys[8], (LAYERS, 2, D), 0.3, 4.0, ((2, 4),))
    out_weight = bell_draw(arg_keys[9], (LAYERS, D, D), (D // 4) ** -0.5, 0.4375, ((1, 4),))
    out_bias = bell_draw(arg_keys[10], (LAYERS, D), 0.1, 1.5)
    norm_gain = jnp.clip(1.0 + 0.1 * jax.random.normal(arg_keys[11], (LAYERS, 2, D), jnp.float32), 0.5, 1.5).astype(jnp.bfloat16)
    norm_bias = bell_draw(arg_keys[12], (LAYERS, 2, D), 0.1, 1.5)
    up_matrix = bell_draw(arg_keys[13], (LAYERS, D, FF), D ** -0.5, 0.21875, ((2, 4),))
    up_bias = bell_draw(arg_keys[14], (LAYERS, FF), 0.3, 4.0, ((1, 4),))
    down_matrix = bell_draw(arg_keys[15], (LAYERS, FF, D), FF ** -0.5, 0.109375, ((1, 4),))
    down_bias = bell_draw(arg_keys[16], (LAYERS, D), 0.1, 1.5)
    return dict(query_states=query_states, passage_states=passage_states, query_lengths=query_lengths, passage_lengths=passage_lengths, query_count=query_count, passage_count=passage_count, positive=positive, query_key_value_matrix=query_key_value_matrix, qv_bias=qv_bias, out_weight=out_weight, out_bias=out_bias, norm_gain=norm_gain, norm_bias=norm_bias, up_matrix=up_matrix, up_bias=up_bias, down_matrix=down_matrix, down_bias=down_bias)


@jax.custom_vjp
def lower_precision(v):
    return lax.optimization_barrier(v.astype(jnp.bfloat16)).astype(jnp.float32)

@jax.custom_vjp
def lower_backward(v):
    return v

def low_keep(v):
    return (lower_precision(v), None)

def low_pass(kept, grad):
    return (grad,)

def back_keep(v):
    return (v, None)

def back_low(kept, grad):
    return (lower_precision(grad),)
lower_precision.defvjp(low_keep, low_pass)
lower_backward.defvjp(back_keep, back_low)
EPS_NORM = 1e-12
INV_TEMP = 50.0
PRECISE_MODE = lax.Precision.HIGHEST

def layer_norm(summed, gain, bias):
    average = lax.optimization_barrier(jnp.mean(summed, axis=-1, keepdims=True))
    centered = summed - average
    variance = lax.optimization_barrier(jnp.mean(centered * centered, axis=-1, keepdims=True))
    return centered * lax.rsqrt(variance + EPS_NORM) * gain + bias

def gelu_exact(inner_rows):
    return 0.5 * inner_rows * (1.0 + jax.scipy.special.erf(inner_rows * (1.0 / math.sqrt(2.0))))

def attend(query_rows, incoming_keys, incoming_values, lengths):
    seq_len = query_rows.shape[1]
    scores = lower_backward(jnp.einsum('sqhe,skhe->shqk', query_rows, incoming_keys, precision=PRECISE_MODE) * HEAD_DIM ** (-0.5))
    keep_mask = (jnp.arange(seq_len, dtype=jnp.int32)[None, :] < lengths[:, None])[:, None, None, :]
    scores = jnp.where(keep_mask, scores, -1e+30)
    top_score = lax.optimization_barrier(jnp.max(scores, axis=-1, keepdims=True))
    expo = jnp.exp(scores - top_score)
    probs = expo / lax.optimization_barrier(jnp.sum(expo, axis=-1, keepdims=True))
    return jnp.einsum('shqk,skhe->sqhe', lower_precision(probs), incoming_values, precision=PRECISE_MODE)

def encoder_layer(states, lengths, weights, layer_number):
    query_key_value_weight, query_value_bias, output_proj_weight, output_proj_bias, gains, biases, up_proj_weight, up_proj_bias, down_proj_weight, down_proj_bias = weights
    num_seqs, seq_len, width = states.shape
    rounded_length = lower_precision(states)
    query_rows = lower_precision(lower_backward(jnp.einsum('hty,yk->htk', rounded_length, query_key_value_weight[layer_number, 0], precision=PRECISE_MODE) + query_value_bias[layer_number, 0]))
    incoming_keys = lower_precision(lower_backward(jnp.einsum('hty,yk->htk', rounded_length, query_key_value_weight[layer_number, 1], precision=PRECISE_MODE)))
    incoming_values = lower_precision(lower_backward(jnp.einsum('hty,yk->htk', rounded_length, query_key_value_weight[layer_number, 2], precision=PRECISE_MODE) + query_value_bias[layer_number, 1]))
    head_shape = (num_seqs, seq_len, HEADS, HEAD_DIM)
    attended_values = attend(query_rows.reshape(head_shape), incoming_keys.reshape(head_shape), incoming_values.reshape(head_shape), lengths)
    attended_values = lower_precision(lower_backward(attended_values.reshape(num_seqs, seq_len, width)))
    attention_result = lower_backward(jnp.einsum('yhe,eu->yhu', attended_values, output_proj_weight[layer_number], precision=PRECISE_MODE) + output_proj_bias[layer_number])
    hidden_rows = layer_norm(states + attention_result, gains[layer_number, 0], biases[layer_number, 0])
    inner_rows = lower_backward(jnp.einsum('igy,yv->igv', lower_precision(hidden_rows), up_proj_weight[layer_number], precision=PRECISE_MODE) + up_proj_bias[layer_number])
    activated_rows = lower_precision(gelu_exact(inner_rows))
    feedforward_result = lower_backward(jnp.einsum('cka,ax->ckx', activated_rows, down_proj_weight[layer_number], precision=PRECISE_MODE) + down_proj_bias[layer_number])
    return layer_norm(hidden_rows + feedforward_result, gains[layer_number, 1], biases[layer_number, 1])

def run_block(weights, pair):
    states, lengths = pair
    hidden_state = states
    for layer_number in range(LAYERS):
        hidden_state = encoder_layer(hidden_state, lengths, weights, layer_number)
    seq_len = states.shape[1]
    live_tok = (jnp.arange(seq_len, dtype=jnp.int32)[None, :] < lengths[:, None]).astype(jnp.float32)
    pooled = lax.optimization_barrier(jnp.sum(hidden_state * live_tok[:, :, None], axis=1))
    return pooled / lengths[:, None].astype(jnp.float32)

def pool_bucket(weights, states, lengths):
    num_seqs, seq_len, width = states.shape
    block_size = math.gcd(num_seqs, max(1, 4096 // seq_len))
    num_blocks = num_seqs // block_size
    shaped = states.reshape(num_blocks, block_size, seq_len, width)
    pooled = lax.map(jax.checkpoint(partial(run_block, weights)), (shaped, lengths.reshape(num_blocks, block_size)))
    return pooled.reshape(num_seqs, width)

def normalize(embedded):
    return embedded * lax.rsqrt(lax.optimization_barrier(jnp.sum(embedded * embedded, axis=-1, keepdims=True)) + 1e-06)

def objective(q_states, p_states, weights, query_lengths, passage_lengths, query_count, passage_count, positive):
    q_norm = normalize(pool_bucket(weights, q_states, query_lengths))
    p_norm = normalize(pool_bucket(weights, p_states, passage_lengths))
    sims = INV_TEMP * jnp.dot(q_norm, p_norm.T, precision=PRECISE_MODE)
    pass_ids = jnp.arange(PASSAGES, dtype=jnp.int32)
    live_pass = pass_ids % P_DEV < passage_count[pass_ids // P_DEV]
    masked = jnp.where(live_pass[None, :], sims, -1e+30)
    top_score = lax.optimization_barrier(jnp.max(masked, axis=1, keepdims=True))
    log_total = top_score[:, 0] + jnp.log(lax.optimization_barrier(jnp.sum(jnp.exp(masked - top_score), axis=1)))
    pos_score = lax.optimization_barrier(jnp.sum(jnp.where(pass_ids[None, :] == positive[:, None], sims, 0.0), axis=1))
    query_ids = jnp.arange(QUERIES, dtype=jnp.int32)
    live_query = (query_ids % Q_DEV < query_count[query_ids // Q_DEV]).astype(jnp.float32)
    loss = jnp.sum(live_query * (log_total - pos_score)) / jnp.sum(live_query)
    return (GRAD_SCALE * loss, loss)

def reference(query_states, passage_states, query_lengths, passage_lengths, query_count, passage_count, positive, query_key_value_matrix, qv_bias, out_weight, out_bias, norm_gain, norm_bias, up_matrix, up_bias, down_matrix, down_bias):
    weights = (query_key_value_matrix.astype(jnp.float32), qv_bias.astype(jnp.float32), out_weight.astype(jnp.float32), out_bias.astype(jnp.float32), norm_gain.astype(jnp.float32), norm_bias.astype(jnp.float32), up_matrix.astype(jnp.float32), up_bias.astype(jnp.float32), down_matrix.astype(jnp.float32), down_bias.astype(jnp.float32))

    def scaled(q_states, p_states, params):
        return objective(q_states, p_states, params, query_lengths, passage_lengths, query_count, passage_count, positive)
    value, pullback, loss = jax.vjp(scaled, query_states.astype(jnp.float32), passage_states.astype(jnp.float32), weights, has_aux=True)
    q_grad, p_grad, w_grads = pullback(jnp.ones_like(value))
    return (loss, q_grad, p_grad, w_grads[0], w_grads[1], w_grads[2], w_grads[3], w_grads[4], w_grads[5], w_grads[6], w_grads[7], w_grads[8], w_grads[9])
```

```python
import math

import jax
import jax.numpy as jnp
from jax import lax
from jax.sharding import PartitionSpec as P

HEAD_DIM = 64
EPS_NORM = 1e-12
INV_TEMP = 50.0
PRECISE_MODE = lax.Precision.HIGHEST
NEG_FILL = -1e30
RSQRT_TWO = 1.0 / math.sqrt(2.0)
RSQRT_TWOPI = 1.0 / math.sqrt(2.0 * math.pi)
F32 = jnp.float32
BF16 = jnp.bfloat16

CORE, XBIT, YBIT = 1, 2, 4
GROUP = 8


def flip(value, bit):
    size = lax.axis_size("dp")
    return lax.ppermute(value, "dp", [(i, i ^ bit) for i in range(size)])


def flip_mp(value, bit):
    size = lax.axis_size("mp")
    return lax.ppermute(value, "mp", [(i, i ^ bit) for i in range(size)])


def ring(value):
    size = lax.axis_size("mp")
    return lax.ppermute(value, "mp", [(i, (i + 1) % size) for i in range(size)])


def spots():
    index = lax.axis_index("dp")
    return index % 2, (index // 2) % 2, (index // 4) % 2


def swap_if(cond, first, second):
    return jnp.where(cond, second, first), jnp.where(cond, first, second)


def gather_plane(piece):
    core, px, py = spots()
    half = piece.shape[-2] // 2
    along_x = flip(piece, XBIT)
    along_y = flip(piece, YBIT)
    diag_a = flip(along_x[..., :half, :], YBIT)
    diag_b = flip(along_y[..., half:, :], XBIT)
    diag = jnp.concatenate([diag_a, diag_b], axis=-2)
    q0, q1 = swap_if(px == 1, piece, along_x)
    q2, q3 = swap_if(px == 1, along_y, diag)
    low = jnp.concatenate([q0, q1], axis=-2)
    high = jnp.concatenate([q2, q3], axis=-2)
    low, high = swap_if(py == 1, low, high)
    mine = jnp.concatenate([low, high], axis=-2)
    other = flip(mine, CORE)
    first, second = swap_if(core == 1, mine, other)
    return jnp.concatenate([first, second], axis=-2)


def gather_weights(shard):
    core, px, py = spots()
    rows = shard.shape[0] // GROUP
    mine = lax.dynamic_slice_in_dim(shard, (core * 4 + py * 2 + px) * rows, rows)
    pieces = []
    current = mine
    for _ in range(lax.axis_size("mp") - 1):
        current = ring(current)
        pieces.append(current)
    foreign = gather_plane(jnp.stack(pieces))
    return jnp.concatenate([shard[None], foreign])


def add_low(left, right):
    return (left.astype(F32) + right.astype(F32)).astype(BF16)


def pick(value, axis, index):
    return lax.dynamic_index_in_dim(value, index, axis=axis, keepdims=False)


def reduce_gradient(grad):
    core, px, py = spots()
    ways, rows, width = grad.shape
    split = width // 2
    blocks = grad.reshape(ways, 2, 2, 2, rows // GROUP, width)
    got = flip(pick(blocks, 1, 1 - core), CORE)
    blocks = add_low(pick(blocks, 1, core), got)
    left, right = blocks[..., :split], blocks[..., split:]
    got_left = flip(pick(left, 2, 1 - px), XBIT)
    got_right = flip(pick(right, 1, 1 - py), YBIT)
    left = add_low(pick(left, 2, px), got_left)
    right = add_low(pick(right, 1, py), got_right)
    got_left = flip(pick(left, 1, 1 - py), YBIT)
    got_right = flip(pick(right, 1, 1 - px), XBIT)
    left = add_low(pick(left, 1, py), got_left)
    right = add_low(pick(right, 1, px), got_right)
    block = jnp.concatenate([left, right], axis=-1)
    total = block[1]
    for step in range(2, ways + 1):
        total = add_low(ring(total), block[step % ways])
    bit = GROUP
    while bit < lax.axis_size("dp"):
        total = add_low(total, flip(total, bit))
        bit *= 2
    return gather_plane(total).astype(F32)


def gather_all(rows):
    bit = 1
    while bit < lax.axis_size("mp"):
        other = flip_mp(rows, bit)
        upper = (lax.axis_index("mp") // bit) % 2 == 1
        rows = jnp.concatenate(swap_if(upper, rows, other))
        bit *= 2
    bit = 1
    while bit < lax.axis_size("dp"):
        other = flip(rows, bit)
        upper = (lax.axis_index("dp") // bit) % 2 == 1
        rows = jnp.concatenate(swap_if(upper, rows, other))
        bit *= 2
    return rows


def sum_all(value):
    bit = 1
    while bit < lax.axis_size("dp"):
        value = value + flip(value, bit)
        bit *= 2
    bit = 1
    while bit < lax.axis_size("mp"):
        value = value + flip_mp(value, bit)
        bit *= 2
    return value


def norm_forward(summed, gain, bias):
    average = jnp.mean(summed, axis=-1, keepdims=True)
    centered = summed - average
    inv_std = lax.rsqrt(jnp.mean(centered * centered, axis=-1, keepdims=True) + EPS_NORM)
    normed = centered * inv_std
    return normed * gain + bias, normed, inv_std


def norm_backward(grad_out, normed, inv_std, gain):
    grad_normed = grad_out * gain
    grad_in = inv_std * (
        grad_normed
        - jnp.mean(grad_normed, axis=-1, keepdims=True)
        - normed * jnp.mean(grad_normed * normed, axis=-1, keepdims=True)
    )
    return grad_in, jnp.sum(grad_out * normed, axis=0), jnp.sum(grad_out, axis=0)


def gelu_value(inner):
    return 0.5 * inner * (1.0 + lax.erf(inner * RSQRT_TWO))


def gelu_slope(inner):
    return 0.5 * (1.0 + lax.erf(inner * RSQRT_TWO)) + inner * jnp.exp(
        -0.5 * inner * inner
    ) * RSQRT_TWOPI


def mm(spec, left, right):
    return jnp.einsum(spec, left, right, preferred_element_type=F32)


def scores_of(q, k, lengths):
    scores = mm("sqhe,skhe->shqk", q, k) * HEAD_DIM ** (-0.5)
    keep = jnp.arange(k.shape[1], dtype=jnp.int32)[None, :] < lengths[:, None]
    return jnp.where(keep[:, None, None, :], scores, NEG_FILL)


def attention_forward(q, k, v, lengths):
    scores = scores_of(q, k, lengths)
    top = jnp.max(scores, axis=-1, keepdims=True)
    expo = jnp.exp(scores - top)
    total = jnp.sum(expo, axis=-1, keepdims=True)
    probs = (expo / total).astype(BF16)
    return mm("shqk,skhe->sqhe", probs, v).astype(BF16), top + jnp.log(total)


def attention_backward(q, k, v, lengths, log_total, grad_context):
    scale = HEAD_DIM ** (-0.5)
    probs = jnp.exp(scores_of(q, k, lengths) - log_total)
    dv = mm("shqk,sqhe->skhe", probs.astype(BF16), grad_context).astype(BF16)
    dp = mm("sqhe,skhe->shqk", grad_context, v)
    ds = (probs * (dp - jnp.sum(probs * dp, axis=-1, keepdims=True))).astype(BF16)
    dq = (mm("shqk,skhe->sqhe", ds, k) * scale).astype(BF16)
    dk = (mm("shqk,sqhe->skhe", ds, q) * scale).astype(BF16)
    return dq, dk, dv


def buckets(rows, shapes):
    parts = []
    start = 0
    for count, length in shapes:
        stop = start + count * length
        parts.append(rows[start:stop].reshape(count, length, -1, HEAD_DIM))
        start = stop
    return parts


def unbucket(parts):
    return jnp.concatenate([part.reshape(-1, part.shape[2] * HEAD_DIM) for part in parts])


def layer_forward(x, attn_w, up_w, down_w, small, shapes, lengths):
    ways, rows, width = attn_w.shape
    part = rows // 4
    xr = x.astype(BF16)
    tokens = x.shape[0]
    q, k, v = (
        mm("td,zkd->tzk", xr, attn_w[:, i * part : (i + 1) * part]).reshape(tokens, -1)
        for i in range(3)
    )
    q = (q + small["q_bias"]).astype(BF16)
    k = k.astype(BF16)
    v = (v + small["v_bias"]).astype(BF16)
    contexts, logs = [], []
    for qs, ks, vs, lens in zip(
        buckets(q, shapes), buckets(k, shapes), buckets(v, shapes), lengths
    ):
        context, log_total = attention_forward(qs, ks, vs, lens)
        contexts.append(context)
        logs.append(log_total)
    ctx = unbucket(contexts)
    attn = mm("tc,cd->td", ctx, attn_w[:, 3 * part :].reshape(-1, width)) + small["out_bias"]
    h, n1, r1 = norm_forward(x + attn, small["gain"][0], small["bias"][0])
    hr = h.astype(BF16)
    u = mm("td,zdk->tzk", hr, up_w).reshape(tokens, -1) + small["up_bias"]
    a = gelu_value(u).astype(BF16)
    f = mm("tk,kd->td", a, down_w.reshape(-1, width)) + small["down_bias"]
    y, n2, r2 = norm_forward(h + f, small["gain"][1], small["bias"][1])
    return y, (xr, q, k, v, logs, ctx, n1, r1, hr, u, a, n2, r2)


def layer_backward(dy, saved, attn_w, up_w, down_w, small, shapes, lengths):
    xr, q, k, v, logs, ctx, n1, r1, hr, u, a, n2, r2 = saved
    ways, rows, width = attn_w.shape
    part = rows // 4
    tokens = dy.shape[0]
    dz2, gain_two, bias_two = norm_backward(dy, n2, r2, small["gain"][1])
    df = dz2.astype(BF16)
    down_b = jnp.sum(df, axis=0, dtype=F32)
    a4 = a.reshape(tokens, ways, -1)
    down_g = mm("tzk,td->zkd", a4, df).astype(BF16)
    da = mm("td,kd->tk", df, down_w.reshape(-1, width))
    du = (da * gelu_slope(u)).astype(BF16)
    up_b = jnp.sum(du, axis=0, dtype=F32)
    du4 = du.reshape(tokens, ways, -1)
    up_g = mm("td,tzk->zdk", hr, du4).astype(BF16)
    dh = dz2 + mm("tzk,zdk->td", du4, up_w)
    dz1, gain_one, bias_one = norm_backward(dh, n1, r1, small["gain"][0])
    dattn = dz1.astype(BF16)
    out_b = jnp.sum(dattn, axis=0, dtype=F32)
    out_g = mm("tzk,td->zkd", ctx.reshape(tokens, ways, -1), dattn)
    dctx = mm("td,cd->tc", dattn, attn_w[:, 3 * part :].reshape(-1, width)).astype(BF16)
    grads = ([], [], [])
    for qs, ks, vs, lens, log_total, gs in zip(
        buckets(q, shapes),
        buckets(k, shapes),
        buckets(v, shapes),
        lengths,
        logs,
        buckets(dctx, shapes),
    ):
        for store, value in zip(grads, attention_backward(qs, ks, vs, lens, log_total, gs)):
            store.append(value)
    dq, dk, dv = (unbucket(store).reshape(tokens, ways, -1) for store in grads)
    attn_g = jnp.concatenate(
        [mm("tzk,td->zkd", dq, xr), mm("tzk,td->zkd", dk, xr), mm("tzk,td->zkd", dv, xr), out_g],
        axis=1,
    ).astype(BF16)
    dx = dz1
    for i, grad in enumerate((dq, dk, dv)):
        dx = dx + mm("tzk,zkd->td", grad, attn_w[:, i * part : (i + 1) * part])
    qv_b = jnp.stack(
        [jnp.sum(dq, axis=0, dtype=F32).reshape(-1), jnp.sum(dv, axis=0, dtype=F32).reshape(-1)]
    )
    shared = (out_b, jnp.stack([gain_one, gain_two]), jnp.stack([bias_one, bias_two]), down_b)
    return dx, (attn_g, up_g, down_g), (qv_b, up_b, shared)


def to_absolute(rows):
    me = lax.axis_index("mp")
    ways = rows.shape[-2]
    wide = jnp.concatenate([rows, rows], axis=-2)
    flipped = jnp.flip(wide, axis=-2)
    return lax.dynamic_slice_in_dim(flipped, ways - 1 - me, ways, axis=-2)


def local(
    query_states,
    passage_states,
    query_lengths,
    passage_lengths,
    query_count,
    passage_count,
    positive,
    query_key_value_matrix,
    qv_bias,
    out_weight,
    out_bias,
    norm_gain,
    norm_bias,
    up_matrix,
    up_bias,
    down_matrix,
    down_bias,
):
    layers = query_key_value_matrix.shape[0]
    width = query_states.shape[-1]
    ways = lax.axis_size("mp")
    mp_rank = lax.axis_index("mp")
    my_rank = lax.axis_index("dp") * ways + mp_rank
    q_slots, q_len, _ = query_states.shape
    p_slots, p_len, _ = passage_states.shape
    shapes = ((q_slots, q_len), (p_slots, p_len))
    lengths = (
        lax.dynamic_slice_in_dim(query_lengths, mp_rank * q_slots, q_slots),
        lax.dynamic_slice_in_dim(passage_lengths, mp_rank * p_slots, p_slots),
    )
    part = qv_bias.shape[-1]

    tiny = jnp.concatenate([qv_bias.reshape(layers * 2, part), up_bias.reshape(layers * 4, part)])
    tiny_all = [tiny]
    for _ in range(ways - 1):
        tiny_all.append(ring(tiny_all[-1]))
    tiny_all = jnp.stack(tiny_all).astype(F32)

    weights = []
    for l in range(layers):
        qkv_t = jnp.swapaxes(query_key_value_matrix[l], 1, 2).reshape(3 * part, width)
        attn_w = gather_weights(jnp.concatenate([qkv_t, out_weight[l]]))
        up_w = gather_weights(up_matrix[l])
        down_w = gather_weights(down_matrix[l])
        small = {
            "q_bias": tiny_all[:, 2 * l].reshape(-1),
            "v_bias": tiny_all[:, 2 * l + 1].reshape(-1),
            "up_bias": tiny_all[:, 2 * layers + 4 * l : 2 * layers + 4 * (l + 1)].reshape(-1),
            "out_bias": out_bias[l].astype(F32),
            "down_bias": down_bias[l].astype(F32),
            "gain": norm_gain[l].astype(F32),
            "bias": norm_bias[l].astype(F32),
        }
        weights.append((attn_w, up_w, down_w, small))

    x = jnp.concatenate(
        [query_states.reshape(-1, width), passage_states.reshape(-1, width)]
    ).astype(F32)
    kept = []
    for l in range(layers):
        x, saved = layer_forward(x, *weights[l], shapes, lengths)
        kept.append(saved)

    masks, embeds, invs = [], [], []
    start = 0
    for (count, length), lens in zip(shapes, lengths):
        y = x[start : start + count * length].reshape(count, length, width)
        start += count * length
        live = jnp.arange(length, dtype=jnp.int32)[None, :] < lens[:, None]
        mask = live.astype(F32) / lens[:, None].astype(F32)
        pooled = jnp.sum(y * mask[:, :, None], axis=1)
        inv = lax.rsqrt(jnp.sum(pooled * pooled, axis=-1, keepdims=True) + 1e-06)
        masks.append(mask)
        embeds.append(pooled * inv)
        invs.append(inv)

    marks = jnp.zeros((1, width), F32).at[0, :q_slots].set(positive.astype(F32))
    everything = gather_all(jnp.concatenate([embeds[0], embeds[1], marks])[None])
    nq = everything[:, :q_slots].reshape(-1, width)
    np_ = everything[:, q_slots : q_slots + p_slots].reshape(-1, width)
    pos = everything[:, q_slots + p_slots, :q_slots].reshape(-1).astype(jnp.int32)
    num_q, num_p = nq.shape[0], np_.shape[0]
    sims = INV_TEMP * jnp.dot(nq, np_.T, precision=PRECISE_MODE)
    live_p = (jnp.arange(p_slots)[None, :] < passage_count[:, None]).reshape(-1)
    live_q = (jnp.arange(q_slots)[None, :] < query_count[:, None]).reshape(-1).astype(F32)
    masked = jnp.where(live_p[None, :], sims, NEG_FILL)
    top = jnp.max(masked, axis=1, keepdims=True)
    expo = jnp.exp(masked - top)
    total = jnp.sum(expo, axis=1, keepdims=True)
    lse = top[:, 0] + jnp.log(total[:, 0])
    is_pos = (jnp.arange(num_p, dtype=jnp.int32)[None, :] == pos[:, None]).astype(F32)
    pos_score = jnp.sum(is_pos * sims, axis=1)
    live_total = jnp.sum(query_count).astype(F32)
    loss = jnp.sum(live_q * (lse - pos_score)) / live_total
    grad_scale = float(num_q * q_len)
    ds = (grad_scale * live_q / live_total)[:, None] * (expo / total - is_pos)
    my_ds = lax.dynamic_slice_in_dim(ds, my_rank * q_slots, q_slots, axis=0)
    my_dst = lax.dynamic_slice_in_dim(ds.T, my_rank * p_slots, p_slots, axis=0)
    dnq = INV_TEMP * jnp.dot(my_ds, np_, precision=PRECISE_MODE)
    dnp = INV_TEMP * jnp.dot(my_dst, nq, precision=PRECISE_MODE)
    dys = []
    for grad, normed, inv, mask in zip((dnq, dnp), embeds, invs, masks):
        pooled_grad = inv * (grad - normed * jnp.sum(normed * grad, axis=-1, keepdims=True))
        dys.append((mask[:, :, None] * pooled_grad[:, None, :]).reshape(-1, width))
    dy = jnp.concatenate(dys)

    summed = [None] * layers
    smalls = [None] * layers
    for l in reversed(range(layers)):
        dy, big, (qv_b, up_b, shared) = layer_backward(
            dy, kept[l], *weights[l], shapes, lengths
        )
        summed[l] = tuple(reduce_gradient(item) for item in big)
        qv_abs = to_absolute(qv_b.reshape(2, ways, part)).reshape(-1)
        up_abs = to_absolute(up_b.reshape(ways, -1)).reshape(-1)
        flat = jnp.concatenate([qv_abs, up_abs] + [item.reshape(-1) for item in shared])
        smalls[l] = sum_all(flat.reshape(-1, width))

    query_grad = dy[: q_slots * q_len].reshape(query_states.shape)
    passage_grad = dy[q_slots * q_len :].reshape(passage_states.shape)
    attn_out = jnp.stack([s[0] for s in summed])
    qkv_grad = jnp.swapaxes(attn_out[:, : 3 * part].reshape(layers, 3, part, width), 2, 3)
    out_grad = attn_out[:, 3 * part :]
    up_grad = jnp.stack([s[1] for s in summed])
    down_grad = jnp.stack([s[2] for s in summed])
    small_all = jnp.stack(smalls)
    hidden = up_bias.shape[-1]
    cut = lambda lo, hi: small_all[:, lo:hi]
    qv_rows = cut(0, 2)
    qv_grad = lax.dynamic_slice_in_dim(qv_rows, mp_rank * part, part, axis=2)
    up_rows = cut(2, 2 + ways * hidden // width).reshape(layers, -1)
    up_b_grad = lax.dynamic_slice_in_dim(up_rows, mp_rank * hidden, hidden, axis=1)
    base = 2 + ways * hidden // width
    return (
        loss,
        query_grad,
        passage_grad,
        qkv_grad,
        qv_grad,
        out_grad,
        cut(base, base + 1)[:, 0],
        cut(base + 1, base + 3),
        cut(base + 3, base + 5),
        up_grad,
        up_b_grad,
        down_grad,
        cut(base + 5, base + 6)[:, 0],
    )


def solution(mesh):
    placed = (
        P(("dp", "mp"), None, None),
        P(("dp", "mp"), None, None),
        P("dp"),
        P("dp"),
        P(),
        P(),
        P(("dp", "mp")),
        P(None, None, None, "mp"),
        P(None, None, "mp"),
        P(None, "mp", None),
        P(),
        P(),
        P(),
        P(None, None, "mp"),
        P(None, "mp"),
        P(None, "mp", None),
        P(),
    )
    return jax.shard_map(
        local,
        mesh=mesh,
        in_specs=placed,
        out_specs=(
            P(),
            P(("dp", "mp"), None, None),
            P(("dp", "mp"), None, None),
            P(None, None, None, "mp"),
            P(None, None, "mp"),
            P(None, "mp", None),
            P(),
            P(),
            P(),
            P(None, None, "mp"),
            P(None, "mp"),
            P(None, "mp", None),
            P(),
        ),
        check_vma=False,
    )
```

```python
import functools
import math

import jax
import jax.numpy as jnp
from jax import lax
from jax.experimental import pallas as pl
from jax.experimental.pallas import tpu as pltpu
from jax.sharding import PartitionSpec as P

HEAD_DIM = 64
EPS_NORM = 1e-12
INV_TEMP = 50.0
PRECISE_MODE = lax.Precision.HIGHEST
NEG_FILL = -1e30
RSQRT_TWO = 1.0 / math.sqrt(2.0)
RSQRT_TWOPI = 1.0 / math.sqrt(2.0 * math.pi)
F32 = jnp.float32
BF16 = jnp.bfloat16


ANY = pl.BlockSpec(memory_space=pl.ANY)

def place():
    d = lax.axis_index("dp")
    z = lax.axis_index("mp")
    nz = lax.axis_size("mp")
    core, px, py = d % 2, (d // 2) % 2, (d // 4) % 2
    peers = {
        "core": {"dp": d + 1 - 2 * core},
        "x": {"dp": d + 2 - 4 * px},
        "y": {"dp": d + 4 - 8 * py},
        "up": {"mp": lax.rem(z + 1, nz)},
        "down": {"mp": lax.rem(z + nz - 1, nz)},
    }
    return core, px, py, peers

def greet(names, peers):
    sem = pltpu.get_barrier_semaphore()
    for n in names:
        pl.semaphore_signal(sem, inc=1, device_id=peers[n], device_id_type=pl.DeviceIdType.MESH)
    pl.semaphore_wait(sem, len(names))

def spot(core, px, py):
    return core * 4 + py * 2 + px

def gather_kernel(kinds, ways, srcs, out, z_send, z_recv, p_send, p_recv, own_send, own_recv):
    core, px, py, peers = place()
    rows = out.shape[2] // 8
    part = out.shape[2] // ways

    def region(g, k, slot, lo=0, n=None):
        n = rows if n is None else n
        if kinds[g][2]:
            return out.at[g, slot // 2, pl.ds(pl.multiple_of(k * part + (slot % 2) * rows + lo, 16), n)]
        return out.at[g, k, pl.ds(pl.multiple_of(slot * rows + lo, 16), n)]

    def source(g):
        ref, layer, _ = kinds[g]
        return srcs[ref].at[layer]

    me = spot(core, px, py)
    slot_x, slot_y, slot_d = spot(core, 1 - px, py), spot(core, px, 1 - py), spot(core, 1 - px, 1 - py)
    other = spot(1 - core, px, py)

    def remote(src, dst, sems, index, peer):
        return pltpu.make_async_remote_copy(
            src_ref=src, dst_ref=dst, send_sem=sems[0].at[index], recv_sem=sems[1].at[index],
            device_id=peers[peer], device_id_type=pl.DeviceIdType.MESH)

    zs, ps = (z_send, z_recv), (p_send, p_recv)
    started = []

    def go(copy):
        copy.start()
        started.append(copy)

    def z_copy(g, k):
        src = source(g).at[pl.ds(pl.multiple_of(me * rows, 16), rows)] if k == 1 else region(g, k - 1, me)
        return remote(src, region(g, k, me), zs, g * (ways - 1) + k - 1, "up")

    half = rows // 2
    plane = [
        ("x", me, slot_x, 0, rows),
        ("y", me, slot_y, 0, rows),
        ("y", slot_x, slot_d, 0, half),
        ("x", slot_y, slot_d, half, half),
        ("core", me, other, 0, rows),
        ("core", slot_x, spot(1 - core, 1 - px, py), 0, rows),
        ("core", slot_y, spot(1 - core, px, 1 - py), 0, rows),
        ("core", slot_d, spot(1 - core, 1 - px, 1 - py), 0, rows),
    ]
    count = len(plane)

    def p_copy(g, k, i, received=False):
        peer, sent, got, lo, n = plane[i]
        slot = got if received else sent
        reg = region(g, k, slot, lo, n)
        return remote(reg, reg, ps, (g * (ways - 1) + k - 1) * count + i, peer)

    groups = len(kinds)
    def own_copy(g, m):
        if kinds[g][2]:
            src, dst = source(g).at[pl.ds(m * part, part)], out.at[g, m, pl.ds(0, part)]
        else:
            src, dst = source(g), out.at[g, 0]
        return remote(src, dst, (own_send, own_recv), g * 4 + m, "core")

    own = [(g, m) for g in range(groups) for m in range(4 if kinds[g][2] else 1)]
    greet(("core", "x", "y", "up", "down"), peers)
    work = [(g, k) for g in range(groups) for k in range(1, ways)]
    go(z_copy(0, 1))
    for item in own:
        go(own_copy(*item))

    def second(g, k):
        p_copy(g, k, 0, True).wait_recv()
        go(p_copy(g, k, 2)); go(p_copy(g, k, 5))
        p_copy(g, k, 1, True).wait_recv()
        go(p_copy(g, k, 3)); go(p_copy(g, k, 6))

    def third(g, k):
        p_copy(g, k, 2, True).wait_recv()
        p_copy(g, k, 3, True).wait_recv()
        go(p_copy(g, k, 7))

    lag2, lag3 = 1, 2
    for i in range(len(work) + lag3):
        if i < len(work):
            g, k = work[i]
            z_copy(g, k).wait_recv()
            if k + 1 < ways:
                go(z_copy(g, k + 1))
            elif g + 1 < groups:
                go(z_copy(g + 1, 1))
            go(p_copy(g, k, 0)); go(p_copy(g, k, 1)); go(p_copy(g, k, 4))
        if 0 <= i - lag2 < len(work):
            second(*work[i - lag2])
        if 0 <= i - lag3 < len(work):
            third(*work[i - lag3])
    for g, k in work:
        for i in range(4, 8):
            p_copy(g, k, i, True).wait_recv()
    for c in started:
        c.wait_send()
    for item in own:
        own_copy(*item).wait_recv()

def gather_weights(sources, kinds, ways, collective_id):
    width = sources[0].shape[-1]
    rows = sources[0].shape[-2]
    groups = len(kinds)
    n = groups * (ways - 1)
    def kern(*refs):
        gather_kernel(kinds, ways, refs[:len(sources)], *refs[len(sources):])
    return pl.pallas_call(
        kern,
        out_shape=jax.ShapeDtypeStruct((groups, ways, rows, width), BF16),
        in_specs=[ANY] * len(sources), out_specs=ANY,
        scratch_shapes=[pltpu.SemaphoreType.DMA((n,)), pltpu.SemaphoreType.DMA((n,)),
                        pltpu.SemaphoreType.DMA((n * 8,)), pltpu.SemaphoreType.DMA((n * 8,)),
                        pltpu.SemaphoreType.DMA((groups * 4,)), pltpu.SemaphoreType.DMA((groups * 4,))],
        compiler_params=pltpu.CompilerParams(collective_id=collective_id, has_side_effects=True),
        name="gather_weights",
    )(*sources)


def add_low(a, b):
    return (a.astype(F32) + b.astype(F32)).astype(BF16)

def far_peers(names):
    d = lax.axis_index("dp")
    found = {}
    bit = 8
    while bit < lax.axis_size("dp"):
        high = (d // bit) % 2
        found[f"far{bit}"] = {"dp": d + bit - 2 * bit * high}
        bit *= 2
    return found

def reduce_kernel(attn, ways, grads, out, own, got, got_a, got_b, got_c, got_d, mix, zin, zout, far,
                  l_sem, r_send, r_recv, g_send, g_recv):
    core, px, py, peers = place()
    extra = far_peers(None)
    peers.update(extra)
    groups = len(attn)
    rows = out.shape[1] // 8
    half = rows // 2
    def remote(src, dst, sems, index, peer):
        return pltpu.make_async_remote_copy(
            src_ref=src, dst_ref=dst, send_sem=sems[0].at[index], recv_sem=sems[1].at[index],
            device_id=peers[peer], device_id_type=pl.DeviceIdType.MESH)
    rs, gs = (r_send, r_recv), (g_send, g_recv)
    per = 6 + ways - 1 + len(extra)
    started = []
    def go(c):
        c.start(); started.append(c)

    def share(g, c, j):
        ref = grads[g]
        return ref.at[2 * c + j] if attn[g] else ref.at[:, 2 * c + j]

    def load(g, j):
        return pltpu.make_async_copy(share(g, core, j), own.at[g, :, j], l_sem.at[g * 2 + j])
    def core_copy(g, j):
        return remote(share(g, 1 - core, j), got.at[g, :, j], rs, g * per + j, "core")
    def a1(g):
        return remote(own.at[g, :, :, pl.ds((1 - px) * rows, half)], got_a.at[g], rs, g * per + 2, "x")
    def b1(g):
        return remote(mix.at[g, :, 1 - py], got_b.at[g], rs, g * per + 3, "y")
    def a2(g):
        return remote(got_a.at[g, :, 1 - py], got_c.at[g], rs, g * per + 4, "y")
    def b2(g):
        return remote(got_b.at[g, :, pl.ds((1 - px) * half, half)], got_d.at[g], rs, g * per + 5, "x")
    def zc(g, s):
        return remote(zout.at[g, s - 1], zin.at[g, s - 1], rs, g * per + 5 + s, "up")
    def fc(g, i, name):
        return remote(zout.at[g, ways - 1 + i], far.at[g, i], rs, g * per + 5 + ways + i, name)

    last = ways - 1 + len(extra)
    me = spot(core, px, py)
    slot_x, slot_y, slot_d = spot(core, 1 - px, py), spot(core, px, 1 - py), spot(core, 1 - px, 1 - py)
    plane = [
        ("x", me, slot_x, 0, rows), ("y", me, slot_y, 0, rows),
        ("y", slot_x, slot_d, 0, half), ("x", slot_y, slot_d, half, half),
        ("core", me, spot(1 - core, px, py), 0, rows),
        ("core", slot_x, spot(1 - core, 1 - px, py), 0, rows),
        ("core", slot_y, spot(1 - core, px, 1 - py), 0, rows),
        ("core", slot_d, spot(1 - core, 1 - px, 1 - py), 0, rows),
    ]
    def pc(g, i, received=False):
        peer, sent, got_slot, lo, n = plane[i]
        slot = got_slot if received else sent
        dst = out.at[g, pl.ds(pl.multiple_of(slot * rows + lo, 16), n)]
        src = zout.at[g, last] if sent is me else dst
        return remote(src, dst, gs, g * 8 + i, peer)
    def mine_out(g):
        return pltpu.make_async_copy(zout.at[g, last], out.at[g, pl.ds(pl.multiple_of(me * rows, 16), rows)], l_sem.at[groups * 2 + g])

    def s0(g):
        for j in range(2):
            load(g, j).start()
            go(core_copy(g, j))
    def s1(g):
        for j in range(2):
            load(g, j).wait()
            core_copy(g, j).wait_recv()
        def body(k, _):
            for j in range(2):
                for x in range(2):
                    lo = slice(x * rows, x * rows + half)
                    own[g, k, j, lo] = add_low(own[g, k, j, lo], got[g, k, j, lo])
                    hi = slice(x * rows + half, (x + 1) * rows)
                    mix[g, k, j, x * half:(x + 1) * half] = add_low(own[g, k, j, hi], got[g, k, j, hi])
            return 0
        lax.fori_loop(0, ways, body, 0)
        go(a1(g)); go(b1(g))
    def s2(g):
        a1(g).wait_recv()
        def body(k, _):
            for j in range(2):
                got_a[g, k, j] = add_low(own[g, k, j, pl.ds(pl.multiple_of(px * rows, 16), half)], got_a[g, k, j])
            return 0
        lax.fori_loop(0, ways, body, 0)
        go(a2(g))
        b1(g).wait_recv()
        def body(k, _):
            got_b[g, k] = add_low(mix[g, k, py], got_b[g, k])
            return 0
        lax.fori_loop(0, ways, body, 0)
        go(b2(g))
    def part(g, k):
        left = add_low(got_a[g, k, py], got_c[g, k])
        right = add_low(got_b[g, k, pl.ds(pl.multiple_of(px * half, 16), half)], got_d[g, k])
        return left, right
    def s3(g):
        a2(g).wait_recv(); b2(g).wait_recv()
        left, right = part(g, 1)
        zout[g, 0, :half] = left
        zout[g, 0, half:] = right
        go(zc(g, 1))
    def sz(g, s):
        zc(g, s).wait_recv()
        left, right = part(g, (s + 1) % ways)
        zout[g, s, :half] = add_low(zin[g, s - 1, :half], left)
        zout[g, s, half:] = add_low(zin[g, s - 1, half:], right)
        if s < ways - 1:
            go(zc(g, s + 1))
    def sfar(g):
        for i, name in enumerate(extra):
            go(fc(g, i, name))
            fc(g, i, name).wait_recv()
            zout[g, ways + i] = add_low(zout[g, ways - 1 + i], far[g, i])
    def sp(g):
        sz(g, ways - 1)
        sfar(g)
        mine_out(g).start()
        for i in (0, 1, 4):
            go(pc(g, i))
    def sq(g):
        pc(g, 0, True).wait_recv()
        go(pc(g, 2)); go(pc(g, 5))
        pc(g, 1, True).wait_recv()
        go(pc(g, 3)); go(pc(g, 6))
    def sr(g):
        pc(g, 2, True).wait_recv()
        pc(g, 3, True).wait_recv()
        go(pc(g, 7))
    stages = [s1, s2, s3] + [functools.partial(lambda s, g: sz(g, s), s) for s in range(1, ways - 1)] + [sp, sq, sr]
    greet(("core", "x", "y", "up", "down") + tuple(extra), peers)
    for g in range(groups):
        s0(g)
    for wave in range(groups + len(stages) - 1):
        for s in range(len(stages)):
            g = wave - s
            if 0 <= g < groups:
                stages[s](g)
    for g in range(groups):
        for i in range(4, 8):
            pc(g, i, True).wait_recv()
        mine_out(g).wait()
    for c in started:
        c.wait_send()

def reduce_gradients(grads, attn, ways, collective_id):
    groups = len(grads)
    quarter, width = grads[0].shape[2:]
    R = quarter * 4
    rows = R // 8
    half = rows // 2
    nfar = 0
    while 8 << nfar < lax.axis_size("dp"):
        nfar += 1
    per = 6 + ways - 1 + nfar
    def kern(*refs):
        reduce_kernel(attn, ways, refs[:groups], *refs[groups:])
    V = lambda *s: pltpu.VMEM(s, BF16)
    return pl.pallas_call(
        kern,
        out_shape=jax.ShapeDtypeStruct((groups, R, width), BF16),
        in_specs=[ANY] * groups, out_specs=ANY,
        scratch_shapes=[V(groups, ways, 2, 2 * rows, width), V(groups, ways, 2, 2 * rows, width),
                        V(groups, ways, 2, half, width), V(groups, ways, 2 * half, width),
                        V(groups, ways, half, width), V(groups, ways, half, width),
                        V(groups, ways, 2, 2 * half, width),
                        V(groups, ways - 1, rows, width), V(groups, ways + nfar, rows, width),
                        V(groups, max(nfar, 1), rows, width),
                        pltpu.SemaphoreType.DMA((groups * 3,)),
                        pltpu.SemaphoreType.DMA((groups * per,)), pltpu.SemaphoreType.DMA((groups * per,)),
                        pltpu.SemaphoreType.DMA((groups * 8,)), pltpu.SemaphoreType.DMA((groups * 8,))],
        compiler_params=pltpu.CompilerParams(collective_id=collective_id, has_side_effects=True, vmem_limit_bytes=60 << 20),
        name="reduce_gradients",
    )(*grads)


def flip(value, bit):
    size = lax.axis_size("dp")
    return lax.ppermute(value, "dp", [(i, i ^ bit) for i in range(size)])


def flip_mp(value, bit):
    size = lax.axis_size("mp")
    return lax.ppermute(value, "mp", [(i, i ^ bit) for i in range(size)])


def ring(value):
    size = lax.axis_size("mp")
    return lax.ppermute(value, "mp", [(i, (i + 1) % size) for i in range(size)])


def swap_if(cond, first, second):
    return jnp.where(cond, second, first), jnp.where(cond, first, second)


def gather_all(rows):
    bit = 1
    while bit < lax.axis_size("mp"):
        other = flip_mp(rows, bit)
        upper = (lax.axis_index("mp") // bit) % 2 == 1
        rows = jnp.concatenate(swap_if(upper, rows, other))
        bit *= 2
    bit = 1
    while bit < lax.axis_size("dp"):
        other = flip(rows, bit)
        upper = (lax.axis_index("dp") // bit) % 2 == 1
        rows = jnp.concatenate(swap_if(upper, rows, other))
        bit *= 2
    return rows


def sum_all(value):
    bit = 1
    while bit < lax.axis_size("dp"):
        value = value + flip(value, bit)
        bit *= 2
    bit = 1
    while bit < lax.axis_size("mp"):
        value = value + flip_mp(value, bit)
        bit *= 2
    return value


def norm_forward(summed, gain, bias):
    average = jnp.mean(summed, axis=-1, keepdims=True)
    centered = summed - average
    inv_std = lax.rsqrt(jnp.mean(centered * centered, axis=-1, keepdims=True) + EPS_NORM)
    normed = centered * inv_std
    return normed * gain + bias, normed, inv_std


def norm_backward(grad_out, normed, inv_std, gain):
    grad_normed = grad_out * gain
    grad_in = inv_std * (
        grad_normed
        - jnp.mean(grad_normed, axis=-1, keepdims=True)
        - normed * jnp.mean(grad_normed * normed, axis=-1, keepdims=True)
    )
    return grad_in, jnp.sum(grad_out * normed, axis=0), jnp.sum(grad_out, axis=0)


def gelu_value(inner):
    return 0.5 * inner * (1.0 + lax.erf(inner * RSQRT_TWO))


def gelu_slope(inner):
    return 0.5 * (1.0 + lax.erf(inner * RSQRT_TWO)) + inner * jnp.exp(
        -0.5 * inner * inner
    ) * RSQRT_TWOPI


def mm(spec, left, right):
    return jnp.einsum(spec, left, right, preferred_element_type=F32)


def scores_of(q, k, lengths):
    scores = mm("sqhe,skhe->shqk", q, k) * HEAD_DIM ** (-0.5)
    keep = jnp.arange(k.shape[1], dtype=jnp.int32)[None, :] < lengths[:, None]
    return jnp.where(keep[:, None, None, :], scores, NEG_FILL)


def attention_forward(q, k, v, lengths):
    scores = scores_of(q, k, lengths)
    top = jnp.max(scores, axis=-1, keepdims=True)
    expo = jnp.exp(scores - top)
    total = jnp.sum(expo, axis=-1, keepdims=True)
    probs = (expo / total).astype(BF16)
    return mm("shqk,skhe->sqhe", probs, v).astype(BF16), top + jnp.log(total)


def attention_backward(q, k, v, lengths, log_total, grad_context):
    scale = HEAD_DIM ** (-0.5)
    probs = jnp.exp(scores_of(q, k, lengths) - log_total)
    dv = mm("shqk,sqhe->skhe", probs.astype(BF16), grad_context).astype(BF16)
    dp = mm("sqhe,skhe->shqk", grad_context, v)
    ds = (probs * (dp - jnp.sum(probs * dp, axis=-1, keepdims=True))).astype(BF16)
    dq = (mm("shqk,skhe->sqhe", ds, k) * scale).astype(BF16)
    dk = (mm("shqk,sqhe->skhe", ds, q) * scale).astype(BF16)
    return dq, dk, dv


def buckets(rows, shapes):
    parts = []
    start = 0
    for count, length in shapes:
        stop = start + count * length
        parts.append(rows[start:stop].reshape(count, length, -1, HEAD_DIM))
        start = stop
    return parts


def unbucket(parts):
    return jnp.concatenate([part.reshape(-1, part.shape[2] * HEAD_DIM) for part in parts])


def layer_forward(x, attn_w, up_w, down_w, small, shapes, lengths):
    width = x.shape[-1]
    xr = x.astype(BF16)
    tokens = x.shape[0]
    q, k, v = (mm("td,kd->tk", xr, attn_w[i]) for i in range(3))
    q = (q + small["q_bias"]).astype(BF16)
    k = k.astype(BF16)
    v = (v + small["v_bias"]).astype(BF16)
    contexts, logs = [], []
    for qs, ks, vs, lens in zip(
        buckets(q, shapes), buckets(k, shapes), buckets(v, shapes), lengths
    ):
        context, log_total = attention_forward(qs, ks, vs, lens)
        contexts.append(context)
        logs.append(log_total)
    ctx = unbucket(contexts)
    attn = mm("tc,cd->td", ctx, attn_w[3]) + small["out_bias"]
    h, n1, r1 = norm_forward(x + attn, small["gain"][0], small["bias"][0])
    hr = h.astype(BF16)
    u = mm("td,zdk->tzk", hr, up_w).reshape(tokens, -1) + small["up_bias"]
    a = gelu_value(u).astype(BF16)
    f = mm("tk,kd->td", a, down_w.reshape(-1, width)) + small["down_bias"]
    y, n2, r2 = norm_forward(h + f, small["gain"][1], small["bias"][1])
    return y, (xr, q, k, v, logs, ctx, n1, r1, hr, u, a, n2, r2)


def layer_backward(dy, saved, attn_w, up_w, down_w, small, shapes, lengths):
    xr, q, k, v, logs, ctx, n1, r1, hr, u, a, n2, r2 = saved
    ways = up_w.shape[0]
    tokens, width = dy.shape
    dz2, gain_two, bias_two = norm_backward(dy, n2, r2, small["gain"][1])
    df = dz2.astype(BF16)
    down_b = jnp.sum(df, axis=0, dtype=F32)
    a4 = a.reshape(tokens, ways, -1)
    down_g = mm("tzk,td->zkd", a4, df).astype(BF16)
    da = mm("td,kd->tk", df, down_w.reshape(-1, width))
    du = (da * gelu_slope(u)).astype(BF16)
    up_b = jnp.sum(du, axis=0, dtype=F32)
    du4 = du.reshape(tokens, ways, -1)
    up_g = mm("td,tzk->zdk", hr, du4).astype(BF16)
    dh = dz2 + mm("tzk,zdk->td", du4, up_w)
    dz1, gain_one, bias_one = norm_backward(dh, n1, r1, small["gain"][0])
    dattn = dz1.astype(BF16)
    out_b = jnp.sum(dattn, axis=0, dtype=F32)
    out_g = mm("tk,td->kd", ctx, dattn)
    dctx = mm("td,cd->tc", dattn, attn_w[3]).astype(BF16)
    grads = ([], [], [])
    for qs, ks, vs, lens, log_total, gs in zip(
        buckets(q, shapes),
        buckets(k, shapes),
        buckets(v, shapes),
        lengths,
        logs,
        buckets(dctx, shapes),
    ):
        for store, value in zip(grads, attention_backward(qs, ks, vs, lens, log_total, gs)):
            store.append(value)
    dq, dk, dv = (unbucket(store) for store in grads)
    attn_g = jnp.stack(
        [mm("tk,td->kd", dq, xr), mm("tk,td->kd", dk, xr), mm("tk,td->kd", dv, xr), out_g]
    ).astype(BF16)
    dx = dz1
    for i, grad in enumerate((dq, dk, dv)):
        dx = dx + mm("tk,kd->td", grad, attn_w[i])
    qv_b = jnp.stack(
        [jnp.sum(dq, axis=0, dtype=F32).reshape(-1), jnp.sum(dv, axis=0, dtype=F32).reshape(-1)]
    )
    shared = (out_b, jnp.stack([gain_one, gain_two]), jnp.stack([bias_one, bias_two]), down_b)
    return dx, (attn_g, up_g, down_g), (qv_b, up_b, shared)


def to_absolute(rows):
    me = lax.axis_index("mp")
    ways = rows.shape[-2]
    wide = jnp.concatenate([rows, rows], axis=-2)
    flipped = jnp.flip(wide, axis=-2)
    return lax.dynamic_slice_in_dim(flipped, ways - 1 - me, ways, axis=-2)


def local(
    query_states,
    passage_states,
    query_lengths,
    passage_lengths,
    query_count,
    passage_count,
    positive,
    query_key_value_matrix,
    qv_bias,
    out_weight,
    out_bias,
    norm_gain,
    norm_bias,
    up_matrix,
    up_bias,
    down_matrix,
    down_bias,
):
    layers = query_key_value_matrix.shape[0]
    width = query_states.shape[-1]
    ways = lax.axis_size("mp")
    mp_rank = lax.axis_index("mp")
    my_rank = lax.axis_index("dp") * ways + mp_rank
    q_slots, q_len, _ = query_states.shape
    p_slots, p_len, _ = passage_states.shape
    shapes = ((q_slots, q_len), (p_slots, p_len))
    lengths = (
        lax.dynamic_slice_in_dim(query_lengths, mp_rank * q_slots, q_slots),
        lax.dynamic_slice_in_dim(passage_lengths, mp_rank * p_slots, p_slots),
    )
    part = qv_bias.shape[-1]

    tiny = jnp.concatenate([qv_bias.reshape(layers * 2, part), up_bias.reshape(layers * 4, part)])
    tiny_all = [tiny]
    for _ in range(ways - 1):
        tiny_all.append(ring(tiny_all[-1]))
    tiny_all = jnp.stack(tiny_all).astype(F32)

    weights = []
    qkv_t = jnp.swapaxes(query_key_value_matrix, 2, 3).reshape(layers, 3 * part, width)
    attn_pack = jnp.concatenate([qkv_t, out_weight], axis=1)
    kinds = tuple((i, l, i == 0) for l in range(layers) for i in range(3))
    gathered = gather_weights((attn_pack, up_matrix, down_matrix), kinds, ways, 0)
    for l in range(layers):
        attn_w, up_w, down_w = (gathered[3 * l + i] for i in range(3))
        small = {
            "q_bias": tiny_all[:, 2 * l].reshape(-1),
            "v_bias": tiny_all[:, 2 * l + 1].reshape(-1),
            "up_bias": tiny_all[:, 2 * layers + 4 * l : 2 * layers + 4 * (l + 1)].reshape(-1),
            "out_bias": out_bias[l].astype(F32),
            "down_bias": down_bias[l].astype(F32),
            "gain": norm_gain[l].astype(F32),
            "bias": norm_bias[l].astype(F32),
        }
        weights.append((attn_w, up_w, down_w, small))

    x = jnp.concatenate(
        [query_states.reshape(-1, width), passage_states.reshape(-1, width)]
    ).astype(F32)
    kept = []
    for l in range(layers):
        x, saved = layer_forward(x, *weights[l], shapes, lengths)
        kept.append(saved)

    masks, embeds, invs = [], [], []
    start = 0
    for (count, length), lens in zip(shapes, lengths):
        y = x[start : start + count * length].reshape(count, length, width)
        start += count * length
        live = jnp.arange(length, dtype=jnp.int32)[None, :] < lens[:, None]
        mask = live.astype(F32) / lens[:, None].astype(F32)
        pooled = jnp.sum(y * mask[:, :, None], axis=1)
        inv = lax.rsqrt(jnp.sum(pooled * pooled, axis=-1, keepdims=True) + 1e-06)
        masks.append(mask)
        embeds.append(pooled * inv)
        invs.append(inv)

    marks = jnp.zeros((1, width), F32).at[0, :q_slots].set(positive.astype(F32))
    everything = gather_all(jnp.concatenate([embeds[0], embeds[1], marks])[None])
    nq = everything[:, :q_slots].reshape(-1, width)
    np_ = everything[:, q_slots : q_slots + p_slots].reshape(-1, width)
    pos = everything[:, q_slots + p_slots, :q_slots].reshape(-1).astype(jnp.int32)
    num_q, num_p = nq.shape[0], np_.shape[0]
    sims = INV_TEMP * jnp.dot(nq, np_.T, precision=PRECISE_MODE)
    live_p = (jnp.arange(p_slots)[None, :] < passage_count[:, None]).reshape(-1)
    live_q = (jnp.arange(q_slots)[None, :] < query_count[:, None]).reshape(-1).astype(F32)
    masked = jnp.where(live_p[None, :], sims, NEG_FILL)
    top = jnp.max(masked, axis=1, keepdims=True)
    expo = jnp.exp(masked - top)
    total = jnp.sum(expo, axis=1, keepdims=True)
    lse = top[:, 0] + jnp.log(total[:, 0])
    is_pos = (jnp.arange(num_p, dtype=jnp.int32)[None, :] == pos[:, None]).astype(F32)
    pos_score = jnp.sum(is_pos * sims, axis=1)
    live_total = jnp.sum(query_count).astype(F32)
    loss = jnp.sum(live_q * (lse - pos_score)) / live_total
    grad_scale = float(num_q * q_len)
    ds = (grad_scale * live_q / live_total)[:, None] * (expo / total - is_pos)
    my_ds = lax.dynamic_slice_in_dim(ds, my_rank * q_slots, q_slots, axis=0)
    my_dst = lax.dynamic_slice_in_dim(ds.T, my_rank * p_slots, p_slots, axis=0)
    dnq = INV_TEMP * jnp.dot(my_ds, np_, precision=PRECISE_MODE)
    dnp = INV_TEMP * jnp.dot(my_dst, nq, precision=PRECISE_MODE)
    dys = []
    for grad, normed, inv, mask in zip((dnq, dnp), embeds, invs, masks):
        pooled_grad = inv * (grad - normed * jnp.sum(normed * grad, axis=-1, keepdims=True))
        dys.append((mask[:, :, None] * pooled_grad[:, None, :]).reshape(-1, width))
    dy = jnp.concatenate(dys)

    summed = [None] * layers
    smalls = [None] * layers
    for l in reversed(range(layers)):
        dy, big, (qv_b, up_b, shared) = layer_backward(
            dy, kept[l], *weights[l], shapes, lengths
        )
        big = [item.reshape(4, 4, -1, width) for item in (big[2], big[1], big[0])]
        summed[l] = reduce_gradients(big, (False, False, True), ways, 1 + l).astype(F32)
        qv_abs = to_absolute(qv_b.reshape(2, ways, part)).reshape(-1)
        up_abs = to_absolute(up_b.reshape(ways, -1)).reshape(-1)
        flat = jnp.concatenate([qv_abs, up_abs] + [item.reshape(-1) for item in shared])
        smalls[l] = sum_all(flat.reshape(-1, width))

    query_grad = dy[: q_slots * q_len].reshape(query_states.shape)
    passage_grad = dy[q_slots * q_len :].reshape(passage_states.shape)
    attn_out = jnp.stack([s[2] for s in summed])
    qkv_grad = jnp.swapaxes(attn_out[:, : 3 * part].reshape(layers, 3, part, width), 2, 3)
    out_grad = attn_out[:, 3 * part :]
    up_grad = jnp.stack([s[1] for s in summed])
    down_grad = jnp.stack([s[0] for s in summed])
    small_all = jnp.stack(smalls)
    hidden = up_bias.shape[-1]
    cut = lambda lo, hi: small_all[:, lo:hi]
    qv_rows = cut(0, 2)
    qv_grad = lax.dynamic_slice_in_dim(qv_rows, mp_rank * part, part, axis=2)
    up_rows = cut(2, 2 + ways * hidden // width).reshape(layers, -1)
    up_b_grad = lax.dynamic_slice_in_dim(up_rows, mp_rank * hidden, hidden, axis=1)
    base = 2 + ways * hidden // width
    return (
        loss,
        query_grad,
        passage_grad,
        qkv_grad,
        qv_grad,
        out_grad,
        cut(base, base + 1)[:, 0],
        cut(base + 1, base + 3),
        cut(base + 3, base + 5),
        up_grad,
        up_b_grad,
        down_grad,
        cut(base + 5, base + 6)[:, 0],
    )


def solution(mesh):
    placed = (
        P(("dp", "mp"), None, None),
        P(("dp", "mp"), None, None),
        P("dp"),
        P("dp"),
        P(),
        P(),
        P(("dp", "mp")),
        P(None, None, None, "mp"),
        P(None, None, "mp"),
        P(None, "mp", None),
        P(),
        P(),
        P(),
        P(None, None, "mp"),
        P(None, "mp"),
        P(None, "mp", None),
        P(),
    )
    return jax.shard_map(
        local,
        mesh=mesh,
        in_specs=placed,
        out_specs=(
            P(),
            P(("dp", "mp"), None, None),
            P(("dp", "mp"), None, None),
            P(None, None, None, "mp"),
            P(None, None, "mp"),
            P(None, "mp", None),
            P(),
            P(),
            P(),
            P(None, None, "mp"),
            P(None, "mp"),
            P(None, "mp", None),
            P(),
        ),
        check_vma=False,
    )
```

```python
import functools
import math

import jax
import jax.numpy as jnp
from jax import lax
from jax.experimental import pallas as pl
from jax.experimental.pallas import tpu as pltpu
from jax.sharding import PartitionSpec as P

HEAD_DIM = 64
EPS_NORM = 1e-12
INV_TEMP = 50.0
PRECISE_MODE = lax.Precision.HIGHEST
NEG_FILL = -1e30
RSQRT_TWO = 1.0 / math.sqrt(2.0)
RSQRT_TWOPI = 1.0 / math.sqrt(2.0 * math.pi)
F32 = jnp.float32
BF16 = jnp.bfloat16


ANY = pl.BlockSpec(memory_space=pl.ANY)

def place():
    d = lax.axis_index("dp")
    z = lax.axis_index("mp")
    nz = lax.axis_size("mp")
    core, px, py = d % 2, (d // 2) % 2, (d // 4) % 2
    peers = {
        "core": {"dp": d + 1 - 2 * core},
        "x": {"dp": d + 2 - 4 * px},
        "y": {"dp": d + 4 - 8 * py},
        "up": {"mp": lax.rem(z + 1, nz)},
        "down": {"mp": lax.rem(z + nz - 1, nz)},
    }
    return core, px, py, peers

def greet(names, peers):
    sem = pltpu.get_barrier_semaphore()
    for n in names:
        pl.semaphore_signal(sem, inc=1, device_id=peers[n], device_id_type=pl.DeviceIdType.MESH)
    pl.semaphore_wait(sem, len(names))

def spot(core, px, py):
    return core * 4 + py * 2 + px

def gather_kernel(kinds, ways, srcs, out, z_send, z_recv, p_send, p_recv, own_send, own_recv):
    core, px, py, peers = place()
    rows = out.shape[2] // 8
    part = out.shape[2] // ways

    def region(g, k, slot, lo=0, n=None):
        n = rows if n is None else n
        if kinds[g][2]:
            return out.at[g, slot // 2, pl.ds(pl.multiple_of(k * part + (slot % 2) * rows + lo, 16), n)]
        return out.at[g, k, pl.ds(pl.multiple_of(slot * rows + lo, 16), n)]

    def source(g):
        ref, layer, _ = kinds[g]
        return srcs[ref].at[layer]

    me = spot(core, px, py)
    slot_x, slot_y, slot_d = spot(core, 1 - px, py), spot(core, px, 1 - py), spot(core, 1 - px, 1 - py)
    other = spot(1 - core, px, py)

    def remote(src, dst, sems, index, peer):
        return pltpu.make_async_remote_copy(
            src_ref=src, dst_ref=dst, send_sem=sems[0].at[index], recv_sem=sems[1].at[index],
            device_id=peers[peer], device_id_type=pl.DeviceIdType.MESH)

    zs, ps = (z_send, z_recv), (p_send, p_recv)
    started = []

    def go(copy):
        copy.start()
        started.append(copy)

    def z_copy(g, k):
        src = source(g).at[pl.ds(pl.multiple_of(me * rows, 16), rows)] if k == 1 else region(g, k - 1, me)
        return remote(src, region(g, k, me), zs, g * (ways - 1) + k - 1, "up")

    half = rows // 2
    plane = [
        ("x", me, slot_x, 0, rows),
        ("y", me, slot_y, 0, rows),
        ("y", slot_x, slot_d, 0, half),
        ("x", slot_y, slot_d, half, half),
        ("core", me, other, 0, rows),
        ("core", slot_x, spot(1 - core, 1 - px, py), 0, rows),
        ("core", slot_y, spot(1 - core, px, 1 - py), 0, rows),
        ("core", slot_d, spot(1 - core, 1 - px, 1 - py), 0, rows),
    ]
    count = len(plane)

    def p_copy(g, k, i, received=False):
        peer, sent, got, lo, n = plane[i]
        slot = got if received else sent
        reg = region(g, k, slot, lo, n)
        return remote(reg, reg, ps, (g * (ways - 1) + k - 1) * count + i, peer)

    groups = len(kinds)
    def own_copy(g, m):
        if kinds[g][2]:
            src, dst = source(g).at[pl.ds(m * part, part)], out.at[g, m, pl.ds(0, part)]
        else:
            src, dst = source(g), out.at[g, 0]
        return remote(src, dst, (own_send, own_recv), g * 4 + m, "core")

    own = [(g, m) for g in range(groups) for m in range(4 if kinds[g][2] else 1)]
    greet(("core", "x", "y", "up", "down"), peers)
    work = [(g, k) for g in range(groups) for k in range(1, ways)]
    go(z_copy(0, 1))
    for item in own:
        go(own_copy(*item))

    def second(g, k):
        p_copy(g, k, 0, True).wait_recv()
        go(p_copy(g, k, 2)); go(p_copy(g, k, 5))
        p_copy(g, k, 1, True).wait_recv()
        go(p_copy(g, k, 3)); go(p_copy(g, k, 6))

    def third(g, k):
        p_copy(g, k, 2, True).wait_recv()
        p_copy(g, k, 3, True).wait_recv()
        go(p_copy(g, k, 7))

    lag2, lag3 = 1, 2
    for i in range(len(work) + lag3):
        if i < len(work):
            g, k = work[i]
            z_copy(g, k).wait_recv()
            if k + 1 < ways:
                go(z_copy(g, k + 1))
            elif g + 1 < groups:
                go(z_copy(g + 1, 1))
            go(p_copy(g, k, 0)); go(p_copy(g, k, 1)); go(p_copy(g, k, 4))
        if 0 <= i - lag2 < len(work):
            second(*work[i - lag2])
        if 0 <= i - lag3 < len(work):
            third(*work[i - lag3])
    for g, k in work:
        for i in range(4, 8):
            p_copy(g, k, i, True).wait_recv()
    for c in started:
        c.wait_send()
    for item in own:
        own_copy(*item).wait_recv()

def gather_weights(sources, kinds, ways, collective_id):
    width = sources[0].shape[-1]
    rows = sources[0].shape[-2]
    groups = len(kinds)
    n = groups * (ways - 1)
    def kern(*refs):
        gather_kernel(kinds, ways, refs[:len(sources)], *refs[len(sources):])
    return pl.pallas_call(
        kern,
        out_shape=jax.ShapeDtypeStruct((groups, ways, rows, width), BF16),
        in_specs=[ANY] * len(sources), out_specs=ANY,
        scratch_shapes=[pltpu.SemaphoreType.DMA((n,)), pltpu.SemaphoreType.DMA((n,)),
                        pltpu.SemaphoreType.DMA((n * 8,)), pltpu.SemaphoreType.DMA((n * 8,)),
                        pltpu.SemaphoreType.DMA((groups * 4,)), pltpu.SemaphoreType.DMA((groups * 4,))],
        compiler_params=pltpu.CompilerParams(collective_id=collective_id, has_side_effects=True),
        name="gather_weights",
    )(*sources)


def add_low(a, b):
    return (a.astype(F32) + b.astype(F32)).astype(BF16)

def far_peers(names):
    d = lax.axis_index("dp")
    found = {}
    bit = 8
    while bit < lax.axis_size("dp"):
        high = (d // bit) % 2
        found[f"far{bit}"] = {"dp": d + bit - 2 * bit * high}
        bit *= 2
    return found

def reduce_kernel(plan, ways, grads, out, own, got, got_a, got_b, got_c, got_d, mix, zin, zout, far,
                  l_sem, r_send, r_recv, g_send, g_recv):
    core, px, py, peers = place()
    extra = far_peers(None)
    peers.update(extra)
    groups = len(plan)
    rows = out.shape[1] // 8
    half = rows // 2
    def remote(src, dst, sems, index, peer):
        return pltpu.make_async_remote_copy(
            src_ref=src, dst_ref=dst, send_sem=sems[0].at[index], recv_sem=sems[1].at[index],
            device_id=peers[peer], device_id_type=pl.DeviceIdType.MESH)
    rs, gs = (r_send, r_recv), (g_send, g_recv)
    per = 6 + ways - 1 + len(extra)
    started = []
    def go(c):
        c.start(); started.append(c)

    def share(g, c, j):
        number, layer, attn = plan[g]
        ref = grads[number].at[layer]
        return ref.at[2 * c + j] if attn else ref.at[:, 2 * c + j]

    def load(g, j):
        return pltpu.make_async_copy(share(g, core, j), own.at[g, :, j], l_sem.at[g * 2 + j])
    def core_copy(g, j):
        return remote(share(g, 1 - core, j), got.at[g, :, j], rs, g * per + j, "core")
    def a1(g):
        return remote(own.at[g, :, :, pl.ds((1 - px) * rows, half)], got_a.at[g], rs, g * per + 2, "x")
    def b1(g):
        return remote(mix.at[g, :, 1 - py], got_b.at[g], rs, g * per + 3, "y")
    def a2(g):
        return remote(got_a.at[g, :, 1 - py], got_c.at[g], rs, g * per + 4, "y")
    def b2(g):
        return remote(got_b.at[g, :, pl.ds((1 - px) * half, half)], got_d.at[g], rs, g * per + 5, "x")
    def zc(g, s):
        return remote(zout.at[g, s - 1], zin.at[g, s - 1], rs, g * per + 5 + s, "up")
    def fc(g, i, name):
        return remote(zout.at[g, ways - 1 + i], far.at[g, i], rs, g * per + 5 + ways + i, name)

    last = ways - 1 + len(extra)
    me = spot(core, px, py)
    slot_x, slot_y, slot_d = spot(core, 1 - px, py), spot(core, px, 1 - py), spot(core, 1 - px, 1 - py)
    plane = [
        ("x", me, slot_x, 0, rows), ("y", me, slot_y, 0, rows),
        ("y", slot_x, slot_d, 0, half), ("x", slot_y, slot_d, half, half),
        ("core", me, spot(1 - core, px, py), 0, rows),
        ("core", slot_x, spot(1 - core, 1 - px, py), 0, rows),
        ("core", slot_y, spot(1 - core, px, 1 - py), 0, rows),
        ("core", slot_d, spot(1 - core, 1 - px, 1 - py), 0, rows),
    ]
    def pc(g, i, received=False):
        peer, sent, got_slot, lo, n = plane[i]
        slot = got_slot if received else sent
        dst = out.at[g, pl.ds(pl.multiple_of(slot * rows + lo, 16), n)]
        src = zout.at[g, last] if sent is me else dst
        return remote(src, dst, gs, g * 8 + i, peer)
    def mine_out(g):
        return pltpu.make_async_copy(zout.at[g, last], out.at[g, pl.ds(pl.multiple_of(me * rows, 16), rows)], l_sem.at[groups * 2 + g])

    def s0(g):
        for j in range(2):
            load(g, j).start()
            go(core_copy(g, j))
    def s1(g):
        for j in range(2):
            load(g, j).wait()
            core_copy(g, j).wait_recv()
        def body(k, _):
            for j in range(2):
                for x in range(2):
                    lo = slice(x * rows, x * rows + half)
                    own[g, k, j, lo] = add_low(own[g, k, j, lo], got[g, k, j, lo])
                    hi = slice(x * rows + half, (x + 1) * rows)
                    mix[g, k, j, x * half:(x + 1) * half] = add_low(own[g, k, j, hi], got[g, k, j, hi])
            return 0
        lax.fori_loop(0, ways, body, 0)
        go(a1(g)); go(b1(g))
    def s2(g):
        a1(g).wait_recv()
        def body(k, _):
            for j in range(2):
                got_a[g, k, j] = add_low(own[g, k, j, pl.ds(pl.multiple_of(px * rows, 16), half)], got_a[g, k, j])
            return 0
        lax.fori_loop(0, ways, body, 0)
        go(a2(g))
        b1(g).wait_recv()
        def body(k, _):
            got_b[g, k] = add_low(mix[g, k, py], got_b[g, k])
            return 0
        lax.fori_loop(0, ways, body, 0)
        go(b2(g))
    def part(g, k):
        left = add_low(got_a[g, k, py], got_c[g, k])
        right = add_low(got_b[g, k, pl.ds(pl.multiple_of(px * half, 16), half)], got_d[g, k])
        return left, right
    def s3(g):
        a2(g).wait_recv(); b2(g).wait_recv()
        left, right = part(g, 1)
        zout[g, 0, :half] = left
        zout[g, 0, half:] = right
        go(zc(g, 1))
    def sz(g, s):
        zc(g, s).wait_recv()
        left, right = part(g, (s + 1) % ways)
        zout[g, s, :half] = add_low(zin[g, s - 1, :half], left)
        zout[g, s, half:] = add_low(zin[g, s - 1, half:], right)
        if s < ways - 1:
            go(zc(g, s + 1))
    def sfar(g):
        for i, name in enumerate(extra):
            go(fc(g, i, name))
            fc(g, i, name).wait_recv()
            zout[g, ways + i] = add_low(zout[g, ways - 1 + i], far[g, i])
    def sp(g):
        sz(g, ways - 1)
        sfar(g)
        mine_out(g).start()
        for i in (0, 1, 4):
            go(pc(g, i))
    def sq(g):
        pc(g, 0, True).wait_recv()
        go(pc(g, 2)); go(pc(g, 5))
        pc(g, 1, True).wait_recv()
        go(pc(g, 3)); go(pc(g, 6))
    def sr(g):
        pc(g, 2, True).wait_recv()
        pc(g, 3, True).wait_recv()
        go(pc(g, 7))
    stages = [s1, s2, s3] + [functools.partial(lambda s, g: sz(g, s), s) for s in range(1, ways - 1)] + [sp, sq, sr]
    greet(("core", "x", "y", "up", "down") + tuple(extra), peers)
    for g in range(groups):
        s0(g)
    for wave in range(groups + len(stages) - 1):
        for s in range(len(stages)):
            g = wave - s
            if 0 <= g < groups:
                stages[s](g)
    for g in range(groups):
        for i in range(4, 8):
            pc(g, i, True).wait_recv()
        mine_out(g).wait()
    for c in started:
        c.wait_send()

def reduce_gradients(grads, plan, ways, collective_id):
    groups = len(plan)
    quarter, width = grads[0].shape[3:]
    R = quarter * 4
    rows = R // 8
    half = rows // 2
    nfar = 0
    while 8 << nfar < lax.axis_size("dp"):
        nfar += 1
    per = 6 + ways - 1 + nfar
    def kern(*refs):
        reduce_kernel(plan, ways, refs[: len(grads)], *refs[len(grads) :])
    V = lambda *s: pltpu.VMEM(s, BF16)
    return pl.pallas_call(
        kern,
        out_shape=jax.ShapeDtypeStruct((groups, R, width), BF16),
        in_specs=[ANY] * len(grads), out_specs=ANY,
        scratch_shapes=[V(groups, ways, 2, 2 * rows, width), V(groups, ways, 2, 2 * rows, width),
                        V(groups, ways, 2, half, width), V(groups, ways, 2 * half, width),
                        V(groups, ways, half, width), V(groups, ways, half, width),
                        V(groups, ways, 2, 2 * half, width),
                        V(groups, ways - 1, rows, width), V(groups, ways + nfar, rows, width),
                        V(groups, max(nfar, 1), rows, width),
                        pltpu.SemaphoreType.DMA((groups * 3,)),
                        pltpu.SemaphoreType.DMA((groups * per,)), pltpu.SemaphoreType.DMA((groups * per,)),
                        pltpu.SemaphoreType.DMA((groups * 8,)), pltpu.SemaphoreType.DMA((groups * 8,))],
        compiler_params=pltpu.CompilerParams(collective_id=collective_id, has_side_effects=True, vmem_limit_bytes=60 << 20),
        name="reduce_gradients",
    )(*grads)


def flip(value, bit):
    size = lax.axis_size("dp")
    return lax.ppermute(value, "dp", [(i, i ^ bit) for i in range(size)])


def flip_mp(value, bit):
    size = lax.axis_size("mp")
    return lax.ppermute(value, "mp", [(i, i ^ bit) for i in range(size)])


def ring(value):
    size = lax.axis_size("mp")
    return lax.ppermute(value, "mp", [(i, (i + 1) % size) for i in range(size)])


def swap_if(cond, first, second):
    return jnp.where(cond, second, first), jnp.where(cond, first, second)


def gather_all(rows):
    bit = 1
    while bit < lax.axis_size("mp"):
        other = flip_mp(rows, bit)
        upper = (lax.axis_index("mp") // bit) % 2 == 1
        rows = jnp.concatenate(swap_if(upper, rows, other))
        bit *= 2
    bit = 1
    while bit < lax.axis_size("dp"):
        other = flip(rows, bit)
        upper = (lax.axis_index("dp") // bit) % 2 == 1
        rows = jnp.concatenate(swap_if(upper, rows, other))
        bit *= 2
    return rows


def sum_all(value):
    bit = 1
    while bit < lax.axis_size("dp"):
        value = value + flip(value, bit)
        bit *= 2
    bit = 1
    while bit < lax.axis_size("mp"):
        value = value + flip_mp(value, bit)
        bit *= 2
    return value


def nn(a, b):
    return lax.dot_general(a, b, (((1,), (0,)), ((), ())), preferred_element_type=F32)
def nt(a, b):
    return lax.dot_general(a, b, (((1,), (1,)), ((), ())), preferred_element_type=F32)
def tn(a, b):
    return lax.dot_general(a, b, (((0,), (0,)), ((), ())), preferred_element_type=F32)

def gelu_both(u):
    w = jnp.abs(u) * RSQRT_TWO
    t = 1.0 / (1.0 + 0.3275911 * w)
    e = jnp.exp(-0.5 * u * u)
    poly = ((((1.061405429 * t - 1.453152027) * t + 1.421413741) * t - 0.284496736) * t + 0.254829592) * t
    tail = 0.5 * poly * e
    phi = jnp.where(u >= 0.0, 1.0 - tail, tail)
    return u * phi, phi + u * e * RSQRT_TWOPI

def norm_rows(z, gain, bias):
    c = z - jnp.mean(z, axis=-1, keepdims=True)
    r = lax.rsqrt(jnp.mean(c * c, axis=-1, keepdims=True) + EPS_NORM)
    n = c * r
    return n, r, n * gain + bias

ROWS = 256

class Forward:
    def __init__(self, l, seqs, r):
        self.l, self.seqs, self.r = l, seqs, r
    def blocks(self):
        T = self.r.x.shape[0]
        return [slice(i, i + ROWS) for i in range(0, T, ROWS)]
    def project(self, m):
        r, l = self.r, self.l
        acc = nt(r.xr[l], r.w_attn[m])
        if m == 0:
            r.q[l] = (acc + r.qv_b[l, 0:1]).astype(BF16) * jnp.bfloat16(0.125)
        elif m == 1:
            r.k[l] = acc.astype(BF16)
        else:
            r.v[l] = (acc + r.qv_b[l, 1:2]).astype(BF16)
    def attend(self, s, i):
        r, l = self.r, self.l
        start, n = self.seqs[s]
        rows, lanes = slice(start, start + n), slice(i * 128, i * 128 + 128)
        kp, qp, vp = r.k[l, rows, lanes], r.q[l, rows, lanes], r.v[l, rows, lanes]
        vt = vp.T
        first = lax.broadcasted_iota(jnp.int32, (n, 128), 1) < HEAD_DIM
        bias = jnp.concatenate([r.mask[rows]] * (n // 128), axis=1)
        out = []
        for h in range(2):
            kh = jnp.where(first if h == 0 else ~first, kp, jnp.zeros_like(kp))
            sc = nt(kh, qp) + bias
            top = jnp.max(sc, axis=0, keepdims=True)
            e = jnp.exp(sc - top)
            tot = jnp.sum(e, axis=0, keepdims=True)
            r.lse[l, 2 * i + h:2 * i + h + 1, rows] = top + jnp.log(tot)
            ct = nn(vt[h * HEAD_DIM:(h + 1) * HEAD_DIM], e.astype(BF16))
            out.append(ct * (1.0 / tot))
        ct = jnp.concatenate(out, axis=0)
        r.ctx[l, rows, lanes] = ct.T.astype(BF16)
    def out_norm(self, b):
        r, l = self.r, self.l
        z = r.x[b] + nn(r.ctx[l, b], r.w_attn[3]) + r.out_b[l:l + 1]
        n, inv, h = norm_rows(z, r.gain[l, 0:1], r.bias[l, 0:1])
        r.n1[l, b] = n
        r.r1[l, b] = jnp.broadcast_to(inv, (ROWS, 128))
        r.h[b] = h
        r.hr[l, b] = h.astype(BF16)
    def ffn(self, c, b, slot):
        r, l = self.r, self.l
        u = nn(r.hr[l, b], r.w_up[c]) + r.up_b[l, c:c + 1]
        a, slope = gelu_both(u)
        a = a.astype(BF16)
        r.a[slot, b] = a
        r.slope[slot, b] = slope.astype(BF16)
        f = nn(a, r.w_down[c])
        if c == 0:
            r.f[b] = f
        else:
            r.f[b] += f
    def ffn_norm(self, b, last):
        r, l = self.r, self.l
        z = r.h[b] + r.f[b] + r.down_b[l:l + 1]
        n, inv, y = norm_rows(z, r.gain[l, 1:2], r.bias[l, 1:2])
        r.n2[l, b] = n
        r.r2[l, b] = jnp.broadcast_to(inv, (ROWS, 128))
        r.x[b] = y
        if not last:
            r.xr[l + 1, b] = y.astype(BF16)

class Refs:
    def __init__(self, **k):
        self.__dict__.update(k)

def forward_kernel(seqs, layers, names, *refs):
    r = Refs(**dict(zip(names, refs)))
    ways = r.w.shape[1]
    T = r.x.shape[0]
    for s, (start, n) in enumerate(seqs):
        row = lax.broadcasted_iota(jnp.int32, (n, 128), 0)
        r.mask[start:start + n] = jnp.where(row < r.lens[s], 0.0, NEG_FILL)
    r.xr[0] = r.states[...]
    r.x[...] = r.states[...].astype(F32)
    bufs = [r.w_attn, r.w_up, r.w_down]
    def load(g):
        return pltpu.make_async_copy(r.w.at[g], bufs[g % 3], r.w_sem.at[g])
    for g in range(3):
        load(g).start()
    pend = {}
    outs = []
    def save(l, c, slot):
        for j, (src, dst) in enumerate(((r.a, r.a_out), (r.slope, r.slope_out))):
            cp = pltpu.make_async_copy(src.at[slot], dst.at[l, c], r.s_sem.at[(l * ways + c) * 2 + j])
            cp.start()
            pend.setdefault(slot, []).append(cp)
    for l in range(layers):
        f = Forward(l, seqs, r)
        load(3 * l).wait()
        for m in range(3):
            f.project(m)
        for s in range(len(seqs)):
            for i in range(r.ctx.shape[2] // 128):
                f.attend(s, i)
        for b in f.blocks():
            f.out_norm(b)
        if l + 1 < layers:
            load(3 * l + 3).start()
        load(3 * l + 1).wait()
        load(3 * l + 2).wait()
        for c in range(ways):
            slot = c % 2
            for cp in pend.pop(slot, []):
                cp.wait()
            for b in f.blocks():
                f.ffn(c, b, slot)
            save(l, c, slot)
        if l + 1 < layers:
            load(3 * l + 4).start()
            load(3 * l + 5).start()
        for b in f.blocks():
            f.ffn_norm(b, l + 1 == layers)
    for cps in pend.values():
        for cp in cps:
            cp.wait()

def forward(states, w, lens, small, seqs):
    T, D = states.shape
    G, ways, R, _ = w.shape
    L = G // 3
    V = pl.BlockSpec(memory_space=pltpu.VMEM)
    A = pl.BlockSpec(memory_space=pl.ANY)
    S = pl.BlockSpec(memory_space=pltpu.SMEM)
    snames = ("qv_b", "out_b", "gain", "bias", "up_b", "down_b")
    heads = D // HEAD_DIM
    outs = dict(
        x=((T, D), F32), xr=((L, T, D), BF16), q=((L, T, D), BF16), k=((L, T, D), BF16), v=((L, T, D), BF16),
        ctx=((L, T, D), BF16), n1=((L, T, D), F32), r1=((L, T, 128), F32), hr=((L, T, D), BF16),
        n2=((L, T, D), F32), r2=((L, T, 128), F32), lse=((L, -(-heads // 8) * 8, T), F32),
        a_out=((L, ways, T, R), BF16), slope_out=((L, ways, T, R), BF16))
    scratch = dict(
        mask=pltpu.VMEM((T, 128), F32), h=pltpu.VMEM((T, D), F32), f=pltpu.VMEM((T, D), F32),
        a=pltpu.VMEM((2, T, R), BF16), slope=pltpu.VMEM((2, T, R), BF16),
        w_attn=pltpu.VMEM((ways, R, D), BF16), w_up=pltpu.VMEM((ways, R, D), BF16), w_down=pltpu.VMEM((ways, R, D), BF16),
        w_sem=pltpu.SemaphoreType.DMA((G,)), s_sem=pltpu.SemaphoreType.DMA((L * ways * 2,)))
    names = ("lens", "states", "w") + snames + tuple(outs) + tuple(scratch)
    res = pl.pallas_call(
        functools.partial(forward_kernel, seqs, L, names),
        out_shape=[jax.ShapeDtypeStruct(s, d) for s, d in outs.values()],
        in_specs=[S, V, A] + [V] * len(snames),
        out_specs=[A if n in ("a_out", "slope_out") else V for n in outs],
        scratch_shapes=list(scratch.values()),
        compiler_params=pltpu.CompilerParams(vmem_limit_bytes=62 << 20),
        name="forward_layers",
    )(lens, states, w, *[small[n] for n in snames])
    return dict(zip(outs, res))


def norm_back(g, n, r, gain):
    gn = g * gain
    return r * (gn - jnp.mean(gn, axis=-1, keepdims=True) - n * jnp.mean(gn * n, axis=-1, keepdims=True))

def total(v):
    return jnp.sum(v, axis=0, keepdims=True)

QB, VB, UB, OB, GAIN, BIAS, DB = 0, 1, 2, 6, 7, 9, 11

class Backward:
    def __init__(self, l, seqs, r):
        self.l, self.seqs, self.r = l, seqs, r
        T = r.dy.shape[0]
        self.blocks = [slice(i, i + ROWS) for i in range(0, T, ROWS)]
    def add_row(self, row, value, first):
        r, l = self.r, self.l
        if first:
            r.sums[l, row:row + 1] = value
        else:
            r.sums[l, row:row + 1] += value
    def norm(self, b, which):
        r, l = self.r, self.l
        g = r.dy[b] if which else r.dz[b] + r.acc[b]
        n, inv = r.n[which, b], r.inv[which, b]
        inv = jnp.concatenate([inv] * (n.shape[1] // 128), axis=1)
        dz = norm_back(g, n, inv, r.gain[l, which:which + 1])
        low = dz.astype(BF16)
        r.dz[b] = dz
        r.low[b] = low
        first = b.start == 0
        self.add_row(GAIN + which, total(g * n), first)
        self.add_row(BIAS + which, total(g), first)
        self.add_row(DB if which else OB, total(low.astype(F32)), first)
    def flip(self, dst, src):
        dst[...] = src[...].T
    def ffn_down(self, c, slot):
        r = self.r
        r.stage[0] = nn(r.low_t[...], r.a[slot]).astype(BF16)
    def ffn_mid(self, c, b, slot, w):
        r = self.r
        da = nt(r.low[b], r.w[w])
        du = (da * r.slope[slot, b].astype(F32)).astype(BF16)
        r.du[b] = du
        self.add_row(UB + c, total(du.astype(F32)), b.start == 0)
    def ffn_up(self, c):
        r = self.r
        r.stage[1] = nn(r.hr_t[...], r.du[...]).astype(BF16)
    def ffn_back(self, c, b, w):
        r = self.r
        dh = nt(r.du[b], r.w[w])
        if c == 0:
            r.acc[b] = dh
        else:
            r.acc[b] += dh
    def context(self, b, w):
        r = self.r
        r.dctx[b] = nt(r.low[b], r.w[w]).astype(BF16)
    def out_grad(self, slot):
        r = self.r
        r.stage[slot] = nn(r.ctx[...].T, r.low[...]).astype(BF16)
    def attend(self, s, i):
        r, l = self.r, self.l
        start, n = self.seqs[s]
        rows, lanes = slice(start, start + n), slice(i * 128, i * 128 + 128)
        kp, qp, vp, gp = r.k[rows, lanes], r.q[rows, lanes], r.v[rows, lanes], r.dctx[rows, lanes]
        kt = kp.T
        first = lax.broadcasted_iota(jnp.int32, (n, 128), 1) < HEAD_DIM
        bias = jnp.concatenate([r.mask[rows]] * (n // 128), axis=1)
        dv, dk, dq = [], [], []
        for h in range(2):
            keep = first if h == 0 else ~first
            kh = jnp.where(keep, kp, jnp.zeros_like(kp))
            vh = jnp.where(keep, vp, jnp.zeros_like(vp))
            p = jnp.exp(nt(kh, qp) + bias - r.lse[2 * i + h:2 * i + h + 1, rows])
            dp = nt(vh, gp)
            ds = (p * (dp - jnp.sum(p * dp, axis=0, keepdims=True))).astype(BF16)
            dv.append(nn(p.astype(BF16), gp))
            dk.append(nn(ds, qp))
            dq.append(nn(kt[h * HEAD_DIM:(h + 1) * HEAD_DIM], ds) * 0.125)
        r.dk[rows, lanes] = jnp.where(first, dk[0], dk[1]).astype(BF16)
        r.dv[rows, lanes] = jnp.where(first, dv[0], dv[1]).astype(BF16)
        r.dq[rows, lanes] = jnp.concatenate(dq, axis=0).T.astype(BF16)
    def qkv_grad(self, m, slot):
        r = self.r
        g = (r.dq, r.dk, r.dv)[m][...]
        r.stage[slot] = nn(g.T, r.xr[...]).astype(BF16)
        if m != 1:
            self.add_row(QB if m == 0 else VB, total(g.astype(F32)), True)
    def back_in(self, b, m, w):
        r = self.r
        d = nn((r.dq, r.dk, r.dv)[m][b], r.w[w])
        if m == 0:
            r.dy[b] = r.dz[b] + d
        else:
            r.dy[b] += d

def backward_kernel(seqs, layers, names, *refs):
    r = Refs(**dict(zip(names, refs)))
    ways = r.a_in.shape[1]
    for s, (start, n) in enumerate(seqs):
        row = lax.broadcasted_iota(jnp.int32, (n, 128), 0)
        r.mask[start:start + n] = jnp.where(row < r.lens[s], 0.0, NEG_FILL)
    r.dy[...] = r.dy_in[...]
    nw = r.w.shape[0]
    order = []
    for l in reversed(range(layers)):
        for c in range(ways):
            order += [(3 * l + 2, c), (3 * l + 1, c)]
        order += [(3 * l, m) for m in (3, 0, 1, 2)]
    def wload(i):
        return pltpu.make_async_copy(r.w_in.at[order[i]], r.w.at[i % nw], r.w_sem.at[i])
    state = {"w": 0, "issued": 0}
    def more():
        while state["issued"] < len(order) and state["issued"] < state["w"] + nw:
            wload(state["issued"]).start()
            state["issued"] += 1
    def take():
        i = state["w"]
        wload(i).wait()
        return i % nw
    def done():
        state["w"] += 1
        more()
    items = ("n2", "r2", "hr", "n1", "r1", "ctx", "q", "k", "v", "lse", "xr")
    dst = dict(n2=r.n.at[1], n1=r.n.at[0], r2=r.inv.at[1], r1=r.inv.at[0], hr=r.hr, ctx=r.ctx, q=r.q, k=r.k, v=r.v, lse=r.lse, xr=r.xr)
    src = dict(n2=r.n2_in, n1=r.n1_in, r2=r.r2_in, r1=r.r1_in, hr=r.hr_in, ctx=r.ctx_in, q=r.q_in, k=r.k_in, v=r.v_in, lse=r.lse_in, xr=r.xr_in)
    def load(l, name):
        return pltpu.make_async_copy(src[name].at[l], dst[name], r.i_sem.at[l * len(items) + items.index(name)])
    def aload(l, c, j):
        return pltpu.make_async_copy((r.a_in, r.slope_in)[j].at[l, c], (r.a, r.slope)[j].at[c % 2], r.a_sem.at[(l * ways + c) * 2 + j])
    more()
    top = layers - 1
    for name in items:
        load(top, name).start()
    for j in range(2):
        aload(top, 0, j).start()
        aload(top, 1, j).start()
    pend = {}
    count = [0]
    def slot_for():
        s = count[0] % 2
        return s
    def save(slot, dst_ref, sem):
        cp = pltpu.make_async_copy(r.stage.at[slot], dst_ref, r.o_sem.at[sem])
        cp.start()
        pend[slot] = cp
    def free(slot):
        if slot in pend:
            pend.pop(slot).wait()
    for l in reversed(range(layers)):
        f = Backward(l, seqs, r)
        prev = l - 1
        def again(*nm):
            if prev >= 0:
                for x in nm:
                    load(prev, x).start()
        base = l * (2 * ways + 4)
        load(l, "n2").wait(); load(l, "r2").wait()
        for b in f.blocks:
            f.norm(b, 1)
        again("n2", "r2")
        f.flip(r.low_t, r.low)
        load(l, "hr").wait()
        f.flip(r.hr_t, r.hr)
        again("hr")
        for c in range(ways):
            slot = c % 2
            aload(l, c, 0).wait()
            free(0)
            f.ffn_down(c, slot)
            save(0, r.g_down.at[l, c], base + 2 * c)
            aload(l, c, 1).wait()
            w = take()
            for b in f.blocks:
                f.ffn_mid(c, b, slot, w)
            done()
            nl, nc = (l, c + 2) if c + 2 < ways else (l - 1, c + 2 - ways)
            if nl >= 0:
                for j in range(2):
                    aload(nl, nc, j).start()
            free(1)
            f.ffn_up(c)
            save(1, r.g_up.at[l, c], base + 2 * c + 1)
            w = take()
            for b in f.blocks:
                f.ffn_back(c, b, w)
            done()
        load(l, "n1").wait(); load(l, "r1").wait()
        for b in f.blocks:
            f.norm(b, 0)
        again("n1", "r1")
        w = take()
        for b in f.blocks:
            f.context(b, w)
        done()
        load(l, "ctx").wait()
        free(0)
        f.out_grad(0)
        save(0, r.g_attn.at[l, 3], base + 2 * ways + 3)
        again("ctx")
        for nm in ("q", "k", "v", "lse"):
            load(l, nm).wait()
        for s in range(len(seqs)):
            for i in range(r.q.shape[1] // 128):
                f.attend(s, i)
        again("q", "k", "v", "lse")
        load(l, "xr").wait()
        for m in range(3):
            slot = (m + 1) % 2
            free(slot)
            f.qkv_grad(m, slot)
            save(slot, r.g_attn.at[l, m], base + 2 * ways + m)
            w = take()
            for b in f.blocks:
                f.back_in(b, m, w)
            done()
        again("xr")
    for s in (0, 1):
        free(s)

def backward(dy, saved, w, lens, small, seqs):
    T, D = dy.shape
    G, ways, R, _ = w.shape
    L = G // 3
    V = pl.BlockSpec(memory_space=pltpu.VMEM)
    A = pl.BlockSpec(memory_space=pl.ANY)
    S = pl.BlockSpec(memory_space=pltpu.SMEM)
    ins = dict(lens=(lens, S), dy_in=(dy, V), w_in=(w, A), gain=(small["gain"], V))
    for n in ("n2", "r2", "hr", "n1", "r1", "ctx", "q", "k", "v", "lse", "xr"):
        ins[n + "_in"] = (saved[n], A)
    ins["a_in"] = (saved["a_out"], A)
    ins["slope_in"] = (saved["slope_out"], A)
    outs = dict(dy=((T, D), F32, V), sums=((L, 16, D), F32, V), g_down=((L, ways, D, R), BF16, A), g_up=((L, ways, D, R), BF16, A), g_attn=((L, 4, D, D), BF16, A))
    H = saved["lse"].shape[1]
    VM = pltpu.VMEM
    scratch = dict(
        mask=VM((T, 128), F32), n=VM((2, T, D), F32), inv=VM((2, T, 128), F32), hr=VM((T, D), BF16), hr_t=VM((D, T), BF16),
        low=VM((T, D), BF16), low_t=VM((D, T), BF16), dz=VM((T, D), F32), acc=VM((T, D), F32), du=VM((T, R), BF16),
        a=VM((2, T, R), BF16), slope=VM((2, T, R), BF16), ctx=VM((T, D), BF16), q=VM((T, D), BF16), k=VM((T, D), BF16), v=VM((T, D), BF16),
        xr=VM((T, D), BF16), lse=VM((H, T), F32), dctx=VM((T, D), BF16), dq=VM((T, D), BF16), dk=VM((T, D), BF16), dv=VM((T, D), BF16),
        stage=VM((2, D, R), BF16), w=VM((4, R, D), BF16),
        w_sem=pltpu.SemaphoreType.DMA((L * (2 * ways + 4),)), i_sem=pltpu.SemaphoreType.DMA((L * 11,)), a_sem=pltpu.SemaphoreType.DMA((L * ways * 2,)),
        o_sem=pltpu.SemaphoreType.DMA((L * (2 * ways + 4),)))
    names = tuple(ins) + tuple(outs) + tuple(scratch)
    res = pl.pallas_call(
        functools.partial(backward_kernel, seqs, L, names),
        out_shape=[jax.ShapeDtypeStruct(s, d) for s, d, _ in outs.values()],
        in_specs=[s for _, s in ins.values()],
        out_specs=[s for _, _, s in outs.values()],
        scratch_shapes=list(scratch.values()),
        compiler_params=pltpu.CompilerParams(vmem_limit_bytes=62 << 20),
        name="backward_layers",
    )(*[v for v, _ in ins.values()])
    return dict(zip(outs, res))


def local(
    query_states,
    passage_states,
    query_lengths,
    passage_lengths,
    query_count,
    passage_count,
    positive,
    query_key_value_matrix,
    qv_bias,
    out_weight,
    out_bias,
    norm_gain,
    norm_bias,
    up_matrix,
    up_bias,
    down_matrix,
    down_bias,
):
    layers = query_key_value_matrix.shape[0]
    width = query_states.shape[-1]
    ways = lax.axis_size("mp")
    mp_rank = lax.axis_index("mp")
    my_rank = lax.axis_index("dp") * ways + mp_rank
    q_slots, q_len, _ = query_states.shape
    p_slots, p_len, _ = passage_states.shape
    shapes = ((q_slots, q_len), (p_slots, p_len))
    lengths = (
        lax.dynamic_slice_in_dim(query_lengths, mp_rank * q_slots, q_slots),
        lax.dynamic_slice_in_dim(passage_lengths, mp_rank * p_slots, p_slots),
    )
    part = qv_bias.shape[-1]

    tiny = jnp.concatenate([qv_bias.reshape(layers * 2, part), up_bias.reshape(layers * 4, part)])
    tiny_all = [tiny]
    for _ in range(ways - 1):
        tiny_all.append(ring(tiny_all[-1]))
    tiny_all = jnp.stack(tiny_all).astype(F32)

    qkv_t = jnp.swapaxes(query_key_value_matrix, 2, 3).reshape(layers, 3 * part, width)
    attn_pack = jnp.concatenate([qkv_t, out_weight], axis=1)
    kinds = tuple((i, l, i == 0) for l in range(layers) for i in range(3))
    gathered = gather_weights((attn_pack, up_matrix, down_matrix), kinds, ways, 0)
    small = {
        "qv_b": jnp.stack(
            [tiny_all[:, i].reshape(-1) for i in range(2 * layers)]
        ).reshape(layers, 2, width),
        "up_b": jnp.swapaxes(tiny_all[:, 2 * layers :].reshape(ways, layers, -1), 0, 1),
        "out_b": out_bias.astype(F32),
        "down_b": down_bias.astype(F32),
        "gain": norm_gain.astype(F32),
        "bias": norm_bias.astype(F32),
    }
    seqs, at = [], 0
    for count, length in shapes:
        for _ in range(count):
            seqs.append((at, length))
            at += length
    seqs = tuple(seqs)
    all_lens = jnp.concatenate(lengths)
    states = jnp.concatenate(
        [query_states.reshape(-1, width), passage_states.reshape(-1, width)]
    )
    saved = forward(states, gathered, all_lens, small, seqs)
    x = saved["x"]

    masks, embeds, invs = [], [], []
    start = 0
    for (count, length), lens in zip(shapes, lengths):
        y = x[start : start + count * length].reshape(count, length, width)
        start += count * length
        live = jnp.arange(length, dtype=jnp.int32)[None, :] < lens[:, None]
        mask = live.astype(F32) / lens[:, None].astype(F32)
        pooled = jnp.sum(y * mask[:, :, None], axis=1)
        inv = lax.rsqrt(jnp.sum(pooled * pooled, axis=-1, keepdims=True) + 1e-06)
        masks.append(mask)
        embeds.append(pooled * inv)
        invs.append(inv)

    marks = jnp.zeros((1, width), F32).at[0, :q_slots].set(positive.astype(F32))
    everything = gather_all(jnp.concatenate([embeds[0], embeds[1], marks])[None])
    nq = everything[:, :q_slots].reshape(-1, width)
    np_ = everything[:, q_slots : q_slots + p_slots].reshape(-1, width)
    pos = everything[:, q_slots + p_slots, :q_slots].reshape(-1).astype(jnp.int32)
    num_q, num_p = nq.shape[0], np_.shape[0]
    sims = INV_TEMP * jnp.dot(nq, np_.T, precision=PRECISE_MODE)
    live_p = (jnp.arange(p_slots)[None, :] < passage_count[:, None]).reshape(-1)
    live_q = (jnp.arange(q_slots)[None, :] < query_count[:, None]).reshape(-1).astype(F32)
    masked = jnp.where(live_p[None, :], sims, NEG_FILL)
    top = jnp.max(masked, axis=1, keepdims=True)
    expo = jnp.exp(masked - top)
    total = jnp.sum(expo, axis=1, keepdims=True)
    lse = top[:, 0] + jnp.log(total[:, 0])
    is_pos = (jnp.arange(num_p, dtype=jnp.int32)[None, :] == pos[:, None]).astype(F32)
    pos_score = jnp.sum(is_pos * sims, axis=1)
    live_total = jnp.sum(query_count).astype(F32)
    loss = jnp.sum(live_q * (lse - pos_score)) / live_total
    grad_scale = float(num_q * q_len)
    ds = (grad_scale * live_q / live_total)[:, None] * (expo / total - is_pos)
    my_ds = lax.dynamic_slice_in_dim(ds, my_rank * q_slots, q_slots, axis=0)
    my_dst = lax.dynamic_slice_in_dim(ds.T, my_rank * p_slots, p_slots, axis=0)
    dnq = INV_TEMP * jnp.dot(my_ds, np_, precision=PRECISE_MODE)
    dnp = INV_TEMP * jnp.dot(my_dst, nq, precision=PRECISE_MODE)
    dys = []
    for grad, normed, inv, mask in zip((dnq, dnp), embeds, invs, masks):
        pooled_grad = inv * (grad - normed * jnp.sum(normed * grad, axis=-1, keepdims=True))
        dys.append((mask[:, :, None] * pooled_grad[:, None, :]).reshape(-1, width))
    dy = jnp.concatenate(dys)

    back = backward(dy, saved, gathered, all_lens, small, seqs)
    dy = back["dy"]
    parts = [
        back[name].reshape(layers, 4, 4, -1, width) for name in ("g_down", "g_up", "g_attn")
    ]
    plan = tuple((i, l, i == 2) for l in reversed(range(layers)) for i in range(3))
    reduced = reduce_gradients(parts, plan, ways, 1)
    in_order = lambda i: jnp.stack(
        [reduced[plan.index((i, l, i == 2))] for l in range(layers)]
    ).astype(F32)
    sums = back["sums"]
    hidden = up_bias.shape[-1]
    qv_rel = sums[:, QB : VB + 1].reshape(layers, 2, ways, part)
    up_rel = sums[:, UB : UB + ways]
    turn = lambda rel, axis: jnp.concatenate(
        [
            lax.dynamic_slice_in_dim(rel, (mp_rank - j) % ways, 1, axis=axis)
            for j in range(ways)
        ],
        axis=axis,
    )
    small_all = sum_all(
        jnp.concatenate(
            [
                turn(qv_rel, 2).reshape(layers, 2, width),
                turn(up_rel, 1),
                sums[:, UB + ways : DB + 1],
            ],
            axis=1,
        )
    )

    query_grad = dy[: q_slots * q_len].reshape(query_states.shape)
    passage_grad = dy[q_slots * q_len :].reshape(passage_states.shape)
    attn_out = in_order(2)
    qkv_grad = jnp.swapaxes(attn_out[:, : 3 * part].reshape(layers, 3, part, width), 2, 3)
    out_grad = attn_out[:, 3 * part :]
    up_grad = in_order(1)
    down_grad = jnp.swapaxes(in_order(0), 1, 2)
    cut = lambda lo, hi: small_all[:, lo:hi]
    qv_rows = cut(0, 2)
    qv_grad = lax.dynamic_slice_in_dim(qv_rows, mp_rank * part, part, axis=2)
    up_rows = cut(2, 2 + ways * hidden // width).reshape(layers, -1)
    up_b_grad = lax.dynamic_slice_in_dim(up_rows, mp_rank * hidden, hidden, axis=1)
    base = 2 + ways * hidden // width
    return (
        loss,
        query_grad,
        passage_grad,
        qkv_grad,
        qv_grad,
        out_grad,
        cut(base, base + 1)[:, 0],
        cut(base + 1, base + 3),
        cut(base + 3, base + 5),
        up_grad,
        up_b_grad,
        down_grad,
        cut(base + 5, base + 6)[:, 0],
    )


def solution(mesh):
    placed = (
        P(("dp", "mp"), None, None),
        P(("dp", "mp"), None, None),
        P("dp"),
        P("dp"),
        P(),
        P(),
        P(("dp", "mp")),
        P(None, None, None, "mp"),
        P(None, None, "mp"),
        P(None, "mp", None),
        P(),
        P(),
        P(),
        P(None, None, "mp"),
        P(None, "mp"),
        P(None, "mp", None),
        P(),
    )
    return jax.shard_map(
        local,
        mesh=mesh,
        in_specs=placed,
        out_specs=(
            P(),
            P(("dp", "mp"), None, None),
            P(("dp", "mp"), None, None),
            P(None, None, None, "mp"),
            P(None, None, "mp"),
            P(None, "mp", None),
            P(),
            P(),
            P(),
            P(None, None, "mp"),
            P(None, "mp"),
            P(None, "mp", None),
            P(),
        ),
        check_vma=False,
    )
```

```python
import functools
import math

import jax
import jax.numpy as jnp
from jax import lax
from jax.experimental import pallas as pl
from jax.experimental.pallas import tpu as pltpu
from jax.sharding import PartitionSpec as P

HEAD_DIM = 64
EPS_NORM = 1e-12
INV_TEMP = 50.0
PRECISE_MODE = lax.Precision.HIGHEST
NEG_FILL = -1e30
RSQRT_TWO = 1.0 / math.sqrt(2.0)
RSQRT_TWOPI = 1.0 / math.sqrt(2.0 * math.pi)
F32 = jnp.float32
BF16 = jnp.bfloat16


ANY = pl.BlockSpec(memory_space=pl.ANY)

def place():
    d = lax.axis_index("dp")
    z = lax.axis_index("mp")
    nz = lax.axis_size("mp")
    core, px, py = d % 2, (d // 2) % 2, (d // 4) % 2
    peers = {
        "core": {"dp": d + 1 - 2 * core},
        "x": {"dp": d + 2 - 4 * px},
        "y": {"dp": d + 4 - 8 * py},
        "up": {"mp": lax.rem(z + 1, nz)},
        "down": {"mp": lax.rem(z + nz - 1, nz)},
    }
    return core, px, py, peers

def greet(names, peers):
    sem = pltpu.get_barrier_semaphore()
    for n in names:
        pl.semaphore_signal(sem, inc=1, device_id=peers[n], device_id_type=pl.DeviceIdType.MESH)
    pl.semaphore_wait(sem, len(names))

def spot(core, px, py):
    return core * 4 + py * 2 + px


def nn(a, b):
    return lax.dot_general(a, b, (((1,), (0,)), ((), ())), preferred_element_type=F32)
def nt(a, b):
    return lax.dot_general(a, b, (((1,), (1,)), ((), ())), preferred_element_type=F32)
def tn(a, b):
    return lax.dot_general(a, b, (((0,), (0,)), ((), ())), preferred_element_type=F32)

def gelu_both(u):
    w = jnp.abs(u) * RSQRT_TWO
    t = 1.0 / (1.0 + 0.3275911 * w)
    e = jnp.exp(-0.5 * u * u)
    poly = ((((1.061405429 * t - 1.453152027) * t + 1.421413741) * t - 0.284496736) * t + 0.254829592) * t
    tail = 0.5 * poly * e
    phi = jnp.where(u >= 0.0, 1.0 - tail, tail)
    return u * phi, phi + u * e * RSQRT_TWOPI

def norm_rows(z, gain, bias):
    c = z - jnp.mean(z, axis=-1, keepdims=True)
    r = lax.rsqrt(jnp.mean(c * c, axis=-1, keepdims=True) + EPS_NORM)
    n = c * r
    return n, r, n * gain + bias

ROWS = 256

class Refs:
    def __init__(self, **k):
        self.__dict__.update(k)

def far_peers():
    d = lax.axis_index("dp")
    found = {}
    bit = 8
    while bit < lax.axis_size("dp"):
        high = (d // bit) % 2
        found[f"far{bit}"] = {"dp": d + bit - 2 * bit * high}
        bit *= 2
    return found


class Weights:
    def __init__(self, r, ways, layers):
        self.r, self.ways, self.layers = r, ways, layers
        self.core, self.px, self.py, self.peers = place()
        core, px, py = self.core, self.px, self.py
        self.rows = r.w.shape[3] // 2
        self.part = r.w.shape[3]
        self.me = spot(core, px, py)
        sx, sy, sd = spot(core, 1 - px, py), spot(core, px, 1 - py), spot(core, 1 - px, 1 - py)
        half = self.rows // 2
        self.plane = [
            ("x", self.me, sx, 0, self.rows), ("y", self.me, sy, 0, self.rows),
            ("y", sx, sd, 0, half), ("x", sy, sd, half, half),
            ("core", self.me, spot(1 - core, px, py), 0, self.rows),
            ("core", sx, spot(1 - core, 1 - px, py), 0, self.rows),
            ("core", sy, spot(1 - core, px, 1 - py), 0, self.rows),
            ("core", sd, spot(1 - core, 1 - px, 1 - py), 0, self.rows),
        ]
    def region(self, l, j, k, slot, lo=0, n=None):
        n = self.rows if n is None else n
        rows = pl.ds(pl.multiple_of((slot % 2) * self.rows + lo, 16), n)
        if j == 0:
            return self.r.w.at[3 * l, slot // 2, k, rows]
        return self.r.w.at[3 * l + j, k, slot // 2, rows]
    def source(self, l, j):
        return (self.r.pack, self.r.up_w, self.r.down_w)[j].at[l]
    def remote(self, src, dst, send, recv, index, peer):
        return pltpu.make_async_remote_copy(
            src_ref=src, dst_ref=dst, send_sem=send.at[index], recv_sem=recv.at[index],
            device_id=self.peers[peer], device_id_type=pl.DeviceIdType.MESH)
    def z_copy(self, l, j, k):
        if k == 1:
            src = self.source(l, j).at[pl.ds(pl.multiple_of(self.me * self.rows, 16), self.rows)]
        else:
            src = self.region(l, j, k - 1, self.me)
        return self.remote(src, self.region(l, j, k, self.me), self.r.z_send, self.r.z_recv, (l * 3 + j) * (self.ways - 1) + k - 1, "z1")
    def p_copy(self, l, j, k, i, received=False):
        peer, sent, got, lo, n = self.plane[i]
        reg = self.region(l, j, k, got if received else sent, lo, n)
        index = ((l * 3 + j) * (self.ways - 1) + k - 1) * len(self.plane) + i
        return self.remote(reg, reg, self.r.p_send, self.r.p_recv, index, peer)
    def own_copy(self, l, j):
        src, dst = self.source(l, j), self.r.w.at[3 * l + j, 0]
        if j == 0:
            dst = self.r.w.at[3 * l, :, 0]
        return self.remote(src.reshape(4, self.part, src.shape[-1]), dst, self.r.own_send, self.r.own_recv, l * 3 + j, "core")
    def first(self, l, j, k):
        self.z_copy(l, j, k).wait_recv()
        if k + 1 < self.ways:
            self.z_copy(l, j, k + 1).start()
        else:
            @pl.when(l + 1 < self.layers)
            def _():
                self.z_copy(l + 1, j, 1).start()
        for i in (0, 1, 4):
            self.p_copy(l, j, k, i).start()
    def second(self, l, j, k):
        self.p_copy(l, j, k, 0, True).wait_recv()
        self.p_copy(l, j, k, 2).start()
        self.p_copy(l, j, k, 5).start()
        self.p_copy(l, j, k, 1, True).wait_recv()
        self.p_copy(l, j, k, 3).start()
        self.p_copy(l, j, k, 6).start()
    def third(self, l, j, k):
        self.p_copy(l, j, k, 2, True).wait_recv()
        self.p_copy(l, j, k, 3, True).wait_recv()
        self.p_copy(l, j, k, 7).start()
    def tick(self, l, step):
        last = self.ways - 1
        def group(n):
            return l + n // 3, n % 3
        now = [(*group(step + i), last - i) for i in range(last)]
        before = [(*group(step - 1 + i), last - i) for i in range(last)]
        def op(kind, item):
            def go():
                if item[0] is l:
                    kind(*item)
                else:
                    @pl.when(item[0] < self.layers)
                    def _():
                        kind(*item)
            return go
        line = before[1:] + now
        ops = []
        for i, item in enumerate(now):
            ops.append(op(self.first, item))
            ops.append(op(self.second, line[last - 2 + i]))
            ops.append(op(self.third, line[last - 3 + i]))
        return ops
    def arrived(self, l, j):
        for k in range(1, self.ways):
            for i in range(4, 8):
                self.p_copy(l, j, k, i, True).wait_recv()
        self.own_copy(l, j).wait_recv()
    def sent(self, l, j):
        for k in range(1, self.ways):
            self.z_copy(l, j, k).wait_send()
            for i in range(len(self.plane)):
                self.p_copy(l, j, k, i).wait_send()
        self.own_copy(l, j).wait_send()

QB, VB, UB, OB, GAIN, BIAS, DB = 0, 1, 2, 6, 7, 9, 11

class Forward:
    def __init__(self, l, seqs, r):
        self.l, self.seqs, self.r = l, seqs, r
        T = r.x.shape[0]
        self.blocks = [slice(i, i + ROWS) for i in range(0, T, ROWS)]
    def par(self, row):
        return self.r.par[self.l, row:row + 1]
    def project(self, m):
        r, l = self.r, self.l
        acc = nt(r.xr[...], r.w_attn[m].reshape(-1, r.x.shape[1]))
        if m == 0:
            r.q[...] = (acc + self.par(QB)).astype(BF16) * jnp.bfloat16(0.125)
        elif m == 1:
            r.k[...] = acc.astype(BF16)
        else:
            r.v[...] = (acc + self.par(VB)).astype(BF16)
    def attend(self, s, i):
        r, l = self.r, self.l
        start, n = self.seqs[s]
        rows = slice(start, start + n)
        lanes = pl.ds(pl.multiple_of(i * 128, 128), 128)
        kp, qp, vp = r.k[rows, lanes], r.q[rows, lanes], r.v[rows, lanes]
        vt = vp.T
        first = lax.broadcasted_iota(jnp.int32, (n, 128), 1) < HEAD_DIM
        bias = jnp.concatenate([r.mask[rows]] * (n // 128), axis=1)
        out = []
        for h in range(2):
            kh = jnp.where(first if h == 0 else ~first, kp, jnp.zeros_like(kp))
            sc = nt(kh, qp) + bias
            top = jnp.max(sc, axis=0, keepdims=True)
            e = jnp.exp(sc - top)
            tot = jnp.sum(e, axis=0, keepdims=True)
            r.lse[i, h:h + 1, rows] = top + jnp.log(tot)
            ct = nn(vt[h * HEAD_DIM:(h + 1) * HEAD_DIM], e.astype(BF16))
            out.append(ct * (1.0 / tot))
        ct = jnp.concatenate(out, axis=0)
        r.ctx[rows, lanes] = ct.T.astype(BF16)
    def out_norm(self, b):
        r, l = self.r, self.l
        z = r.x[b] + nn(r.ctx[b], r.w_attn[3].reshape(-1, r.x.shape[1])) + self.par(OB)
        n, inv, h = norm_rows(z, self.par(GAIN), self.par(BIAS))
        r.n1[b] = n
        r.r1[b] = jnp.broadcast_to(inv, (ROWS, 128))
        r.hr[b] = h.astype(BF16)
        r.x[b] = h + self.par(DB)
    def ffn(self, c, b, slot):
        r, l = self.r, self.l
        u = nn(r.hr[b], r.w_up[c].reshape(r.x.shape[1], -1)) + r.up_b[l, c]
        a, slope = gelu_both(u)
        a = a.astype(BF16)
        r.a[slot, b] = a
        r.slope[slot, b] = slope.astype(BF16)
        r.x[b] += nn(a, r.w_down[c].reshape(-1, r.x.shape[1]))
    def ffn_norm(self, b):
        r, l = self.r, self.l
        n, inv, y = norm_rows(r.x[b], self.par(GAIN + 1), self.par(BIAS + 1))
        r.n2[b] = n
        r.r2[b] = jnp.broadcast_to(inv, (ROWS, 128))
        r.x[b] = y
        r.xr[b] = y.astype(BF16)

def contrast(r, z, seqs, ways, extra):
    d, me = lax.axis_index("dp"), lax.axis_index("mp")
    rank = d * ways + me
    q_slots, p_slots = r.q_in.shape[0], r.p_in.shape[0]
    width = r.x.shape[1]
    parts = width // 128
    shape = r.emb.shape
    count = 1
    for size in shape[:-2]:
        count *= size
    block = shape[-2]
    flat = r.emb.reshape(count * block, 128)
    invs, sizes = [], []
    lane = lax.broadcasted_iota(jnp.int32, (1, 128), 1)
    for s, (start, n) in enumerate(seqs):
        row = lax.broadcasted_iota(jnp.int32, (n, 128), 0)
        live = jnp.concatenate([row < r.lens[s]] * parts, axis=1)
        size = jnp.full((1, 1), r.lens[s], jnp.int32).astype(F32)
        pooled = jnp.sum(jnp.where(live, r.x[start:start + n], 0.0), axis=0, keepdims=True) / size
        inv = lax.rsqrt(jnp.sum(pooled * pooled, axis=1, keepdims=True) + 1e-06)
        normed = pooled * inv
        for c in range(parts):
            r.own_rows[s * parts + c:s * parts + c + 1] = normed[:, c * 128:(c + 1) * 128]
        invs.append(inv)
        sizes.append(size)
    at = len(seqs) * parts
    marks = jnp.zeros((1, 128), F32)
    values = [r.positive[j] for j in range(q_slots)] + [r.q_count[rank], r.p_count[rank]]
    for i, value in enumerate(values):
        marks = jnp.where(lane == i, jnp.full((1, 128), value, jnp.int32).astype(F32), marks)
    r.own_rows[at:] = jnp.zeros((block - at, 128), F32)
    r.own_rows[at:at + 1] = marks
    flat[pl.ds(pl.multiple_of(rank * block, 8), block)] = r.own_rows[...]
    bits = []
    bit = lax.axis_size("dp") // 2
    while bit:
        bits.append(bit)
        bit //= 2
    name_of = {1: "core", 2: "x", 4: "y"}
    mine = [(d // b) % 2 for b in bits]
    steps = []
    span = 1
    while span < ways:
        low = me - lax.rem(me, span)
        other = me + span - 2 * span * lax.rem(me // span, 2)
        steps.append((tuple(mine) + (pl.ds(low, span),), tuple(mine) + (pl.ds(other - lax.rem(other, span), span),), {"mp": other}))
        span *= 2
    held = list(mine)
    for i, b in enumerate(bits):
        there = list(held)
        there[i] = 1 - mine[i]
        steps.append((tuple(held), tuple(there), z.peers[name_of.get(b, f"far{b}")]))
        held[i] = slice(None)
    copies = []
    for i, (here, there, peer) in enumerate(steps):
        def move(where):
            return pltpu.make_async_remote_copy(
                src_ref=r.emb.at[where], dst_ref=r.emb.at[where], send_sem=r.e_send.at[i], recv_sem=r.e_recv.at[i],
                device_id=peer, device_id_type=pl.DeviceIdType.MESH)
        copies.append(move(here))
        copies[-1].start()
        move(there).wait_recv()
    def rows(i):
        return flat[pl.ds(i, count, stride=block), :]
    def precise(a, b, dims):
        return lax.dot_general(a, b, (dims, ((), ())), precision=PRECISE_MODE, preferred_element_type=F32)
    q = [[rows(j * parts + c) for c in range(parts)] for j in range(q_slots)]
    p = [[rows((q_slots + i) * parts + c) for c in range(parts)] for i in range(p_slots)]
    marks = rows(at)
    marks_t = marks.T
    down = lax.broadcasted_iota(jnp.int32, (count, count), 0)
    across = lax.broadcasted_iota(jnp.int32, (count, count), 1)
    live_total = jnp.sum(marks[:, q_slots:q_slots + 1], axis=0, keepdims=True)
    scale = float(count * q_slots * seqs[0][1])
    loss = jnp.zeros((1, 1), F32)
    dn = [[jnp.zeros((1, 128), F32) for _ in range(parts)] for _ in seqs]
    for j in range(q_slots):
        sims, masked, is_pos = [], [], []
        for i in range(p_slots):
            s = precise(q[j][0], p[i][0], ((1,), (1,)))
            for c in range(1, parts):
                s = s + precise(q[j][c], p[i][c], ((1,), (1,)))
            s = INV_TEMP * s
            sims.append(s)
            masked.append(jnp.where(marks_t[q_slots + 1:q_slots + 2] > i, s, NEG_FILL))
            is_pos.append(jnp.where((across * p_slots + i).astype(F32) == marks[:, j:j + 1], 1.0, 0.0))
        top = functools.reduce(jnp.maximum, [jnp.max(s, axis=1, keepdims=True) for s in masked])
        expo = [jnp.exp(s - top) for s in masked]
        tot = sum(jnp.sum(e, axis=1, keepdims=True) for e in expo)
        pos = sum(jnp.sum(m * s, axis=1, keepdims=True) for m, s in zip(is_pos, sims))
        live = jnp.where(marks[:, q_slots:q_slots + 1] > j, 1.0, 0.0)
        loss = loss + jnp.sum(live * (top + jnp.log(tot) - pos), axis=0, keepdims=True)
        for i in range(p_slots):
            ds = (scale * live / live_total) * (expo[i] / tot - is_pos[i])
            row = jnp.sum(jnp.where(down == rank, ds, 0.0), axis=0, keepdims=True)
            row = jnp.broadcast_to(row, (8, count))
            col = jnp.sum(jnp.where(across == rank, ds, 0.0), axis=1, keepdims=True)
            for c in range(parts):
                dn[j][c] = dn[j][c] + INV_TEMP * precise(row, p[i][c], ((1,), (0,)))[0:1]
                dn[q_slots + i][c] = dn[q_slots + i][c] + INV_TEMP * jnp.sum(col * q[j][c], axis=0, keepdims=True)
    r.loss[...] = jnp.broadcast_to(loss / live_total, r.loss.shape)
    r.token[...] = jnp.zeros(r.token.shape, F32)
    for s in range(len(seqs)):
        normed = [r.own_rows[s * parts + c:s * parts + c + 1] for c in range(parts)]
        along = sum(jnp.sum(a * b, axis=1, keepdims=True) for a, b in zip(normed, dn[s]))
        for c in range(parts):
            r.token[s:s + 1, c * 128:(c + 1) * 128] = invs[s] * (dn[s][c] - normed[c] * along) / sizes[s]
    for copy in copies:
        copy.wait_send()


def forward_kernel(seqs, layers, ways, names, *refs):
    r = Refs(**dict(zip(names, refs)))
    z = Weights(r, ways, layers)
    width = r.x.shape[1]
    zpeers = []
    for k in range(1, ways):
        zpeers.append(f"z{k}")
        z.peers[f"z{k}"] = {"mp": lax.rem(lax.axis_index("mp") + k, ways)}
    part = z.part
    for l in range(layers):
        for m in range(3):
            r.pack[l, m * part:(m + 1) * part] = r.qkv_w[l, m]
        r.pack[l, 3 * part:] = r.out_w[l]
    r.tiny[0] = r.tiny_in[...]
    extra = far_peers()
    z.peers.update(extra)
    greet(["core", "x", "y"] + zpeers + list(extra), z.peers)
    def tiny_copy(k):
        return z.remote(r.tiny.at[0], r.tiny.at[k], r.t_send, r.t_recv, k - 1, f"z{k}")
    z.z_copy(0, 0, 1).start()
    for k in range(1, ways):
        tiny_copy(k).start()
    for l in range(layers):
        for j in range(3):
            z.own_copy(l, j).start()
    for s, (start, n) in enumerate(seqs):
        row = lax.broadcasted_iota(jnp.int32, (n, 128), 0)
        r.mask[start:start + n] = jnp.where(row < r.lens[s], 0.0, NEG_FILL)
    at = 0
    for ref in (r.q_in, r.p_in):
        for i in range(ref.shape[0]):
            r.xr[at:at + ref.shape[1]] = ref[i]
            r.x[at:at + ref.shape[1]] = ref[i].astype(F32)
            at += ref.shape[1]
    out_b, down_b = r.out_b_in[...].astype(F32), r.down_b_in[...].astype(F32)
    for l in range(layers):
        r.par[l, OB:OB + 1] = out_b[l:l + 1]
        r.par[l, DB:DB + 1] = down_b[l:l + 1]
        r.par[l, GAIN:GAIN + 2] = r.gain_in[l].astype(F32)
        r.par[l, BIAS:BIAS + 2] = r.bias_in[l].astype(F32)
    z.first(0, 0, 1)
    z.z_copy(0, 1, 1).start()
    z.z_copy(0, 2, 1).start()
    z.first(0, 0, 2)
    z.second(0, 0, 1)
    z.first(0, 1, 1)
    z.second(0, 0, 2)
    z.third(0, 0, 1)
    z.first(0, 0, 3)
    z.second(0, 1, 1)
    z.third(0, 0, 2)
    z.first(0, 1, 2)
    z.second(0, 0, 3)
    z.third(0, 1, 1)
    for k in range(1, ways):
        tiny_copy(k).wait_recv()
    for l in range(layers):
        for i in range(2):
            row = r.tiny[0, 2 * l + i:2 * l + i + 1].astype(F32)
            for k in range(1, ways):
                row = row + pltpu.roll(r.tiny[k, 2 * l + i:2 * l + i + 1].astype(F32), k * part, 1)
            r.par[l, i:i + 1] = row
        for k in range(ways):
            r.up_b[l, k] = r.tiny[k, 2 * layers + l:2 * layers + l + 1].astype(F32)
    z.first(0, 2, 1)
    z.second(0, 1, 2)
    z.third(0, 0, 3)
    kept = ("xr", "q", "k", "v", "ctx", "lse", "n1", "r1", "hr", "n2", "r2")
    def keep(l, name):
        return pltpu.make_async_copy(getattr(r, name), getattr(r, name + "_out").at[l], r.k_sem.at[l * len(kept) + kept.index(name)])
    bufs = [r.w_attn, r.w_up, r.w_down]
    def load(l, j):
        return pltpu.make_async_copy(r.w.at[3 * l + j], bufs[j], r.w_sem.at[3 * l + j])
    def save(l, c, j):
        src, dst = ((r.a, r.a_out), (r.slope, r.slope_out))[j]
        return pltpu.make_async_copy(src.at[lax.rem(c, 2)], dst.at[l, c], r.s_sem.at[(l * ways + c) * 2 + j])
    z.arrived(0, 0)
    load(0, 0).start()
    pairs = width // 128
    def layer(l, _):
        f = Forward(l, seqs, r)
        more = l + 1 < layers
        early = z.tick(l, 1) + z.tick(l, 2)
        late = z.tick(l, 3)
        def run(ops, n):
            for _ in range(min(n, len(ops))):
                ops.pop(0)()
        keep(l, "xr").start()
        load(l, 0).wait()
        for m in range(3):
            f.project(m)
            keep(l, "qkv"[m]).start()
            run(early, 1)
        def pair(i, _):
            for s in range(len(seqs)):
                f.attend(s, i)
            for at in range(pairs):
                @pl.when(i == at)
                def _():
                    run(early, 2)
            return 0
        lax.fori_loop(0, pairs, pair, 0)
        keep(l, "ctx").start()
        keep(l, "lse").start()
        for b in f.blocks:
            f.out_norm(b)
            run(early, 1)
        for name in ("n1", "r1", "hr"):
            keep(l, name).start()
        run(early, len(early))
        z.arrived(l, 1)
        load(l, 1).start()
        z.arrived(l, 2)
        load(l, 2).start()
        load(l, 1).wait()
        load(l, 2).wait()
        def chunk(c, _):
            @pl.when(c >= 2)
            def _():
                for j in range(2):
                    save(l, c - 2, j).wait()
            for b in f.blocks:
                f.ffn(c, b, lax.rem(c, 2))
            for j in range(2):
                save(l, c, j).start()
            for at in range(ways):
                @pl.when(c == at)
                def _():
                    run(late, 3)
            return 0
        lax.fori_loop(0, ways, chunk, 0)
        for c in range(ways - 2, ways):
            for j in range(2):
                save(l, c, j).wait()
        @pl.when(more)
        def _():
            z.arrived(l + 1, 0)
            load(l + 1, 0).start()
        for name in kept[:-2]:
            keep(l, name).wait()
        @pl.when(l > 0)
        def _():
            for name in kept[-2:]:
                keep(l - 1, name).wait()
        for b in f.blocks:
            f.ffn_norm(b)
        for name in kept[-2:]:
            keep(l, name).start()
        return 0
    lax.fori_loop(0, layers, layer, 0)
    contrast(r, z, seqs, ways, extra)
    def finish(l, _):
        for j in range(3):
            z.sent(l, j)
        return 0
    lax.fori_loop(0, layers, finish, 0)
    for k in range(1, ways):
        tiny_copy(k).wait_send()
    for name in kept[-2:]:
        keep(layers - 1, name).wait()

def forward(query_states, passage_states, qkv_w, out_w, up_w, down_w, lens, targets, tiny, shared, seqs, ways, collective_id):
    D = query_states.shape[-1]
    T = sum(n for _, n in seqs)
    L = qkv_w.shape[0]
    R = up_w.shape[-1]
    G = 3 * L
    V = pl.BlockSpec(memory_space=pltpu.VMEM)
    S = pl.BlockSpec(memory_space=pltpu.SMEM)
    heads = D // HEAD_DIM
    ins = dict(lens=(lens, S), q_in=(query_states, V), p_in=(passage_states, V), qkv_w=(qkv_w, V), out_w=(out_w, V),
               up_w=(up_w, ANY), down_w=(down_w, ANY), tiny_in=(tiny, V))
    for name, value in zip(("out_b_in", "gain_in", "bias_in", "down_b_in"), shared):
        ins[name] = (value, V)
    for name, value in zip(("positive", "q_count", "p_count"), targets):
        ins[name] = (value, S)
    states = dict(xr=((T, D), BF16), q=((T, D), BF16), k=((T, D), BF16), v=((T, D), BF16), ctx=((T, D), BF16),
                  lse=((heads // 2, 8, T), F32), n1=((T, D), F32), r1=((T, 128), F32), hr=((T, D), BF16), n2=((T, D), F32), r2=((T, 128), F32))
    outs = dict(loss=((8, 128), F32, V), token=((-(-len(seqs) // 8) * 8, D), F32, V))
    for name, (shape, kind) in states.items():
        outs[name + "_out"] = ((L, *shape), kind, ANY)
    outs.update(a_out=((L, ways, T, R), BF16, ANY), slope_out=((L, ways, T, R), BF16, ANY), w=((G, ways, 4, R // 4, D), BF16, ANY))
    VM, DMA = pltpu.VMEM, pltpu.SemaphoreType.DMA
    waves = G * (ways - 1)
    scratch = {name: VM(shape, kind) for name, (shape, kind) in states.items()}
    nbits = 0
    while 1 << nbits < lax.axis_size("dp"):
        nbits += 1
    block = -(-(len(seqs) * (D // 128) + 1) // 8) * 8
    scratch.update(
        x=VM((T, D), F32), emb=VM((2,) * nbits + (ways, block, 128), F32), own_rows=VM((block, 128), F32),
        e_send=DMA((nbits + ways,)), e_recv=DMA((nbits + ways,)))
    scratch.update(
        mask=VM((T, 128), F32), par=VM((L, 16, D), F32), up_b=VM((L, ways, 1, R), F32), pack=VM((L, R, D), BF16), tiny=VM((ways, 16, D), BF16),
        a=VM((2, T, R), BF16), slope=VM((2, T, R), BF16),
        w_attn=VM((4, ways, R // 4, D), BF16), w_up=VM((ways, 4, R // 4, D), BF16), w_down=VM((ways, 4, R // 4, D), BF16),
        w_sem=DMA((G,)), s_sem=DMA((L * ways * 2,)), k_sem=DMA((L * 11,)), z_send=DMA((waves,)), z_recv=DMA((waves,)),
        p_send=DMA((waves * 8,)), p_recv=DMA((waves * 8,)), own_send=DMA((G,)), own_recv=DMA((G,)),
        t_send=DMA((ways - 1,)), t_recv=DMA((ways - 1,)))
    names = tuple(ins) + tuple(outs) + tuple(scratch)
    res = pl.pallas_call(
        functools.partial(forward_kernel, seqs, L, ways, names),
        out_shape=[jax.ShapeDtypeStruct(s, d) for s, d, _ in outs.values()],
        in_specs=[s for _, s in ins.values()],
        out_specs=[s for _, _, s in outs.values()],
        scratch_shapes=list(scratch.values()),
        compiler_params=pltpu.CompilerParams(collective_id=collective_id, has_side_effects=True, vmem_limit_bytes=62 << 20),
        name="forward_layers",
    )(*[v for v, _ in ins.values()])
    return {name.removesuffix("_out") if name[:-4] in states else name: value for name, value in zip(outs, res)}


def add_low(a, b):
    return a + b


class Reduce:
    def __init__(self, r, ways, layers):
        self.r, self.ways, self.layers = r, ways, layers
        self.core, self.px, self.py, self.peers = place()
        for k in range(1, ways):
            self.peers[f"z{k}"] = {"mp": lax.rem(lax.axis_index("mp") + k, ways)}
        self.extra = far_peers()
        self.peers.update(self.extra)
        core, px, py = self.core, self.px, self.py
        self.me = spot(core, px, py)
        sx, sy, sd = spot(core, 1 - px, py), spot(core, px, 1 - py), spot(core, 1 - px, 1 - py)
        self.plane = [
            ("x", self.me, sx, None), ("y", self.me, sy, None), ("y", sx, sd, 0), ("x", sy, sd, 1),
            ("core", self.me, spot(1 - core, px, py), None), ("core", sx, spot(1 - core, 1 - px, py), None),
            ("core", sy, spot(1 - core, px, 1 - py), None), ("core", sd, spot(1 - core, 1 - px, 1 - py), None),
        ]
        self.per = 8 + ways - 1 + len(self.extra)
    def remote(self, src, dst, sems, index, peer):
        return pltpu.make_async_remote_copy(
            src_ref=src, dst_ref=dst, send_sem=sems[0].at[index], recv_sem=sems[1].at[index],
            device_id=self.peers[peer], device_id_type=pl.DeviceIdType.MESH)
    def step(self, src, dst, t, j, i, peer):
        return self.remote(src, dst, (self.r.r_send, self.r.r_recv), (3 * t + j) * self.per + i, peer)
    def share(self, t, j, c, i):
        ref = (self.r.g_down, self.r.g_up, self.r.g_attn)[j].at[self.layers - 1 - t]
        return ref.at[2 * c + i] if j == 2 else ref.at[i, pl.ds(2 * c, 2)]
    def place_of(self, ref, j, i):
        return ref.at[:, i] if j == 2 else ref.at[i]
    def pieces(self, j):
        return range(2 if j == 2 else self.ways)
    def load(self, t, j, i):
        return pltpu.make_async_copy(self.share(t, j, self.core, i), self.place_of(self.r.own.at[j], j, i), self.r.l_sem.at[(3 * t + j) * 4 + i])
    def core_copy(self, t, j, i):
        return self.step(self.share(t, j, 1 - self.core, i), self.place_of(self.r.got.at[3 * t + j], j, i), t, j, i, "core")
    def fetch(self, t, j):
        return pltpu.make_async_copy(self.r.got.at[3 * t + j], self.r.got_v, self.r.f_sem.at[3 * t + j])
    def a1(self, t, j):
        return self.step(self.r.own.at[j, :, :, 1 - self.px, 0], self.r.got_a.at[3 * t + j], t, j, 4, "x")
    def b1(self, t, j):
        return self.step(self.r.own.at[j, :, 1 - self.py, :, 1], self.r.got_b.at[3 * t + j], t, j, 5, "y")
    def a2(self, t, j):
        return self.step(self.r.got_a.at[3 * t + j, :, 1 - self.py], self.r.got_c.at[3 * t + j], t, j, 6, "y")
    def b2(self, t, j):
        return self.step(self.r.got_b.at[3 * t + j, :, 1 - self.px], self.r.got_d.at[3 * t + j], t, j, 7, "x")
    def zc(self, t, j, s):
        return self.step(self.r.zout.at[3 * t + j, s - 1], self.r.zin.at[3 * t + j, s - 1], t, j, 7 + s, "z1")
    def slot(self, i):
        return self.ways - 1 if i == 0 else i - 1
    def fc(self, t, j, i, name):
        return self.step(self.r.zout.at[3 * t + j, self.slot(i)], self.r.far.at[3 * t + j, i], t, j, 7 + self.ways + i, name)
    def pc(self, t, j, i, received=False):
        peer, sent, got, h = self.plane[i]
        dst = self.r.reduced.at[3 * t + j, got if received else sent]
        src = self.r.zout.at[3 * t + j, self.slot(len(self.extra))] if i in (0, 1, 4) and not received else dst
        if h is not None:
            src, dst = src.at[h], dst.at[h]
        return self.remote(src, dst, (self.r.g_send, self.r.g_recv), (3 * t + j) * 8 + i, peer)
    def mine(self, t, j):
        return pltpu.make_async_copy(self.r.zout.at[3 * t + j, self.slot(len(self.extra))], self.r.reduced.at[3 * t + j, self.me], self.r.m_sem.at[3 * t + j])
    def s0(self, t, j, i):
        self.core_copy(t, j, i).start()
        self.load(t, j, i).start()
    def s1(self, t, j):
        r = self.r
        for i in self.pieces(j):
            self.core_copy(t, j, i).wait_recv()
        self.fetch(t, j).start()
        for i in self.pieces(j):
            self.load(t, j, i).wait()
        self.fetch(t, j).wait()
        def body(k, _):
            for y in range(2):
                r.own[j, k, y] = add_low(r.own[j, k, y], r.got_v[k, y])
            return 0
        lax.fori_loop(0, self.ways, body, 0)
        self.a1(t, j).start()
        self.b1(t, j).start()
    def s2(self, t, j):
        r, g, px, py = self.r, 3 * t + j, self.px, self.py
        self.a1(t, j).wait_recv()
        def body(k, _):
            for y in range(2):
                r.got_a[g, k, y] = add_low(r.own[j, k, y, px, 0], r.got_a[g, k, y])
            return 0
        lax.fori_loop(0, self.ways, body, 0)
        self.a2(t, j).start()
        self.b1(t, j).wait_recv()
        def body(k, _):
            for x in range(2):
                r.got_b[g, k, x] = add_low(r.own[j, k, py, x, 1], r.got_b[g, k, x])
            return 0
        lax.fori_loop(0, self.ways, body, 0)
        self.b2(t, j).start()
        self.a1(t, j).wait_send()
        self.b1(t, j).wait_send()
    def part(self, g, k):
        r = self.r
        left = add_low(r.got_a[g, k, self.py], r.got_c[g, k])
        right = add_low(r.got_b[g, k, self.px], r.got_d[g, k])
        return left, right
    def s3(self, t, j):
        g = 3 * t + j
        self.a2(t, j).wait_recv()
        self.b2(t, j).wait_recv()
        for h, value in enumerate(self.part(g, 1)):
            self.r.zout[g, 0, h] = value
        self.zc(t, j, 1).start()
    def sz(self, t, j, s):
        r, g = self.r, 3 * t + j
        self.zc(t, j, s).wait_recv()
        for h, value in enumerate(self.part(g, (s + 1) % self.ways)):
            r.zout[g, s, h] = add_low(r.zin[g, s - 1, h], value)
        if s < self.ways - 1:
            self.zc(t, j, s + 1).start()
    def sz1(self, t, j):
        self.sz(t, j, 1)
    def sz2(self, t, j):
        for s in range(2, self.ways - 1):
            self.sz(t, j, s)
    def sp(self, t, j):
        r, g = self.r, 3 * t + j
        self.sz(t, j, self.ways - 1)
        for s in range(1, self.ways):
            self.zc(t, j, s).wait_send()
        for i, name in enumerate(self.extra):
            self.fc(t, j, i, name).start()
            self.fc(t, j, i, name).wait_recv()
            r.zout[g, self.slot(i + 1)] = add_low(r.zout[g, self.slot(i)], r.far[g, i])
        self.mine(t, j).start()
        for i in (0, 1, 4):
            self.pc(t, j, i).start()
    def sq(self, t, j):
        self.pc(t, j, 0, True).wait_recv()
        self.pc(t, j, 2).start()
        self.pc(t, j, 5).start()
        self.pc(t, j, 1, True).wait_recv()
        self.pc(t, j, 3).start()
        self.pc(t, j, 6).start()
    def sr(self, t, j):
        self.pc(t, j, 2, True).wait_recv()
        self.pc(t, j, 3, True).wait_recv()
        self.pc(t, j, 7).start()
    def end(self, t, j):
        for i in range(4, 8):
            self.pc(t, j, i, True).wait_recv()
        self.mine(t, j).wait()
        for i in self.pieces(j):
            self.core_copy(t, j, i).wait_send()
        self.a2(t, j).wait_send()
        self.b2(t, j).wait_send()
        for i, name in enumerate(self.extra):
            self.fc(t, j, i, name).wait_send()
        for i in range(8):
            self.pc(t, j, i).wait_send()


def norm_back(g, n, r, gain):
    gn = g * gain
    return r * (gn - jnp.mean(gn, axis=-1, keepdims=True) - n * jnp.mean(gn * n, axis=-1, keepdims=True))


def total(v):
    return jnp.sum(v, axis=0, keepdims=True)


class Backward:
    def __init__(self, l, seqs, r):
        self.l, self.seqs, self.r = l, seqs, r
        T = r.dy.shape[0]
        self.blocks = [slice(i, i + ROWS) for i in range(0, T, ROWS)]
    def add_row(self, row, value, first):
        r, l = self.r, self.l
        if first:
            r.sums[l, row:row + 1] = value
        else:
            r.sums[l, row:row + 1] += value
    def norm(self, b, which):
        r, l = self.r, self.l
        g = r.dy[b] if which else r.dz[b]
        n, inv = r.n[b], r.inv[b]
        inv = jnp.concatenate([inv] * (n.shape[1] // 128), axis=1)
        dz = norm_back(g, n, inv, r.gain[l, which:which + 1])
        low = dz.astype(BF16)
        r.dz[b] = dz
        r.low[b] = low
        first = b.start == 0
        self.add_row(GAIN + which, total(g * n), first)
        self.add_row(BIAS + which, total(g), first)
        self.add_row(DB if which else OB, total(low.astype(F32)), first)
    def put(self, slot, value):
        stage = self.r.stage
        stage[slot] = value.astype(BF16).reshape(stage.shape[1:])
    def ffn_down(self, slot):
        self.put(0, nn(self.r.low_t[...], self.r.a[slot]))
    def ffn_mid(self, c, b, slot, w):
        r, l = self.r, self.l
        da = nt(r.low[b], r.w[w])
        du = (da * r.slope[slot, b].astype(F32)).astype(BF16)
        r.du[b] = du
        if b.start == 0:
            r.su[l, c] = total(du.astype(F32))
        else:
            r.su[l, c] += total(du.astype(F32))
    def ffn_up(self):
        self.put(1, nn(self.r.hr_t[...], self.r.du[...]))
    def ffn_back(self, b, w):
        r = self.r
        r.dz[b] += nt(r.du[b], r.w[w])
    def context(self, b, w):
        r = self.r
        r.dctx[b] = nt(r.low[b], r.w[w]).astype(BF16)
    def out_grad(self, slot):
        r = self.r
        self.put(slot, nn(r.hc[...].T, r.low[...]))
    def attend(self, s, i):
        r = self.r
        start, n = self.seqs[s]
        rows = slice(start, start + n)
        lanes = pl.ds(pl.multiple_of(i * 128, 128), 128)
        kp, qp, vp, gp = r.k[rows, lanes], r.q[rows, lanes], r.v[rows, lanes], r.dctx[rows, lanes]
        kt = kp.T
        first = lax.broadcasted_iota(jnp.int32, (n, 128), 1) < HEAD_DIM
        bias = jnp.concatenate([r.mask[rows]] * (n // 128), axis=1)
        dv, dk, dq = [], [], []
        for h in range(2):
            keep = first if h == 0 else ~first
            kh = jnp.where(keep, kp, jnp.zeros_like(kp))
            vh = jnp.where(keep, vp, jnp.zeros_like(vp))
            p = jnp.exp(nt(kh, qp) + bias - r.lse[i, h:h + 1, rows])
            dp = nt(vh, gp)
            ds = (p * (dp - jnp.sum(p * dp, axis=0, keepdims=True))).astype(BF16)
            dv.append(nn(p.astype(BF16), gp))
            dk.append(nn(ds, qp))
            dq.append(nn(kt[h * HEAD_DIM:(h + 1) * HEAD_DIM], ds) * 0.125)
        r.dk[rows, lanes] = jnp.where(first, dk[0], dk[1]).astype(BF16)
        r.dv[rows, lanes] = jnp.where(first, dv[0], dv[1]).astype(BF16)
        r.dq[rows, lanes] = jnp.concatenate(dq, axis=0).T.astype(BF16)
    def qkv_grad(self, m, slot):
        r = self.r
        g = (r.dq, r.dk, r.dv)[m][...]
        self.put(slot, nn(g.T, r.du[...]))
        if m != 1:
            self.add_row(QB if m == 0 else VB, total(g.astype(F32)), True)
    def back_in(self, b, m, w):
        r = self.r
        d = nn((r.dq, r.dk, r.dv)[m][b], r.w[w])
        if m == 0:
            r.dy[b] = r.dz[b] + d
        else:
            r.dy[b] += d


def backward_kernel(seqs, layers, ways, names, *refs):
    r = Refs(**dict(zip(names, refs)))
    if r.low_t.shape == r.dy.shape:
        r.dctx, r.dq = r.low_t, r.hr_t
    red = Reduce(r, ways, layers)
    far = list(red.extra)
    greet(["core", "x", "y"] + [f"z{k}" for k in range(1, ways)] + far, red.peers)
    for s, (start, n) in enumerate(seqs):
        row = lax.broadcasted_iota(jnp.int32, (n, 128), 0)
        r.mask[start:start + n] = jnp.where(row < r.lens[s], 0.0, NEG_FILL)
    each = 2 * ways + 4
    heads_order = (3, 0, 1, 2)
    def wload(t, local, group, block):
        return pltpu.make_async_copy(r.w_in.at[group, block], r.w.at[lax.rem(local, 4)], r.w_sem.at[t * each + local])
    def ffn_w(t, c, half):
        return wload(t, 2 * c + half, 3 * (layers - 1 - t) + 2 - half, c)
    def attn_w(t, i):
        return wload(t, 2 * ways + i, 3 * (layers - 1 - t), heads_order[i])
    items = ("n2", "r2", "hr", "n1", "r1", "ctx", "q", "k", "v", "lse", "xr")
    dst = dict(n2=r.n, n1=r.n, r2=r.inv, r1=r.inv, hr=r.hc, ctx=r.hc, q=r.q, k=r.k, v=r.v, lse=r.lse, xr=r.du)
    src = {name: getattr(r, name + "_in") for name in items}
    def load(l, name):
        return pltpu.make_async_copy(src[name].at[l], dst[name], r.i_sem.at[l * len(items) + items.index(name)])
    def aload(l, c, j):
        return pltpu.make_async_copy((r.a_in, r.slope_in)[j].at[l, c], (r.a, r.slope)[j].at[lax.rem(c, 2)], r.a_sem.at[(l * ways + c) * 2 + j])
    def ffn_save(l, c, j):
        return pltpu.make_async_copy(r.stage.at[j], (r.g_down, r.g_up)[j].at[l, c], r.o_sem.at[l * each + 2 * c + j])
    def attn_save(l, m, slot):
        return pltpu.make_async_copy(r.stage.at[slot], r.g_attn.at[l, m], r.o_sem.at[l * each + 2 * ways + m])
    top = layers - 1
    for c in range(2):
        for half in range(2):
            ffn_w(0, c, half).start()
    for name in ("n2", "r2", "hr"):
        load(top, name).start()
    for c in range(2):
        for j in range(2):
            aload(top, c, j).start()
    for name in ("q", "k", "v", "lse"):
        load(top, name).start()
    for s, (start, n) in enumerate(seqs):
        row = lax.broadcasted_iota(jnp.int32, (n, r.dy.shape[1]), 0)
        r.dy[start:start + n] = jnp.where(row < r.lens[s], r.token[s:s + 1], 0.0)
    pairs = r.q.shape[1] // 128

    def layer(t, _):
        l = layers - 1 - t
        f = Backward(l, seqs, r)
        after, more = t > 0, t + 1 < layers
        def old(kind, j):
            def go():
                @pl.when(after)
                def _():
                    kind(t - 1, j)
            return go
        def new(kind, j):
            return lambda: kind(t, j)
        def run(ops, n=1):
            for _ in range(min(n, len(ops))):
                ops.pop(0)()
        def again(*nm):
            @pl.when(more)
            def _():
                for x in nm:
                    load(l - 1, x).start()
        ops = [old(*x) for x in (
            (red.s2, 1), (red.sz1, 0), (red.s1, 2), (red.sz2, 0), (red.s3, 1), (red.sp, 0), (red.sz1, 1), (red.sq, 0), (red.s2, 2),
            (red.sz2, 1), (red.sr, 0), (red.s3, 2), (red.sp, 1), (red.sq, 1), (red.sr, 1))]
        load(l, "n2").wait()
        load(l, "r2").wait()
        for b in f.blocks:
            f.norm(b, 1)
            run(ops)
        load(l, "n1").start()
        load(l, "r1").start()
        r.low_t[...] = r.low[...].T
        load(l, "hr").wait()
        r.hr_t[...] = r.hc[...].T
        load(l, "ctx").start()
        def chunk(c, _):
            slot = lax.rem(c, 2)
            w = 2 * slot
            aload(l, c, 0).wait()
            @pl.when(c > 0)
            def _():
                ffn_save(l, c - 1, 0).wait()
                red.s0(t, 0, c - 1)
            f.ffn_down(slot)
            ffn_save(l, c, 0).start()
            aload(l, c, 1).wait()
            ffn_w(t, c, 0).wait()
            for b in f.blocks:
                f.ffn_mid(c, b, slot, w)
            for half in range(2):
                if half == 1:
                    @pl.when(c > 0)
                    def _():
                        ffn_save(l, c - 1, 1).wait()
                        red.s0(t, 1, c - 1)
                    f.ffn_up()
                    ffn_save(l, c, 1).start()
                    ffn_w(t, c, 1).wait()
                    for b in f.blocks:
                        f.ffn_back(b, w + 1)
                @pl.when(c + 2 < ways)
                def _():
                    ffn_w(t, c + 2, half).start()
                for late in range(2):
                    @pl.when(c == ways - 2 + late)
                    def _():
                        attn_w(t, 2 * late + half).start()
                if half == 0:
                    over = (c + 2) // ways
                    @pl.when(l - over >= 0)
                    def _():
                        for j in range(2):
                            aload(l - over, c + 2 - over * ways, j).start()
            for at in range(ways):
                @pl.when(c == at)
                def _():
                    run(ops, 3)
            return 0
        lax.fori_loop(0, ways, chunk, 0)
        load(l, "xr").start()
        ops = [new(red.s1, 0), new(red.s1, 1), old(red.sz1, 2), old(red.sz2, 2), old(red.sp, 2), new(red.s2, 0), old(red.sq, 2), new(red.s3, 0), old(red.sr, 2)]
        for j in range(2):
            ffn_save(l, ways - 1, j).wait()
            red.s0(t, j, ways - 1)
        load(l, "n1").wait()
        load(l, "r1").wait()
        for b in f.blocks:
            f.norm(b, 0)
        again("n2", "r2")
        run(ops)
        attn_w(t, 0).wait()
        for b in f.blocks:
            f.context(b, 0)
        @pl.when(more)
        def _():
            ffn_w(t + 1, 0, 0).start()
        run(ops)
        load(l, "ctx").wait()
        f.out_grad(0)
        attn_save(l, 3, 0).start()
        again("hr")
        for nm in ("q", "k", "v", "lse"):
            load(l, nm).wait()
        def pair(i, _):
            for s in range(len(seqs)):
                f.attend(s, i)
            for at in (0, 2, 4):
                @pl.when(i == at)
                def _():
                    run(ops)
            return 0
        lax.fori_loop(0, pairs, pair, 0)
        again("q", "k", "v", "lse")
        load(l, "xr").wait()
        for m in range(3):
            slot = (m + 1) % 2
            if m == 1:
                attn_save(l, 3, 0).wait()
            if m == 2:
                attn_save(l, 0, 1).wait()
            f.qkv_grad(m, slot)
            attn_save(l, m, slot).start()
            run(ops)
        run(ops, len(ops))
        attn_save(l, 1, 0).wait()
        attn_save(l, 2, 1).wait()
        for i in red.pieces(2):
            red.s0(t, 2, i)
        for m in range(3):
            attn_w(t, m + 1).wait()
            for b in f.blocks:
                f.back_in(b, m, m + 1)
            @pl.when(more)
            def _():
                ffn_w(t + 1, (m + 1) // 2, (m + 1) % 2).start()
        return 0
    lax.fori_loop(0, layers, layer, 0)

    names_dp = ["core", "x", "y"] + far
    for l in range(layers):
        r.small[0, l] = r.sums[l]
        for c in range(ways):
            r.small[0, l, UB + c:UB + c + 1] = r.su[l, c]
    def sd(i):
        return red.remote(r.small.at[i], r.small_in.at[i], (r.v_send, r.v_recv), i, names_dp[i])
    def sm(k):
        n = len(names_dp)
        return red.remote(r.small.at[n], r.small_in.at[n + k - 1], (r.v_send, r.v_recv), n + k - 1, f"z{k}")
    def small_step(i):
        def go():
            if i > 0:
                sd(i - 1).wait_recv()
                r.small[i] = r.small[i - 1] + r.small_in[i - 1]
            if i < len(names_dp):
                sd(i).start()
            else:
                for k in range(1, ways):
                    sm(k).start()
        return go
    def small_end():
        n = len(names_dp)
        for k in range(1, ways):
            sm(k).wait_recv()
        v = [r.small.at[n]] + [r.small_in.at[n + k - 1] for k in range(1, ways)]
        for l in range(layers):
            part = v[0].shape[-1] // ways
            even, odd = v[0][l], v[1][l]
            for k in range(2, ways):
                if k % 2:
                    odd = odd + v[k][l]
                else:
                    even = even + v[k][l]
            r.small_out[l] = even + odd
            split, up = None, None
            for k in range(ways):
                back = (ways - k) % ways
                row = v[k][l, QB:VB + 1]
                if back:
                    row = pltpu.roll(row, (ways - back) * part, 1)
                split = row if split is None else split + row
                one = v[k][l, UB + back:UB + back + 1]
                up = one if up is None else up + one
            r.small_out[l, QB:VB + 1] = split
            r.small_out[l, UB:UB + 1] = up
    t = layers - 1
    a, b, c = 0, 1, 2
    tail = [(red.s2, b), (red.sz1, a), (red.s1, c), (red.sz2, a), (red.s3, b), (red.sp, a), (red.sz1, b), (red.s2, c), (red.sq, a), (red.sz2, b),
            (red.s3, c), (red.sr, a), (red.sp, b), (red.sz1, c), (red.sq, b), (red.sz2, c), (red.sr, b), (red.sp, c), (red.sq, c), (red.sr, c)]
    smalls = [small_step(i) for i in range(len(names_dp) + 1)]
    for i, (kind, j) in enumerate(tail):
        kind(t, j)
        if smalls and i % 2 == 0:
            smalls.pop(0)()
    for go in smalls:
        go()
    small_end()
    def finish(t, _):
        for j in range(3):
            red.end(t, j)
        return 0
    lax.fori_loop(0, layers, finish, 0)
    for i in range(len(names_dp)):
        sd(i).wait_send()
    for k in range(1, ways):
        sm(k).wait_send()


def backward(saved, w, lens, gain, seqs, collective_id):
    T, D = saved["q"].shape[1:]
    G, ways, R, _ = w.shape
    L = G // 3
    V = pl.BlockSpec(memory_space=pltpu.VMEM)
    S = pl.BlockSpec(memory_space=pltpu.SMEM)
    ins = dict(lens=(lens, S), token=(saved["token"], V), w_in=(w, ANY), gain=(gain, V))
    for n in ("n2", "r2", "hr", "n1", "r1", "ctx", "q", "k", "v", "lse", "xr"):
        ins[n + "_in"] = (saved[n], ANY)
    ins["a_in"] = (saved["a_out"], ANY)
    ins["slope_in"] = (saved["slope_out"], ANY)
    half = R // 16
    block = (2, 2, half, D)
    outs = dict(
        dy=((T, D), F32, V), small_out=((L, 16, D), F32, V), reduced=((G, 8, 2, half, D), BF16, ANY),
        g_down=((L, ways, 4, *block), BF16, ANY), g_up=((L, ways, 4, *block), BF16, ANY), g_attn=((L, 4, ways, *block), BF16, ANY),
        got=((G, ways, 2, *block), BF16, ANY))
    H = saved["lse"].shape[1]
    nfar = 0
    while 8 << nfar < lax.axis_size("dp"):
        nfar += 1
    VM, DMA = pltpu.VMEM, pltpu.SemaphoreType.DMA
    per = 8 + ways - 1 + nfar
    steps = 3 + nfar
    each = 2 * ways + 4
    scratch = dict(
        mask=VM((T, 128), F32), n=VM((T, D), F32), inv=VM((T, 128), F32), hc=VM((T, D), BF16), hr_t=VM((D, T), BF16),
        low=VM((T, D), BF16), low_t=VM((D, T), BF16), dz=VM((T, D), F32), du=VM((T, R), BF16),
        a=VM((2, T, R), BF16), slope=VM((2, T, R), BF16), q=VM((T, D), BF16), k=VM((T, D), BF16), v=VM((T, D), BF16),
        lse=VM((H, 8, T), F32), dk=VM((T, D), BF16), dv=VM((T, D), BF16),
        stage=VM((2, 4, *block), BF16), w=VM((4, R, D), BF16), sums=VM((L, 16, D), F32), su=VM((L, ways, 1, R), F32),
        own=VM((3, ways, 2, *block), BF16), got_v=VM((ways, 2, *block), BF16),
        got_a=VM((G, ways, 2, half, D), BF16), got_b=VM((G, ways, 2, half, D), BF16),
        got_c=VM((G, ways, half, D), BF16), got_d=VM((G, ways, half, D), BF16),
        zin=VM((G, ways - 1, 2, half, D), BF16), zout=VM((G, ways, 2, half, D), BF16),
        small=VM((steps + 1, L, 16, D), F32), small_in=VM((steps + ways - 1, L, 16, D), F32),
        w_sem=DMA((L * each,)), i_sem=DMA((L * 11,)), a_sem=DMA((L * ways * 2,)), o_sem=DMA((L * each,)),
        l_sem=DMA((G * 4,)), f_sem=DMA((G,)), m_sem=DMA((G,)), r_send=DMA((G * per,)), r_recv=DMA((G * per,)),
        g_send=DMA((G * 8,)), g_recv=DMA((G * 8,)), v_send=DMA((steps + ways - 1,)), v_recv=DMA((steps + ways - 1,)))
    if T != D:
        scratch["dctx"] = VM((T, D), BF16)
        scratch["dq"] = VM((T, D), BF16)
    if nfar:
        scratch["far"] = VM((G, nfar, 2, half, D), BF16)
    names = tuple(ins) + tuple(outs) + tuple(scratch)
    res = pl.pallas_call(
        functools.partial(backward_kernel, seqs, L, ways, names),
        out_shape=[jax.ShapeDtypeStruct(s, d) for s, d, _ in outs.values()],
        in_specs=[s for _, s in ins.values()],
        out_specs=[s for _, _, s in outs.values()],
        scratch_shapes=list(scratch.values()),
        compiler_params=pltpu.CompilerParams(collective_id=collective_id, has_side_effects=True, vmem_limit_bytes=255 << 18),
        name="backward_layers",
    )(*[v for v, _ in ins.values()])
    return dict(zip(outs, res))


def finish_kernel(order, reduced, dy, qkv, out, up, down, q_grad, p_grad):
    layers = out.shape[0]
    part = out.shape[1]
    for l in range(layers):
        attn = reduced[order[l, 2]].astype(F32)
        qkv[l] = attn[:3 * part]
        out[l] = attn[3 * part:]
        up[l] = reduced[order[l, 1]].astype(F32)
        down[l] = reduced[order[l, 0]].astype(F32).T
    rows = q_grad.shape[0]
    q_grad[...] = dy[:rows]
    p_grad[...] = dy[rows:]


def finish(reduced, dy, layers, part, rows):
    G, R, D = reduced.shape
    T = dy.shape[0]
    order = {(l, j): 3 * (layers - 1 - l) + j for l in range(layers) for j in range(3)}
    V = pl.BlockSpec(memory_space=pltpu.VMEM)
    shapes = [(layers, 3 * part, D), (layers, part, D), (layers, D, R), (layers, R, D), (rows, D), (T - rows, D)]
    return pl.pallas_call(
        functools.partial(finish_kernel, order),
        out_shape=[jax.ShapeDtypeStruct(s, F32) for s in shapes],
        in_specs=[V, V], out_specs=[V] * 6,
        compiler_params=pltpu.CompilerParams(vmem_limit_bytes=60 << 20),
        name="finish",
    )(reduced, dy)


def local(
    query_states,
    passage_states,
    query_lengths,
    passage_lengths,
    query_count,
    passage_count,
    positive,
    query_key_value_matrix,
    qv_bias,
    out_weight,
    out_bias,
    norm_gain,
    norm_bias,
    up_matrix,
    up_bias,
    down_matrix,
    down_bias,
):
    layers = query_key_value_matrix.shape[0]
    width = query_states.shape[-1]
    ways = lax.axis_size("mp")
    mp_rank = lax.axis_index("mp")
    q_slots, q_len, _ = query_states.shape
    p_slots, p_len, _ = passage_states.shape
    shapes = ((q_slots, q_len), (p_slots, p_len))
    lengths = (
        lax.dynamic_slice_in_dim(query_lengths, mp_rank * q_slots, q_slots),
        lax.dynamic_slice_in_dim(passage_lengths, mp_rank * p_slots, p_slots),
    )
    part = qv_bias.shape[-1]

    hidden = up_bias.shape[-1]
    tiny = jnp.concatenate(
        [
            jnp.pad(qv_bias.reshape(2 * layers, part), ((0, 0), (0, width - part))),
            up_bias,
            jnp.zeros((16 - 3 * layers, width), BF16),
        ]
    )
    seqs, at = [], 0
    for count, length in shapes:
        for _ in range(count):
            seqs.append((at, length))
            at += length
    seqs = tuple(seqs)
    all_lens = jnp.concatenate(lengths)
    saved = forward(
        query_states, passage_states, jnp.swapaxes(query_key_value_matrix, 2, 3), out_weight, up_matrix, down_matrix,
        all_lens, (positive, query_count, passage_count), tiny, (out_bias, norm_gain, norm_bias, down_bias), seqs, ways, 0,
    )
    loss = saved["loss"][0, 0]
    back = backward(
        saved, saved["w"].reshape(3 * layers, 4, -1, width), all_lens, norm_gain.astype(F32), seqs, 1
    )
    reduced = back["reduced"].reshape(3 * layers, -1, width)
    qkv_grad, out_grad, up_grad, down_grad, query_grad, passage_grad = finish(
        reduced, back["dy"], layers, part, q_slots * q_len
    )
    qkv_grad = jnp.swapaxes(qkv_grad.reshape(layers, 3, part, width), 2, 3)
    query_grad = query_grad.reshape(query_states.shape)
    passage_grad = passage_grad.reshape(passage_states.shape)
    small = back["small_out"]

    return (
        loss,
        query_grad,
        passage_grad,
        qkv_grad,
        small[:, QB : VB + 1, :part],
        out_grad,
        small[:, OB],
        small[:, GAIN : GAIN + 2],
        small[:, BIAS : BIAS + 2],
        up_grad,
        small[:, UB, : up_bias.shape[-1]],
        down_grad,
        small[:, DB],
    )


def solution(mesh):
    placed = (
        P(("dp", "mp"), None, None),
        P(("dp", "mp"), None, None),
        P("dp"),
        P("dp"),
        P(),
        P(),
        P(("dp", "mp")),
        P(None, None, None, "mp"),
        P(None, None, "mp"),
        P(None, "mp", None),
        P(),
        P(),
        P(),
        P(None, None, "mp"),
        P(None, "mp"),
        P(None, "mp", None),
        P(),
    )
    return jax.shard_map(
        local,
        mesh=mesh,
        in_specs=placed,
        out_specs=(
            P(),
            P(("dp", "mp"), None, None),
            P(("dp", "mp"), None, None),
            P(None, None, None, "mp"),
            P(None, None, "mp"),
            P(None, "mp", None),
            P(),
            P(),
            P(),
            P(None, None, "mp"),
            P(None, "mp"),
            P(None, "mp", None),
            P(),
        ),
        check_vma=False,
    )
```

```python
import functools
import math

import jax
import jax.numpy as jnp
from jax import lax
from jax.experimental import pallas as pl
from jax.experimental.pallas import tpu as pltpu
from jax.sharding import PartitionSpec as P

HEAD_DIM = 64
EPS_NORM = 1e-12
INV_TEMP = 50.0
PRECISE_MODE = lax.Precision.HIGHEST
NEG_FILL = -1e30
RSQRT_TWO = 1.0 / math.sqrt(2.0)
RSQRT_TWOPI = 1.0 / math.sqrt(2.0 * math.pi)
F32 = jnp.float32
BF16 = jnp.bfloat16


ANY = pl.BlockSpec(memory_space=pl.ANY)

def place():
    d = lax.axis_index("dp")
    z = lax.axis_index("mp")
    nz = lax.axis_size("mp")
    core, px, py = d % 2, (d // 2) % 2, (d // 4) % 2
    peers = {
        "core": {"dp": d + 1 - 2 * core},
        "x": {"dp": d + 2 - 4 * px},
        "y": {"dp": d + 4 - 8 * py},
        "up": {"mp": lax.rem(z + 1, nz)},
        "down": {"mp": lax.rem(z + nz - 1, nz)},
    }
    return core, px, py, peers

def greet(names, peers):
    sem = pltpu.get_barrier_semaphore()
    for n in names:
        pl.semaphore_signal(sem, inc=1, device_id=peers[n], device_id_type=pl.DeviceIdType.MESH)
    pl.semaphore_wait(sem, len(names))

def spot(core, px, py):
    return core * 4 + py * 2 + px


def nn(a, b):
    return lax.dot_general(a, b, (((1,), (0,)), ((), ())), preferred_element_type=F32)
def nt(a, b):
    return lax.dot_general(a, b, (((1,), (1,)), ((), ())), preferred_element_type=F32)
def tn(a, b):
    return lax.dot_general(a, b, (((0,), (0,)), ((), ())), preferred_element_type=F32)

def gelu_both(u):
    w = jnp.abs(u) * RSQRT_TWO
    t = 1.0 / (1.0 + 0.3275911 * w)
    e = jnp.exp(-0.5 * u * u)
    poly = ((((1.061405429 * t - 1.453152027) * t + 1.421413741) * t - 0.284496736) * t + 0.254829592) * t
    tail = 0.5 * poly * e
    phi = jnp.where(u >= 0.0, 1.0 - tail, tail)
    return u * phi, phi + u * e * RSQRT_TWOPI

def norm_rows(z, gain, bias):
    c = z - jnp.mean(z, axis=-1, keepdims=True)
    r = lax.rsqrt(jnp.mean(c * c, axis=-1, keepdims=True) + EPS_NORM)
    n = c * r
    return n, r, n * gain + bias

ROWS = 256

class Refs:
    def __init__(self, **k):
        self.__dict__.update(k)

def far_peers():
    d = lax.axis_index("dp")
    found = {}
    bit = 8
    while bit < lax.axis_size("dp"):
        high = (d // bit) % 2
        found[f"far{bit}"] = {"dp": d + bit - 2 * bit * high}
        bit *= 2
    return found


class Weights:
    def __init__(self, r, ways, layers):
        self.r, self.ways, self.layers = r, ways, layers
        self.core, self.px, self.py, self.peers = place()
        core, px, py = self.core, self.px, self.py
        self.rows = r.w.shape[3] // 2
        self.part = r.w.shape[3]
        self.me = spot(core, px, py)
        sx, sy, sd = spot(core, 1 - px, py), spot(core, px, 1 - py), spot(core, 1 - px, 1 - py)
        half = self.rows // 2
        self.plane = [
            ("x", self.me, sx, 0, self.rows), ("y", self.me, sy, 0, self.rows),
            ("y", sx, sd, 0, half), ("x", sy, sd, half, half),
            ("core", self.me, spot(1 - core, px, py), 0, self.rows),
            ("core", sx, spot(1 - core, 1 - px, py), 0, self.rows),
            ("core", sy, spot(1 - core, px, 1 - py), 0, self.rows),
            ("core", sd, spot(1 - core, 1 - px, 1 - py), 0, self.rows),
        ]
    def region(self, l, j, k, slot, lo=0, n=None):
        n = self.rows if n is None else n
        rows = pl.ds(pl.multiple_of((slot % 2) * self.rows + lo, 16), n)
        if j == 0:
            return self.r.w.at[3 * l, slot // 2, k, rows]
        return self.r.w.at[3 * l + j, k, slot // 2, rows]
    def source(self, l, j):
        return (self.r.pack, self.r.up_w, self.r.down_w)[j].at[l]
    def remote(self, src, dst, send, recv, index, peer):
        return pltpu.make_async_remote_copy(
            src_ref=src, dst_ref=dst, send_sem=send.at[index], recv_sem=recv.at[index],
            device_id=self.peers[peer], device_id_type=pl.DeviceIdType.MESH)
    def z_copy(self, l, j, k):
        if k == 1:
            src = self.source(l, j).at[pl.ds(pl.multiple_of(self.me * self.rows, 16), self.rows)]
        else:
            src = self.region(l, j, k - 1, self.me)
        return self.remote(src, self.region(l, j, k, self.me), self.r.z_send, self.r.z_recv, (l * 3 + j) * (self.ways - 1) + k - 1, "z1")
    def p_copy(self, l, j, k, i, received=False):
        peer, sent, got, lo, n = self.plane[i]
        reg = self.region(l, j, k, got if received else sent, lo, n)
        index = ((l * 3 + j) * (self.ways - 1) + k - 1) * len(self.plane) + i
        return self.remote(reg, reg, self.r.p_send, self.r.p_recv, index, peer)
    def own_copy(self, l, j):
        src, dst = self.source(l, j), self.r.w.at[3 * l + j, 0]
        if j == 0:
            dst = self.r.w.at[3 * l, :, 0]
        return self.remote(src.reshape(4, self.part, src.shape[-1]), dst, self.r.own_send, self.r.own_recv, l * 3 + j, "core")
    def first(self, l, j, k):
        self.z_copy(l, j, k).wait_recv()
        if k + 1 < self.ways:
            self.z_copy(l, j, k + 1).start()
        else:
            @pl.when(l + 1 < self.layers)
            def _():
                self.z_copy(l + 1, j, 1).start()
        for i in (0, 1, 4):
            self.p_copy(l, j, k, i).start()
    def second(self, l, j, k):
        self.p_copy(l, j, k, 0, True).wait_recv()
        self.p_copy(l, j, k, 2).start()
        self.p_copy(l, j, k, 5).start()
        self.p_copy(l, j, k, 1, True).wait_recv()
        self.p_copy(l, j, k, 3).start()
        self.p_copy(l, j, k, 6).start()
    def third(self, l, j, k):
        self.p_copy(l, j, k, 2, True).wait_recv()
        self.p_copy(l, j, k, 3, True).wait_recv()
        self.p_copy(l, j, k, 7).start()
    def tick(self, l, step):
        last = self.ways - 1
        def group(n):
            return l + n // 3, n % 3
        now = [(*group(step + i), last - i) for i in range(last)]
        before = [(*group(step - 1 + i), last - i) for i in range(last)]
        def op(kind, item):
            def go():
                if item[0] is l:
                    kind(*item)
                else:
                    @pl.when(item[0] < self.layers)
                    def _():
                        kind(*item)
            return go
        line = before[1:] + now
        ops = []
        for i, item in enumerate(now):
            ops.append(op(self.first, item))
            ops.append(op(self.second, line[last - 2 + i]))
            ops.append(op(self.third, line[last - 3 + i]))
        return ops
    def arrived(self, l, j):
        for k in range(1, self.ways):
            for i in range(4, 8):
                self.p_copy(l, j, k, i, True).wait_recv()
        self.own_copy(l, j).wait_recv()
    def sent(self, l, j):
        for k in range(1, self.ways):
            self.z_copy(l, j, k).wait_send()
            for i in range(len(self.plane)):
                self.p_copy(l, j, k, i).wait_send()
        self.own_copy(l, j).wait_send()

QB, VB, UB, OB, GAIN, BIAS, DB = 0, 1, 2, 6, 7, 9, 11

class Forward:
    def __init__(self, l, seqs, r):
        self.l, self.seqs, self.r = l, seqs, r
        T = r.x.shape[0]
        self.blocks = [slice(i, i + ROWS) for i in range(0, T, ROWS)]
    def par(self, row):
        return self.r.par[self.l, row:row + 1]
    def project(self, m):
        r, l = self.r, self.l
        acc = nt(r.xr[...], r.w_attn[m].reshape(-1, r.x.shape[1]))
        if m == 0:
            r.q[...] = (acc + self.par(QB)).astype(BF16) * jnp.bfloat16(0.125)
        elif m == 1:
            r.k[...] = acc.astype(BF16)
        else:
            r.v[...] = (acc + self.par(VB)).astype(BF16)
    def attend(self, s, i):
        r, l = self.r, self.l
        start, n = self.seqs[s]
        rows = slice(start, start + n)
        lanes = pl.ds(pl.multiple_of(i * 128, 128), 128)
        kp, qp, vp = r.k[rows, lanes], r.q[rows, lanes], r.v[rows, lanes]
        vt = vp.T
        first = lax.broadcasted_iota(jnp.int32, (n, 128), 1) < HEAD_DIM
        bias = jnp.concatenate([r.mask[rows]] * (n // 128), axis=1)
        out = []
        for h in range(2):
            kh = jnp.where(first if h == 0 else ~first, kp, jnp.zeros_like(kp))
            sc = nt(kh, qp) + bias
            top = jnp.max(sc, axis=0, keepdims=True)
            e = jnp.exp(sc - top)
            tot = jnp.sum(e, axis=0, keepdims=True)
            r.lse[i, h:h + 1, rows] = top + jnp.log(tot)
            ct = nn(vt[h * HEAD_DIM:(h + 1) * HEAD_DIM], e.astype(BF16))
            out.append(ct * (1.0 / tot))
        ct = jnp.concatenate(out, axis=0)
        r.ctx[rows, lanes] = ct.T.astype(BF16)
    def out_norm(self, b):
        r, l = self.r, self.l
        z = r.x[b] + nn(r.ctx[b], r.w_attn[3].reshape(-1, r.x.shape[1])) + self.par(OB)
        n, inv, h = norm_rows(z, self.par(GAIN), self.par(BIAS))
        r.n1[b] = n
        r.r1[b] = jnp.broadcast_to(inv, (ROWS, 128))
        r.hr[b] = h.astype(BF16)
        r.x[b] = h + self.par(DB)
    def ffn(self, c, b, slot):
        r, l = self.r, self.l
        u = nn(r.hr[b], r.w_up[c].reshape(r.x.shape[1], -1)) + r.up_b[l, c]
        a, slope = gelu_both(u)
        a = a.astype(BF16)
        r.a[slot, b] = a
        r.slope[slot, b] = slope.astype(BF16)
        r.x[b] += nn(a, r.w_down[c].reshape(-1, r.x.shape[1]))
    def ffn_norm(self, b):
        r, l = self.r, self.l
        n, inv, y = norm_rows(r.x[b], self.par(GAIN + 1), self.par(BIAS + 1))
        r.n2[b] = n
        r.r2[b] = jnp.broadcast_to(inv, (ROWS, 128))
        r.x[b] = y
        r.xr[b] = y.astype(BF16)

def length(r, ways, s):
    me = lax.axis_index("mp")
    q_slots, p_slots = r.q_lens.shape[0] // ways, r.p_lens.shape[0] // ways
    return r.q_lens[me * q_slots + s] if s < q_slots else r.p_lens[me * p_slots + s - q_slots]


def contrast(r, z, seqs, ways, extra):
    d, me = lax.axis_index("dp"), lax.axis_index("mp")
    rank = d * ways + me
    q_slots, p_slots = r.q_in.shape[0], r.p_in.shape[0]
    width = r.x.shape[1]
    parts = width // 128
    shape = r.emb.shape
    count = 1
    for size in shape[:-2]:
        count *= size
    block = shape[-2]
    flat = r.emb.reshape(count * block, 128)
    invs, sizes = [], []
    lane = lax.broadcasted_iota(jnp.int32, (1, 128), 1)
    for s, (start, n) in enumerate(seqs):
        row = lax.broadcasted_iota(jnp.int32, (n, 128), 0)
        live = jnp.concatenate([row < length(r, ways, s)] * parts, axis=1)
        size = jnp.full((1, 1), length(r, ways, s), jnp.int32).astype(F32)
        pooled = jnp.sum(jnp.where(live, r.x[start:start + n], 0.0), axis=0, keepdims=True) / size
        inv = lax.rsqrt(jnp.sum(pooled * pooled, axis=1, keepdims=True) + 1e-06)
        normed = pooled * inv
        for c in range(parts):
            r.own_rows[s * parts + c:s * parts + c + 1] = normed[:, c * 128:(c + 1) * 128]
        invs.append(inv)
        sizes.append(size)
    at = len(seqs) * parts
    marks = jnp.zeros((1, 128), F32)
    values = [r.positive[j] for j in range(q_slots)] + [r.q_count[rank], r.p_count[rank]]
    for i, value in enumerate(values):
        marks = jnp.where(lane == i, jnp.full((1, 128), value, jnp.int32).astype(F32), marks)
    r.own_rows[at:] = jnp.zeros((block - at, 128), F32)
    r.own_rows[at:at + 1] = marks
    flat[pl.ds(pl.multiple_of(rank * block, 8), block)] = r.own_rows[...]
    bits = []
    bit = lax.axis_size("dp") // 2
    while bit:
        bits.append(bit)
        bit //= 2
    name_of = {1: "core", 2: "x", 4: "y"}
    mine = [(d // b) % 2 for b in bits]
    steps = []
    span = 1
    while span < ways:
        low = me - lax.rem(me, span)
        other = me + span - 2 * span * lax.rem(me // span, 2)
        steps.append((tuple(mine) + (pl.ds(low, span),), tuple(mine) + (pl.ds(other - lax.rem(other, span), span),), {"mp": other}))
        span *= 2
    held = list(mine)
    for i, b in enumerate(bits):
        there = list(held)
        there[i] = 1 - mine[i]
        steps.append((tuple(held), tuple(there), z.peers[name_of.get(b, f"far{b}")]))
        held[i] = slice(None)
    copies = []
    for i, (here, there, peer) in enumerate(steps):
        def move(where):
            return pltpu.make_async_remote_copy(
                src_ref=r.emb.at[where], dst_ref=r.emb.at[where], send_sem=r.e_send.at[i], recv_sem=r.e_recv.at[i],
                device_id=peer, device_id_type=pl.DeviceIdType.MESH)
        copies.append(move(here))
        copies[-1].start()
        move(there).wait_recv()
    def rows(i):
        return flat[pl.ds(i, count, stride=block), :]
    def precise(a, b, dims):
        return lax.dot_general(a, b, (dims, ((), ())), precision=PRECISE_MODE, preferred_element_type=F32)
    q = [[rows(j * parts + c) for c in range(parts)] for j in range(q_slots)]
    p = [[rows((q_slots + i) * parts + c) for c in range(parts)] for i in range(p_slots)]
    marks = rows(at)
    marks_t = marks.T
    down = lax.broadcasted_iota(jnp.int32, (count, count), 0)
    across = lax.broadcasted_iota(jnp.int32, (count, count), 1)
    live_total = jnp.sum(marks[:, q_slots:q_slots + 1], axis=0, keepdims=True)
    scale = float(count * q_slots * seqs[0][1])
    loss = jnp.zeros((1, 1), F32)
    dn = [[jnp.zeros((1, 128), F32) for _ in range(parts)] for _ in seqs]
    for j in range(q_slots):
        sims, masked, is_pos = [], [], []
        for i in range(p_slots):
            s = precise(q[j][0], p[i][0], ((1,), (1,)))
            for c in range(1, parts):
                s = s + precise(q[j][c], p[i][c], ((1,), (1,)))
            s = INV_TEMP * s
            sims.append(s)
            masked.append(jnp.where(marks_t[q_slots + 1:q_slots + 2] > i, s, NEG_FILL))
            is_pos.append(jnp.where((across * p_slots + i).astype(F32) == marks[:, j:j + 1], 1.0, 0.0))
        top = functools.reduce(jnp.maximum, [jnp.max(s, axis=1, keepdims=True) for s in masked])
        expo = [jnp.exp(s - top) for s in masked]
        tot = sum(jnp.sum(e, axis=1, keepdims=True) for e in expo)
        pos = sum(jnp.sum(m * s, axis=1, keepdims=True) for m, s in zip(is_pos, sims))
        live = jnp.where(marks[:, q_slots:q_slots + 1] > j, 1.0, 0.0)
        loss = loss + jnp.sum(live * (top + jnp.log(tot) - pos), axis=0, keepdims=True)
        for i in range(p_slots):
            ds = (scale * live / live_total) * (expo[i] / tot - is_pos[i])
            row = jnp.sum(jnp.where(down == rank, ds, 0.0), axis=0, keepdims=True)
            row = jnp.broadcast_to(row, (8, count))
            col = jnp.sum(jnp.where(across == rank, ds, 0.0), axis=1, keepdims=True)
            for c in range(parts):
                dn[j][c] = dn[j][c] + INV_TEMP * precise(row, p[i][c], ((1,), (0,)))[0:1]
                dn[q_slots + i][c] = dn[q_slots + i][c] + INV_TEMP * jnp.sum(col * q[j][c], axis=0, keepdims=True)
    r.loss[...] = jnp.broadcast_to(loss / live_total, r.loss.shape)
    r.token[...] = jnp.zeros(r.token.shape, F32)
    for s in range(len(seqs)):
        normed = [r.own_rows[s * parts + c:s * parts + c + 1] for c in range(parts)]
        along = sum(jnp.sum(a * b, axis=1, keepdims=True) for a, b in zip(normed, dn[s]))
        for c in range(parts):
            r.token[s:s + 1, c * 128:(c + 1) * 128] = invs[s] * (dn[s][c] - normed[c] * along) / sizes[s]
    for copy in copies:
        copy.wait_send()


def forward_kernel(seqs, layers, ways, names, *refs):
    r = Refs(**dict(zip(names, refs)))
    z = Weights(r, ways, layers)
    width = r.x.shape[1]
    zpeers = []
    for k in range(1, ways):
        zpeers.append(f"z{k}")
        z.peers[f"z{k}"] = {"mp": lax.rem(lax.axis_index("mp") + k, ways)}
    part = z.part
    for l in range(layers):
        for m in range(3):
            r.pack[l, m * part:(m + 1) * part] = r.qkv_w[l, m]
        r.pack[l, 3 * part:] = r.out_w[l]
    r.tiny[0] = r.tiny_in[...]
    extra = far_peers()
    z.peers.update(extra)
    greet(["core", "x", "y"] + zpeers + list(extra), z.peers)
    def tiny_copy(k):
        return z.remote(r.tiny.at[0], r.tiny.at[k], r.t_send, r.t_recv, k - 1, f"z{k}")
    z.z_copy(0, 0, 1).start()
    for k in range(1, ways):
        tiny_copy(k).start()
    for l in range(layers):
        for j in range(3):
            z.own_copy(l, j).start()
    for s, (start, n) in enumerate(seqs):
        row = lax.broadcasted_iota(jnp.int32, (n, 128), 0)
        r.mask[start:start + n] = jnp.where(row < length(r, ways, s), 0.0, NEG_FILL)
    at = 0
    for ref in (r.q_in, r.p_in):
        for i in range(ref.shape[0]):
            r.xr[at:at + ref.shape[1]] = ref[i]
            r.x[at:at + ref.shape[1]] = ref[i].astype(F32)
            at += ref.shape[1]
    out_b, down_b = r.out_b_in[...].astype(F32), r.down_b_in[...].astype(F32)
    for l in range(layers):
        r.par[l, OB:OB + 1] = out_b[l:l + 1]
        r.par[l, DB:DB + 1] = down_b[l:l + 1]
        r.par[l, GAIN:GAIN + 2] = r.gain_in[l].astype(F32)
        r.par[l, BIAS:BIAS + 2] = r.bias_in[l].astype(F32)
    z.first(0, 0, 1)
    z.z_copy(0, 1, 1).start()
    z.z_copy(0, 2, 1).start()
    z.first(0, 0, 2)
    z.second(0, 0, 1)
    z.first(0, 1, 1)
    z.second(0, 0, 2)
    z.third(0, 0, 1)
    z.first(0, 0, 3)
    z.second(0, 1, 1)
    z.third(0, 0, 2)
    z.first(0, 1, 2)
    z.second(0, 0, 3)
    z.third(0, 1, 1)
    for k in range(1, ways):
        tiny_copy(k).wait_recv()
    for l in range(layers):
        for i in range(2):
            row = r.tiny[0, 2 * l + i:2 * l + i + 1].astype(F32)
            for k in range(1, ways):
                row = row + pltpu.roll(r.tiny[k, 2 * l + i:2 * l + i + 1].astype(F32), k * part, 1)
            r.par[l, i:i + 1] = row
        for k in range(ways):
            r.up_b[l, k] = r.tiny[k, 2 * layers + l:2 * layers + l + 1].astype(F32)
    z.first(0, 2, 1)
    z.second(0, 1, 2)
    z.third(0, 0, 3)
    kept = ("xr", "q", "k", "v", "ctx", "lse", "n1", "r1", "hr", "n2", "r2")
    def keep(l, name):
        return pltpu.make_async_copy(getattr(r, name), getattr(r, name + "_out").at[l], r.k_sem.at[l * len(kept) + kept.index(name)])
    bufs = [r.w_attn, r.w_up, r.w_down]
    def load(l, j):
        return pltpu.make_async_copy(r.w.at[3 * l + j], bufs[j], r.w_sem.at[3 * l + j])
    def save(l, c, j):
        src, dst = ((r.a, r.a_out), (r.slope, r.slope_out))[j]
        return pltpu.make_async_copy(src.at[lax.rem(c, 2)], dst.at[l, c], r.s_sem.at[(l * ways + c) * 2 + j])
    z.arrived(0, 0)
    load(0, 0).start()
    pairs = width // 128
    def layer(l, _):
        f = Forward(l, seqs, r)
        more = l + 1 < layers
        early = z.tick(l, 1) + z.tick(l, 2)
        late = z.tick(l, 3)
        def run(ops, n):
            for _ in range(min(n, len(ops))):
                ops.pop(0)()
        keep(l, "xr").start()
        load(l, 0).wait()
        for m in range(3):
            f.project(m)
            keep(l, "qkv"[m]).start()
            run(early, 1)
        def pair(i, _):
            for s in range(len(seqs)):
                f.attend(s, i)
            for at in range(pairs):
                @pl.when(i == at)
                def _():
                    run(early, 2)
            return 0
        lax.fori_loop(0, pairs, pair, 0)
        keep(l, "ctx").start()
        keep(l, "lse").start()
        for b in f.blocks:
            f.out_norm(b)
            run(early, 1)
        for name in ("n1", "r1", "hr"):
            keep(l, name).start()
        run(early, len(early))
        z.arrived(l, 1)
        load(l, 1).start()
        z.arrived(l, 2)
        load(l, 2).start()
        load(l, 1).wait()
        load(l, 2).wait()
        def chunk(c, _):
            @pl.when(c >= 2)
            def _():
                for j in range(2):
                    save(l, c - 2, j).wait()
            for b in f.blocks:
                f.ffn(c, b, lax.rem(c, 2))
            for j in range(2):
                save(l, c, j).start()
            for at in range(ways):
                @pl.when(c == at)
                def _():
                    run(late, 3)
            return 0
        lax.fori_loop(0, ways, chunk, 0)
        for c in range(ways - 2, ways):
            for j in range(2):
                save(l, c, j).wait()
        @pl.when(more)
        def _():
            z.arrived(l + 1, 0)
            load(l + 1, 0).start()
        for name in kept[:-2]:
            keep(l, name).wait()
        @pl.when(l > 0)
        def _():
            for name in kept[-2:]:
                keep(l - 1, name).wait()
        for b in f.blocks:
            f.ffn_norm(b)
        for name in kept[-2:]:
            keep(l, name).start()
        return 0
    lax.fori_loop(0, layers, layer, 0)
    contrast(r, z, seqs, ways, extra)
    def finish(l, _):
        for j in range(3):
            z.sent(l, j)
        return 0
    lax.fori_loop(0, layers, finish, 0)
    for k in range(1, ways):
        tiny_copy(k).wait_send()
    for name in kept[-2:]:
        keep(layers - 1, name).wait()

def forward(query_states, passage_states, qkv_w, out_w, up_w, down_w, q_lens, p_lens, targets, tiny, shared, seqs, ways, collective_id):
    D = query_states.shape[-1]
    T = sum(n for _, n in seqs)
    L = qkv_w.shape[0]
    R = up_w.shape[-1]
    G = 3 * L
    V = pl.BlockSpec(memory_space=pltpu.VMEM)
    S = pl.BlockSpec(memory_space=pltpu.SMEM)
    heads = D // HEAD_DIM
    ins = dict(q_lens=(q_lens, S), p_lens=(p_lens, S), q_in=(query_states, V), p_in=(passage_states, V), qkv_w=(qkv_w, V), out_w=(out_w, V),
               up_w=(up_w, ANY), down_w=(down_w, ANY), tiny_in=(tiny, V))
    for name, value in zip(("out_b_in", "gain_in", "bias_in", "down_b_in"), shared):
        ins[name] = (value, V)
    for name, value in zip(("positive", "q_count", "p_count"), targets):
        ins[name] = (value, S)
    states = dict(xr=((T, D), BF16), q=((T, D), BF16), k=((T, D), BF16), v=((T, D), BF16), ctx=((T, D), BF16),
                  lse=((heads // 2, 8, T), F32), n1=((T, D), F32), r1=((T, 128), F32), hr=((T, D), BF16), n2=((T, D), F32), r2=((T, 128), F32))
    outs = dict(loss=((8, 128), F32, V), token=((-(-len(seqs) // 8) * 8, D), F32, V))
    for name, (shape, kind) in states.items():
        outs[name + "_out"] = ((L, *shape), kind, ANY)
    outs.update(a_out=((L, ways, T, R), BF16, ANY), slope_out=((L, ways, T, R), BF16, ANY), w=((G, ways, 4, R // 4, D), BF16, ANY))
    VM, DMA = pltpu.VMEM, pltpu.SemaphoreType.DMA
    waves = G * (ways - 1)
    scratch = {name: VM(shape, kind) for name, (shape, kind) in states.items()}
    nbits = 0
    while 1 << nbits < lax.axis_size("dp"):
        nbits += 1
    block = -(-(len(seqs) * (D // 128) + 1) // 8) * 8
    scratch.update(
        x=VM((T, D), F32), emb=VM((2,) * nbits + (ways, block, 128), F32), own_rows=VM((block, 128), F32),
        e_send=DMA((nbits + ways,)), e_recv=DMA((nbits + ways,)))
    scratch.update(
        mask=VM((T, 128), F32), par=VM((L, 16, D), F32), up_b=VM((L, ways, 1, R), F32), pack=VM((L, R, D), BF16), tiny=VM((ways, 16, D), BF16),
        a=VM((2, T, R), BF16), slope=VM((2, T, R), BF16),
        w_attn=VM((4, ways, R // 4, D), BF16), w_up=VM((ways, 4, R // 4, D), BF16), w_down=VM((ways, 4, R // 4, D), BF16),
        w_sem=DMA((G,)), s_sem=DMA((L * ways * 2,)), k_sem=DMA((L * 11,)), z_send=DMA((waves,)), z_recv=DMA((waves,)),
        p_send=DMA((waves * 8,)), p_recv=DMA((waves * 8,)), own_send=DMA((G,)), own_recv=DMA((G,)),
        t_send=DMA((ways - 1,)), t_recv=DMA((ways - 1,)))
    names = tuple(ins) + tuple(outs) + tuple(scratch)
    res = pl.pallas_call(
        functools.partial(forward_kernel, seqs, L, ways, names),
        out_shape=[jax.ShapeDtypeStruct(s, d) for s, d, _ in outs.values()],
        in_specs=[s for _, s in ins.values()],
        out_specs=[s for _, _, s in outs.values()],
        scratch_shapes=list(scratch.values()),
        compiler_params=pltpu.CompilerParams(collective_id=collective_id, has_side_effects=True, vmem_limit_bytes=62 << 20),
        name="forward_layers",
    )(*[v for v, _ in ins.values()])
    return {name.removesuffix("_out") if name[:-4] in states else name: value for name, value in zip(outs, res)}


def add_low(a, b):
    return a + b


class Reduce:
    def __init__(self, r, ways, layers):
        self.r, self.ways, self.layers = r, ways, layers
        self.core, self.px, self.py, self.peers = place()
        for k in range(1, ways):
            self.peers[f"z{k}"] = {"mp": lax.rem(lax.axis_index("mp") + k, ways)}
        self.extra = far_peers()
        self.peers.update(self.extra)
        core, px, py = self.core, self.px, self.py
        self.me = spot(core, px, py)
        sx, sy, sd = spot(core, 1 - px, py), spot(core, px, 1 - py), spot(core, 1 - px, 1 - py)
        self.plane = [
            ("x", self.me, sx, None), ("y", self.me, sy, None), ("y", sx, sd, 0), ("x", sy, sd, 1),
            ("core", self.me, spot(1 - core, px, py), None), ("core", sx, spot(1 - core, 1 - px, py), None),
            ("core", sy, spot(1 - core, px, 1 - py), None), ("core", sd, spot(1 - core, 1 - px, 1 - py), None),
        ]
        self.per = 8 + ways - 1 + len(self.extra)
    def remote(self, src, dst, sems, index, peer):
        return pltpu.make_async_remote_copy(
            src_ref=src, dst_ref=dst, send_sem=sems[0].at[index], recv_sem=sems[1].at[index],
            device_id=self.peers[peer], device_id_type=pl.DeviceIdType.MESH)
    def step(self, src, dst, t, j, i, peer):
        return self.remote(src, dst, (self.r.r_send, self.r.r_recv), (3 * t + j) * self.per + i, peer)
    def share(self, t, j, c, i):
        ref = (self.r.g_down, self.r.g_up, self.r.g_attn)[j].at[self.layers - 1 - t]
        return ref.at[2 * c + i] if j == 2 else ref.at[i, pl.ds(2 * c, 2)]
    def place_of(self, ref, j, i):
        return ref.at[:, i] if j == 2 else ref.at[i]
    def pieces(self, j):
        return range(2 if j == 2 else self.ways)
    def load(self, t, j, i):
        return pltpu.make_async_copy(self.share(t, j, self.core, i), self.place_of(self.r.own.at[j], j, i), self.r.l_sem.at[(3 * t + j) * 4 + i])
    def core_copy(self, t, j, i):
        return self.step(self.share(t, j, 1 - self.core, i), self.place_of(self.r.got.at[3 * t + j], j, i), t, j, i, "core")
    def fetch(self, t, j):
        return pltpu.make_async_copy(self.r.got.at[3 * t + j], self.r.got_v, self.r.f_sem.at[3 * t + j])
    def a1(self, t, j):
        return self.step(self.r.own.at[j, :, :, 1 - self.px, 0], self.r.got_a.at[3 * t + j], t, j, 4, "x")
    def b1(self, t, j):
        return self.step(self.r.own.at[j, :, 1 - self.py, :, 1], self.r.got_b.at[3 * t + j], t, j, 5, "y")
    def a2(self, t, j):
        return self.step(self.r.got_a.at[3 * t + j, :, 1 - self.py], self.r.got_c.at[3 * t + j], t, j, 6, "y")
    def b2(self, t, j):
        return self.step(self.r.got_b.at[3 * t + j, :, 1 - self.px], self.r.got_d.at[3 * t + j], t, j, 7, "x")
    def zc(self, t, j, s):
        return self.step(self.r.zout.at[3 * t + j, s - 1], self.r.zin.at[3 * t + j, s - 1], t, j, 7 + s, "z1")
    def slot(self, i):
        return self.ways - 1 if i == 0 else i - 1
    def fc(self, t, j, i, name):
        return self.step(self.r.zout.at[3 * t + j, self.slot(i)], self.r.far.at[3 * t + j, i], t, j, 7 + self.ways + i, name)
    def pc(self, t, j, i, received=False):
        peer, sent, got, h = self.plane[i]
        dst = self.r.reduced.at[3 * t + j, got if received else sent]
        src = self.r.zout.at[3 * t + j, self.slot(len(self.extra))] if i in (0, 1, 4) and not received else dst
        if h is not None:
            src, dst = src.at[h], dst.at[h]
        return self.remote(src, dst, (self.r.g_send, self.r.g_recv), (3 * t + j) * 8 + i, peer)
    def mine(self, t, j):
        return pltpu.make_async_copy(self.r.zout.at[3 * t + j, self.slot(len(self.extra))], self.r.reduced.at[3 * t + j, self.me], self.r.m_sem.at[3 * t + j])
    def s0(self, t, j, i):
        self.core_copy(t, j, i).start()
        self.load(t, j, i).start()
    def s1(self, t, j):
        r = self.r
        for i in self.pieces(j):
            self.core_copy(t, j, i).wait_recv()
        self.fetch(t, j).start()
        for i in self.pieces(j):
            self.load(t, j, i).wait()
        self.fetch(t, j).wait()
        def body(k, _):
            for y in range(2):
                r.own[j, k, y] = add_low(r.own[j, k, y], r.got_v[k, y])
            return 0
        lax.fori_loop(0, self.ways, body, 0)
        self.a1(t, j).start()
        self.b1(t, j).start()
    def s2(self, t, j):
        r, g, px, py = self.r, 3 * t + j, self.px, self.py
        self.a1(t, j).wait_recv()
        def body(k, _):
            for y in range(2):
                r.got_a[g, k, y] = add_low(r.own[j, k, y, px, 0], r.got_a[g, k, y])
            return 0
        lax.fori_loop(0, self.ways, body, 0)
        self.a2(t, j).start()
        self.b1(t, j).wait_recv()
        def body(k, _):
            for x in range(2):
                r.got_b[g, k, x] = add_low(r.own[j, k, py, x, 1], r.got_b[g, k, x])
            return 0
        lax.fori_loop(0, self.ways, body, 0)
        self.b2(t, j).start()
        self.a1(t, j).wait_send()
        self.b1(t, j).wait_send()
    def part(self, g, k):
        r = self.r
        left = add_low(r.got_a[g, k, self.py], r.got_c[g, k])
        right = add_low(r.got_b[g, k, self.px], r.got_d[g, k])
        return left, right
    def s3(self, t, j):
        g = 3 * t + j
        self.a2(t, j).wait_recv()
        self.b2(t, j).wait_recv()
        for h, value in enumerate(self.part(g, 1)):
            self.r.zout[g, 0, h] = value
        self.zc(t, j, 1).start()
    def sz(self, t, j, s):
        r, g = self.r, 3 * t + j
        self.zc(t, j, s).wait_recv()
        for h, value in enumerate(self.part(g, (s + 1) % self.ways)):
            r.zout[g, s, h] = add_low(r.zin[g, s - 1, h], value)
        if s < self.ways - 1:
            self.zc(t, j, s + 1).start()
    def sz1(self, t, j):
        self.sz(t, j, 1)
    def sz2(self, t, j):
        for s in range(2, self.ways - 1):
            self.sz(t, j, s)
    def sp(self, t, j):
        r, g = self.r, 3 * t + j
        self.sz(t, j, self.ways - 1)
        for s in range(1, self.ways):
            self.zc(t, j, s).wait_send()
        for i, name in enumerate(self.extra):
            self.fc(t, j, i, name).start()
            self.fc(t, j, i, name).wait_recv()
            r.zout[g, self.slot(i + 1)] = add_low(r.zout[g, self.slot(i)], r.far[g, i])
        self.mine(t, j).start()
        for i in (0, 1, 4):
            self.pc(t, j, i).start()
    def sq(self, t, j):
        self.pc(t, j, 0, True).wait_recv()
        self.pc(t, j, 2).start()
        self.pc(t, j, 5).start()
        self.pc(t, j, 1, True).wait_recv()
        self.pc(t, j, 3).start()
        self.pc(t, j, 6).start()
    def sr(self, t, j):
        self.pc(t, j, 2, True).wait_recv()
        self.pc(t, j, 3, True).wait_recv()
        self.pc(t, j, 7).start()
    def end(self, t, j):
        for i in range(4, 8):
            self.pc(t, j, i, True).wait_recv()
        self.mine(t, j).wait()
        for i in self.pieces(j):
            self.core_copy(t, j, i).wait_send()
        self.a2(t, j).wait_send()
        self.b2(t, j).wait_send()
        for i, name in enumerate(self.extra):
            self.fc(t, j, i, name).wait_send()
        for i in range(8):
            self.pc(t, j, i).wait_send()


def norm_back(g, n, r, gain):
    gn = g * gain
    return r * (gn - jnp.mean(gn, axis=-1, keepdims=True) - n * jnp.mean(gn * n, axis=-1, keepdims=True))


def total(v):
    return jnp.sum(v, axis=0, keepdims=True)


class Backward:
    def __init__(self, l, seqs, r):
        self.l, self.seqs, self.r = l, seqs, r
        T = r.dy.shape[0]
        self.blocks = [slice(i, i + ROWS) for i in range(0, T, ROWS)]
    def add_row(self, row, value, first):
        r, l = self.r, self.l
        if first:
            r.sums[l, row:row + 1] = value
        else:
            r.sums[l, row:row + 1] += value
    def norm(self, b, which):
        r, l = self.r, self.l
        g = r.dy[b] if which else r.dz[b]
        n, inv = r.n[b], r.inv[b]
        inv = jnp.concatenate([inv] * (n.shape[1] // 128), axis=1)
        dz = norm_back(g, n, inv, r.gain[l, which:which + 1])
        low = dz.astype(BF16)
        r.dz[b] = dz
        r.low[b] = low
        first = b.start == 0
        self.add_row(GAIN + which, total(g * n), first)
        self.add_row(BIAS + which, total(g), first)
        self.add_row(DB if which else OB, total(low.astype(F32)), first)
    def put(self, slot, value):
        stage = self.r.stage
        stage[slot] = value.astype(BF16).reshape(stage.shape[1:])
    def ffn_down(self, slot):
        self.put(0, nn(self.r.low_t[...], self.r.a[slot]))
    def ffn_mid(self, c, b, slot, w):
        r, l = self.r, self.l
        da = nt(r.low[b], r.w[w])
        du = (da * r.slope[slot, b].astype(F32)).astype(BF16)
        r.du[b] = du
        if b.start == 0:
            r.su[l, c] = total(du.astype(F32))
        else:
            r.su[l, c] += total(du.astype(F32))
    def ffn_up(self):
        self.put(1, nn(self.r.hr_t[...], self.r.du[...]))
    def ffn_back(self, b, w):
        r = self.r
        r.dz[b] += nt(r.du[b], r.w[w])
    def context(self, b, w):
        r = self.r
        r.dctx[b] = nt(r.low[b], r.w[w]).astype(BF16)
    def out_grad(self, slot):
        r = self.r
        self.put(slot, nn(r.hc[...].T, r.low[...]))
    def attend(self, s, i):
        r = self.r
        start, n = self.seqs[s]
        rows = slice(start, start + n)
        lanes = pl.ds(pl.multiple_of(i * 128, 128), 128)
        kp, qp, vp, gp = r.k[rows, lanes], r.q[rows, lanes], r.v[rows, lanes], r.dctx[rows, lanes]
        kt = kp.T
        first = lax.broadcasted_iota(jnp.int32, (n, 128), 1) < HEAD_DIM
        bias = jnp.concatenate([r.mask[rows]] * (n // 128), axis=1)
        dv, dk, dq = [], [], []
        for h in range(2):
            keep = first if h == 0 else ~first
            kh = jnp.where(keep, kp, jnp.zeros_like(kp))
            vh = jnp.where(keep, vp, jnp.zeros_like(vp))
            p = jnp.exp(nt(kh, qp) + bias - r.lse[i, h:h + 1, rows])
            dp = nt(vh, gp)
            ds = (p * (dp - jnp.sum(p * dp, axis=0, keepdims=True))).astype(BF16)
            dv.append(nn(p.astype(BF16), gp))
            dk.append(nn(ds, qp))
            dq.append(nn(kt[h * HEAD_DIM:(h + 1) * HEAD_DIM], ds) * 0.125)
        r.dk[rows, lanes] = jnp.where(first, dk[0], dk[1]).astype(BF16)
        r.dv[rows, lanes] = jnp.where(first, dv[0], dv[1]).astype(BF16)
        r.dq[rows, lanes] = jnp.concatenate(dq, axis=0).T.astype(BF16)
    def qkv_grad(self, m, slot):
        r = self.r
        g = (r.dq, r.dk, r.dv)[m][...]
        self.put(slot, nn(g.T, r.du[...]))
        if m != 1:
            self.add_row(QB if m == 0 else VB, total(g.astype(F32)), True)
    def back_in(self, b, m, w):
        r = self.r
        d = nn((r.dq, r.dk, r.dv)[m][b], r.w[w])
        if m == 0:
            r.dy[b] = r.dz[b] + d
        else:
            r.dy[b] += d


def backward_kernel(seqs, layers, ways, names, *refs):
    r = Refs(**dict(zip(names, refs)))
    if r.low_t.shape == r.dy.shape:
        r.dctx, r.dq = r.low_t, r.hr_t
    red = Reduce(r, ways, layers)
    far = list(red.extra)
    greet(["core", "x", "y"] + [f"z{k}" for k in range(1, ways)] + far, red.peers)
    for s, (start, n) in enumerate(seqs):
        row = lax.broadcasted_iota(jnp.int32, (n, 128), 0)
        r.mask[start:start + n] = jnp.where(row < length(r, ways, s), 0.0, NEG_FILL)
    r.gain[...] = r.gain_in[...].astype(F32)
    each = 2 * ways + 4
    heads_order = (3, 0, 1, 2)
    def wload(t, local, group, block):
        return pltpu.make_async_copy(r.w_in.at[group, block], r.w.at[lax.rem(local, 4)], r.w_sem.at[t * each + local])
    def ffn_w(t, c, half):
        return wload(t, 2 * c + half, 3 * (layers - 1 - t) + 2 - half, c)
    def attn_w(t, i):
        return wload(t, 2 * ways + i, 3 * (layers - 1 - t), heads_order[i])
    items = ("n2", "r2", "hr", "n1", "r1", "ctx", "q", "k", "v", "lse", "xr")
    dst = dict(n2=r.n, n1=r.n, r2=r.inv, r1=r.inv, hr=r.hc, ctx=r.hc, q=r.q, k=r.k, v=r.v, lse=r.lse, xr=r.du)
    src = {name: getattr(r, name + "_in") for name in items}
    def load(l, name):
        return pltpu.make_async_copy(src[name].at[l], dst[name], r.i_sem.at[l * len(items) + items.index(name)])
    def aload(l, c, j):
        return pltpu.make_async_copy((r.a_in, r.slope_in)[j].at[l, c], (r.a, r.slope)[j].at[lax.rem(c, 2)], r.a_sem.at[(l * ways + c) * 2 + j])
    def ffn_save(l, c, j):
        return pltpu.make_async_copy(r.stage.at[j], (r.g_down, r.g_up)[j].at[l, c], r.o_sem.at[l * each + 2 * c + j])
    def attn_save(l, m, slot):
        return pltpu.make_async_copy(r.stage.at[slot], r.g_attn.at[l, m], r.o_sem.at[l * each + 2 * ways + m])
    top = layers - 1
    for c in range(2):
        for half in range(2):
            ffn_w(0, c, half).start()
    for name in ("n2", "r2", "hr"):
        load(top, name).start()
    for c in range(2):
        for j in range(2):
            aload(top, c, j).start()
    for name in ("q", "k", "v", "lse"):
        load(top, name).start()
    for s, (start, n) in enumerate(seqs):
        row = lax.broadcasted_iota(jnp.int32, (n, r.dy.shape[1]), 0)
        r.dy[start:start + n] = jnp.where(row < length(r, ways, s), r.token[s:s + 1], 0.0)
    pairs = r.q.shape[1] // 128

    def layer(t, _):
        l = layers - 1 - t
        f = Backward(l, seqs, r)
        after, more = t > 0, t + 1 < layers
        def old(kind, j):
            def go():
                @pl.when(after)
                def _():
                    kind(t - 1, j)
            return go
        def new(kind, j):
            return lambda: kind(t, j)
        def run(ops, n=1):
            for _ in range(min(n, len(ops))):
                ops.pop(0)()
        def again(*nm):
            @pl.when(more)
            def _():
                for x in nm:
                    load(l - 1, x).start()
        ops = [old(*x) for x in (
            (red.s2, 1), (red.sz1, 0), (red.s1, 2), (red.sz2, 0), (red.s3, 1), (red.sp, 0), (red.sz1, 1), (red.sq, 0), (red.s2, 2),
            (red.sz2, 1), (red.sr, 0), (red.s3, 2), (red.sp, 1), (red.sq, 1), (red.sr, 1))]
        load(l, "n2").wait()
        load(l, "r2").wait()
        for b in f.blocks:
            f.norm(b, 1)
            run(ops)
        load(l, "n1").start()
        load(l, "r1").start()
        r.low_t[...] = r.low[...].T
        load(l, "hr").wait()
        r.hr_t[...] = r.hc[...].T
        load(l, "ctx").start()
        def chunk(c, _):
            slot = lax.rem(c, 2)
            w = 2 * slot
            aload(l, c, 0).wait()
            @pl.when(c > 0)
            def _():
                ffn_save(l, c - 1, 0).wait()
                red.s0(t, 0, c - 1)
            f.ffn_down(slot)
            ffn_save(l, c, 0).start()
            aload(l, c, 1).wait()
            ffn_w(t, c, 0).wait()
            for b in f.blocks:
                f.ffn_mid(c, b, slot, w)
            for half in range(2):
                if half == 1:
                    @pl.when(c > 0)
                    def _():
                        ffn_save(l, c - 1, 1).wait()
                        red.s0(t, 1, c - 1)
                    f.ffn_up()
                    ffn_save(l, c, 1).start()
                    ffn_w(t, c, 1).wait()
                    for b in f.blocks:
                        f.ffn_back(b, w + 1)
                @pl.when(c + 2 < ways)
                def _():
                    ffn_w(t, c + 2, half).start()
                for late in range(2):
                    @pl.when(c == ways - 2 + late)
                    def _():
                        attn_w(t, 2 * late + half).start()
                if half == 0:
                    over = (c + 2) // ways
                    @pl.when(l - over >= 0)
                    def _():
                        for j in range(2):
                            aload(l - over, c + 2 - over * ways, j).start()
            for at in range(ways):
                @pl.when(c == at)
                def _():
                    run(ops, 3)
            return 0
        lax.fori_loop(0, ways, chunk, 0)
        load(l, "xr").start()
        ops = [new(red.s1, 0), new(red.s1, 1), old(red.sz1, 2), old(red.sz2, 2), old(red.sp, 2), new(red.s2, 0), old(red.sq, 2), new(red.s3, 0), old(red.sr, 2)]
        for j in range(2):
            ffn_save(l, ways - 1, j).wait()
            red.s0(t, j, ways - 1)
        load(l, "n1").wait()
        load(l, "r1").wait()
        for b in f.blocks:
            f.norm(b, 0)
        again("n2", "r2")
        run(ops)
        attn_w(t, 0).wait()
        for b in f.blocks:
            f.context(b, 0)
        @pl.when(more)
        def _():
            ffn_w(t + 1, 0, 0).start()
        run(ops)
        load(l, "ctx").wait()
        f.out_grad(0)
        attn_save(l, 3, 0).start()
        again("hr")
        for nm in ("q", "k", "v", "lse"):
            load(l, nm).wait()
        def pair(i, _):
            for s in range(len(seqs)):
                f.attend(s, i)
            for at in (0, 2, 4):
                @pl.when(i == at)
                def _():
                    run(ops)
            return 0
        lax.fori_loop(0, pairs, pair, 0)
        again("q", "k", "v", "lse")
        load(l, "xr").wait()
        for m in range(3):
            slot = (m + 1) % 2
            if m == 1:
                attn_save(l, 3, 0).wait()
            if m == 2:
                attn_save(l, 0, 1).wait()
            f.qkv_grad(m, slot)
            attn_save(l, m, slot).start()
            run(ops)
        run(ops, len(ops))
        attn_save(l, 1, 0).wait()
        attn_save(l, 2, 1).wait()
        for i in red.pieces(2):
            red.s0(t, 2, i)
        for m in range(3):
            attn_w(t, m + 1).wait()
            for b in f.blocks:
                f.back_in(b, m, m + 1)
            @pl.when(more)
            def _():
                ffn_w(t + 1, (m + 1) // 2, (m + 1) % 2).start()
        return 0
    lax.fori_loop(0, layers, layer, 0)

    names_dp = ["core", "x", "y"] + far
    for l in range(layers):
        r.small[0, l] = r.sums[l]
        for c in range(ways):
            r.small[0, l, UB + c:UB + c + 1] = r.su[l, c]
    def sd(i):
        return red.remote(r.small.at[i], r.small_in.at[i], (r.v_send, r.v_recv), i, names_dp[i])
    def sm(k):
        n = len(names_dp)
        return red.remote(r.small.at[n], r.small_in.at[n + k - 1], (r.v_send, r.v_recv), n + k - 1, f"z{k}")
    def small_step(i):
        def go():
            if i > 0:
                sd(i - 1).wait_recv()
                r.small[i] = r.small[i - 1] + r.small_in[i - 1]
            if i < len(names_dp):
                sd(i).start()
            else:
                for k in range(1, ways):
                    sm(k).start()
        return go
    def small_end():
        n = len(names_dp)
        for k in range(1, ways):
            sm(k).wait_recv()
        v = [r.small.at[n]] + [r.small_in.at[n + k - 1] for k in range(1, ways)]
        for l in range(layers):
            part = v[0].shape[-1] // ways
            even, odd = v[0][l], v[1][l]
            for k in range(2, ways):
                if k % 2:
                    odd = odd + v[k][l]
                else:
                    even = even + v[k][l]
            r.small_out[l] = even + odd
            split, up = None, None
            for k in range(ways):
                back = (ways - k) % ways
                row = v[k][l, QB:VB + 1]
                if back:
                    row = pltpu.roll(row, (ways - back) * part, 1)
                split = row if split is None else split + row
                one = v[k][l, UB + back:UB + back + 1]
                up = one if up is None else up + one
            r.small_out[l, QB:VB + 1] = split
            r.small_out[l, UB:UB + 1] = up
    t = layers - 1
    a, b, c = 0, 1, 2
    tail = [(red.s2, b), (red.sz1, a), (red.s1, c), (red.sz2, a), (red.s3, b), (red.sp, a), (red.sz1, b), (red.s2, c), (red.sq, a), (red.sz2, b),
            (red.s3, c), (red.sr, a), (red.sp, b), (red.sz1, c), (red.sq, b), (red.sz2, c), (red.sr, b), (red.sp, c), (red.sq, c), (red.sr, c)]
    smalls = [small_step(i) for i in range(len(names_dp) + 1)]
    for i, (kind, j) in enumerate(tail):
        kind(t, j)
        if smalls and i % 2 == 0:
            smalls.pop(0)()
    for go in smalls:
        go()
    small_end()
    def finish(t, _):
        for j in range(3):
            red.end(t, j)
        return 0
    lax.fori_loop(0, layers, finish, 0)
    for i in range(len(names_dp)):
        sd(i).wait_send()
    for k in range(1, ways):
        sm(k).wait_send()


def backward(saved, w, q_lens, p_lens, gain, seqs, collective_id):
    T, D = saved["q"].shape[1:]
    G, ways, R, _ = w.shape
    L = G // 3
    V = pl.BlockSpec(memory_space=pltpu.VMEM)
    S = pl.BlockSpec(memory_space=pltpu.SMEM)
    ins = dict(q_lens=(q_lens, S), p_lens=(p_lens, S), token=(saved["token"], V), w_in=(w, ANY), gain_in=(gain, V))
    for n in ("n2", "r2", "hr", "n1", "r1", "ctx", "q", "k", "v", "lse", "xr"):
        ins[n + "_in"] = (saved[n], ANY)
    ins["a_in"] = (saved["a_out"], ANY)
    ins["slope_in"] = (saved["slope_out"], ANY)
    half = R // 16
    block = (2, 2, half, D)
    outs = dict(
        dy=((T, D), F32, V), small_out=((L, 16, D), F32, V), reduced=((G, 8, 2, half, D), BF16, ANY),
        g_down=((L, ways, 4, *block), BF16, ANY), g_up=((L, ways, 4, *block), BF16, ANY), g_attn=((L, 4, ways, *block), BF16, ANY),
        got=((G, ways, 2, *block), BF16, ANY))
    H = saved["lse"].shape[1]
    nfar = 0
    while 8 << nfar < lax.axis_size("dp"):
        nfar += 1
    VM, DMA = pltpu.VMEM, pltpu.SemaphoreType.DMA
    per = 8 + ways - 1 + nfar
    steps = 3 + nfar
    each = 2 * ways + 4
    scratch = dict(
        gain=VM(gain.shape, F32), mask=VM((T, 128), F32), n=VM((T, D), F32), inv=VM((T, 128), F32), hc=VM((T, D), BF16), hr_t=VM((D, T), BF16),
        low=VM((T, D), BF16), low_t=VM((D, T), BF16), dz=VM((T, D), F32), du=VM((T, R), BF16),
        a=VM((2, T, R), BF16), slope=VM((2, T, R), BF16), q=VM((T, D), BF16), k=VM((T, D), BF16), v=VM((T, D), BF16),
        lse=VM((H, 8, T), F32), dk=VM((T, D), BF16), dv=VM((T, D), BF16),
        stage=VM((2, 4, *block), BF16), w=VM((4, R, D), BF16), sums=VM((L, 16, D), F32), su=VM((L, ways, 1, R), F32),
        own=VM((3, ways, 2, *block), BF16), got_v=VM((ways, 2, *block), BF16),
        got_a=VM((G, ways, 2, half, D), BF16), got_b=VM((G, ways, 2, half, D), BF16),
        got_c=VM((G, ways, half, D), BF16), got_d=VM((G, ways, half, D), BF16),
        zin=VM((G, ways - 1, 2, half, D), BF16), zout=VM((G, ways, 2, half, D), BF16),
        small=VM((steps + 1, L, 16, D), F32), small_in=VM((steps + ways - 1, L, 16, D), F32),
        w_sem=DMA((L * each,)), i_sem=DMA((L * 11,)), a_sem=DMA((L * ways * 2,)), o_sem=DMA((L * each,)),
        l_sem=DMA((G * 4,)), f_sem=DMA((G,)), m_sem=DMA((G,)), r_send=DMA((G * per,)), r_recv=DMA((G * per,)),
        g_send=DMA((G * 8,)), g_recv=DMA((G * 8,)), v_send=DMA((steps + ways - 1,)), v_recv=DMA((steps + ways - 1,)))
    if T != D:
        scratch["dctx"] = VM((T, D), BF16)
        scratch["dq"] = VM((T, D), BF16)
    if nfar:
        scratch["far"] = VM((G, nfar, 2, half, D), BF16)
    names = tuple(ins) + tuple(outs) + tuple(scratch)
    res = pl.pallas_call(
        functools.partial(backward_kernel, seqs, L, ways, names),
        out_shape=[jax.ShapeDtypeStruct(s, d) for s, d, _ in outs.values()],
        in_specs=[s for _, s in ins.values()],
        out_specs=[s for _, _, s in outs.values()],
        scratch_shapes=list(scratch.values()),
        compiler_params=pltpu.CompilerParams(collective_id=collective_id, has_side_effects=True, vmem_limit_bytes=255 << 18),
        name="backward_layers",
    )(*[v for v, _ in ins.values()])
    return dict(zip(outs, res))


def finish_kernel(reduced, dy, small, qkv, out, up, down, q_grad, p_grad, qv_bias, out_bias, gain, bias, up_bias, down_bias):
    part = out.shape[1]
    attn = reduced[2].astype(F32)
    qkv[0] = attn[:3 * part]
    out[0] = attn[3 * part:]
    up[0] = reduced[1].astype(F32)
    down[0] = reduced[0].astype(F32).T

    @pl.when(pl.program_id(0) == 0)
    def _():
        rows = q_grad.shape[0]
        q_grad[...] = dy[:rows]
        p_grad[...] = dy[rows:]
        for l in range(small.shape[0]):
            qv_bias[l] = small[l, QB:VB + 1, :part]
            out_bias[l:l + 1] = small[l, OB:OB + 1]
            gain[l] = small[l, GAIN:GAIN + 2]
            bias[l] = small[l, BIAS:BIAS + 2]
            up_bias[l:l + 1] = small[l, UB:UB + 1, :up_bias.shape[1]]
            down_bias[l:l + 1] = small[l, DB:DB + 1]


def finish(reduced, dy, small, layers, part, rows):
    G, R, D = reduced.shape
    T = dy.shape[0]
    per_layer = [(3 * part, D), (part, D), (D, R), (R, D)]
    once = [(rows, D), (T - rows, D), (layers, 2, part), (layers, D), (layers, 2, D), (layers, 2, D), (layers, R), (layers, D)]
    whole = lambda shape: pl.BlockSpec(shape, lambda l: (0,) * len(shape))
    return pl.pallas_call(
        finish_kernel,
        grid=(layers,),
        out_shape=[jax.ShapeDtypeStruct((layers, *s), F32) for s in per_layer] + [jax.ShapeDtypeStruct(s, F32) for s in once],
        in_specs=[pl.BlockSpec((3, R, D), lambda l: (layers - 1 - l, 0, 0)), whole(dy.shape), whole(small.shape)],
        out_specs=[pl.BlockSpec((1, *s), lambda l: (l, 0, 0)) for s in per_layer] + [whole(s) for s in once],
        compiler_params=pltpu.CompilerParams(vmem_limit_bytes=60 << 20),
        name="finish",
    )(reduced, dy, small)


def local(
    query_states,
    passage_states,
    query_lengths,
    passage_lengths,
    query_count,
    passage_count,
    positive,
    query_key_value_matrix,
    qv_bias,
    out_weight,
    out_bias,
    norm_gain,
    norm_bias,
    up_matrix,
    up_bias,
    down_matrix,
    down_bias,
):
    layers = query_key_value_matrix.shape[0]
    width = query_states.shape[-1]
    ways = lax.axis_size("mp")
    q_slots, q_len, _ = query_states.shape
    p_slots, p_len, _ = passage_states.shape
    shapes = ((q_slots, q_len), (p_slots, p_len))
    part = qv_bias.shape[-1]

    hidden = up_bias.shape[-1]
    tiny = jnp.concatenate(
        [
            jnp.pad(qv_bias.reshape(2 * layers, part), ((0, 0), (0, width - part))),
            up_bias,
            jnp.zeros((16 - 3 * layers, width), BF16),
        ]
    )
    seqs, at = [], 0
    for count, length in shapes:
        for _ in range(count):
            seqs.append((at, length))
            at += length
    seqs = tuple(seqs)
    saved = forward(
        query_states, passage_states, jnp.swapaxes(query_key_value_matrix, 2, 3), out_weight, up_matrix, down_matrix,
        query_lengths, passage_lengths, (positive, query_count, passage_count), tiny, (out_bias, norm_gain, norm_bias, down_bias), seqs, ways, 0,
    )
    loss = saved["loss"][0, 0]
    back = backward(
        saved, saved["w"].reshape(3 * layers, 4, -1, width), query_lengths, passage_lengths, norm_gain, seqs, 1
    )
    reduced = back["reduced"].reshape(3 * layers, -1, width)
    qkv_grad, out_grad, up_grad, down_grad, query_grad, passage_grad, qv_b, out_b, gain_g, bias_g, up_b, down_b = finish(
        reduced, back["dy"], back["small_out"], layers, part, q_slots * q_len
    )
    qkv_grad = jnp.swapaxes(qkv_grad.reshape(layers, 3, part, width), 2, 3)
    query_grad = query_grad.reshape(query_states.shape)
    passage_grad = passage_grad.reshape(passage_states.shape)
    return (
        loss, query_grad, passage_grad, qkv_grad, qv_b, out_grad, out_b, gain_g, bias_g, up_grad, up_b, down_grad, down_b
    )


def solution(mesh):
    placed = (
        P(("dp", "mp"), None, None),
        P(("dp", "mp"), None, None),
        P("dp"),
        P("dp"),
        P(),
        P(),
        P(("dp", "mp")),
        P(None, None, None, "mp"),
        P(None, None, "mp"),
        P(None, "mp", None),
        P(),
        P(),
        P(),
        P(None, None, "mp"),
        P(None, "mp"),
        P(None, "mp", None),
        P(),
    )
    return jax.shard_map(
        local,
        mesh=mesh,
        in_specs=placed,
        out_specs=(
            P(),
            P(("dp", "mp"), None, None),
            P(("dp", "mp"), None, None),
            P(None, None, None, "mp"),
            P(None, None, "mp"),
            P(None, "mp", None),
            P(),
            P(),
            P(),
            P(None, None, "mp"),
            P(None, "mp"),
            P(None, "mp", None),
            P(),
        ),
        check_vma=False,
    )
```

```python
import functools
import math

import jax
import jax.numpy as jnp
from jax import lax
from jax.experimental import pallas as pl
from jax.experimental.pallas import tpu as pltpu
from jax.sharding import PartitionSpec as P

HEAD_DIM = 64
EPS_NORM = 1e-12
INV_TEMP = 50.0
PRECISE_MODE = lax.Precision.HIGHEST
NEG_FILL = -1e30
RSQRT_TWO = 1.0 / math.sqrt(2.0)
RSQRT_TWOPI = 1.0 / math.sqrt(2.0 * math.pi)
F32 = jnp.float32
BF16 = jnp.bfloat16


ANY = pl.BlockSpec(memory_space=pl.ANY)

def place():
    d = lax.axis_index("dp")
    z = lax.axis_index("mp")
    nz = lax.axis_size("mp")
    core, px, py = d % 2, (d // 2) % 2, (d // 4) % 2
    peers = {
        "core": {"dp": d + 1 - 2 * core},
        "x": {"dp": d + 2 - 4 * px},
        "y": {"dp": d + 4 - 8 * py},
        "up": {"mp": lax.rem(z + 1, nz)},
        "down": {"mp": lax.rem(z + nz - 1, nz)},
    }
    return core, px, py, peers

def greet(names, peers):
    sem = pltpu.get_barrier_semaphore()
    for n in names:
        pl.semaphore_signal(sem, inc=1, device_id=peers[n], device_id_type=pl.DeviceIdType.MESH)
    pl.semaphore_wait(sem, len(names))

def spot(core, px, py):
    return core * 4 + py * 2 + px


def nn(a, b):
    return lax.dot_general(a, b, (((1,), (0,)), ((), ())), preferred_element_type=F32)
def nt(a, b):
    return lax.dot_general(a, b, (((1,), (1,)), ((), ())), preferred_element_type=F32)
def tn(a, b):
    return lax.dot_general(a, b, (((0,), (0,)), ((), ())), preferred_element_type=F32)

def gelu_both(u):
    w = jnp.abs(u) * RSQRT_TWO
    t = 1.0 / (1.0 + 0.3275911 * w)
    e = jnp.exp(-0.5 * u * u)
    poly = ((((1.061405429 * t - 1.453152027) * t + 1.421413741) * t - 0.284496736) * t + 0.254829592) * t
    tail = 0.5 * poly * e
    phi = jnp.where(u >= 0.0, 1.0 - tail, tail)
    return u * phi, phi + u * e * RSQRT_TWOPI

def norm_rows(z, gain, bias):
    c = z - jnp.mean(z, axis=-1, keepdims=True)
    r = lax.rsqrt(jnp.mean(c * c, axis=-1, keepdims=True) + EPS_NORM)
    n = c * r
    return n, r, n * gain + bias

ROWS = 256

class Refs:
    def __init__(self, **k):
        self.__dict__.update(k)

def far_peers():
    d = lax.axis_index("dp")
    found = {}
    bit = 8
    while bit < lax.axis_size("dp"):
        high = (d // bit) % 2
        found[f"far{bit}"] = {"dp": d + bit - 2 * bit * high}
        bit *= 2
    return found


class Weights:
    def __init__(self, r, ways, layers):
        self.r, self.ways, self.layers = r, ways, layers
        self.core, self.px, self.py, self.peers = place()
        core, px, py = self.core, self.px, self.py
        self.rows = r.w.shape[3] // 2
        self.part = r.w.shape[3]
        self.me = spot(core, px, py)
        sx, sy, sd = spot(core, 1 - px, py), spot(core, px, 1 - py), spot(core, 1 - px, 1 - py)
        half = self.rows // 2
        self.plane = [
            ("x", self.me, sx, 0, self.rows), ("y", self.me, sy, 0, self.rows),
            ("y", sx, sd, 0, half), ("x", sy, sd, half, half),
            ("core", self.me, spot(1 - core, px, py), 0, self.rows),
            ("core", sx, spot(1 - core, 1 - px, py), 0, self.rows),
            ("core", sy, spot(1 - core, px, 1 - py), 0, self.rows),
            ("core", sd, spot(1 - core, 1 - px, 1 - py), 0, self.rows),
        ]
    def region(self, l, j, k, slot, lo=0, n=None):
        n = self.rows if n is None else n
        rows = pl.ds(pl.multiple_of((slot % 2) * self.rows + lo, 16), n)
        if j == 0:
            return self.r.w.at[3 * l, slot // 2, k, rows]
        return self.r.w.at[3 * l + j, k, slot // 2, rows]
    def source(self, l, j):
        return (self.r.pack, self.r.up_w, self.r.down_w)[j].at[l]
    def remote(self, src, dst, send, recv, index, peer):
        return pltpu.make_async_remote_copy(
            src_ref=src, dst_ref=dst, send_sem=send.at[index], recv_sem=recv.at[index],
            device_id=self.peers[peer], device_id_type=pl.DeviceIdType.MESH)
    def z_copy(self, l, j, k):
        if k == 1:
            src = self.source(l, j).at[pl.ds(pl.multiple_of(self.me * self.rows, 16), self.rows)]
        else:
            src = self.region(l, j, k - 1, self.me)
        return self.remote(src, self.region(l, j, k, self.me), self.r.z_send, self.r.z_recv, (l * 3 + j) * (self.ways - 1) + k - 1, "z1")
    def p_copy(self, l, j, k, i, received=False):
        peer, sent, got, lo, n = self.plane[i]
        reg = self.region(l, j, k, got if received else sent, lo, n)
        index = ((l * 3 + j) * (self.ways - 1) + k - 1) * len(self.plane) + i
        return self.remote(reg, reg, self.r.p_send, self.r.p_recv, index, peer)
    def own_copy(self, l, j):
        src, dst = self.source(l, j), self.r.w.at[3 * l + j, 0]
        if j == 0:
            dst = self.r.w.at[3 * l, :, 0]
        return self.remote(src.reshape(4, self.part, src.shape[-1]), dst, self.r.own_send, self.r.own_recv, l * 3 + j, "core")
    def first(self, l, j, k):
        self.z_copy(l, j, k).wait_recv()
        if k + 1 < self.ways:
            self.z_copy(l, j, k + 1).start()
        else:
            @pl.when(l + 1 < self.layers)
            def _():
                self.z_copy(l + 1, j, 1).start()
        for i in (0, 1, 4):
            self.p_copy(l, j, k, i).start()
    def second(self, l, j, k):
        self.p_copy(l, j, k, 0, True).wait_recv()
        self.p_copy(l, j, k, 2).start()
        self.p_copy(l, j, k, 5).start()
        self.p_copy(l, j, k, 1, True).wait_recv()
        self.p_copy(l, j, k, 3).start()
        self.p_copy(l, j, k, 6).start()
    def third(self, l, j, k):
        self.p_copy(l, j, k, 2, True).wait_recv()
        self.p_copy(l, j, k, 3, True).wait_recv()
        self.p_copy(l, j, k, 7).start()
    def tick(self, l, step):
        last = self.ways - 1
        def group(n):
            return l + n // 3, n % 3
        now = [(*group(step + i), last - i) for i in range(last)]
        before = [(*group(step - 1 + i), last - i) for i in range(last)]
        def op(kind, item):
            def go():
                if item[0] is l:
                    kind(*item)
                else:
                    @pl.when(item[0] < self.layers)
                    def _():
                        kind(*item)
            return go
        line = before[1:] + now
        ops = []
        for i, item in enumerate(now):
            ops.append(op(self.first, item))
            ops.append(op(self.second, line[last - 2 + i]))
            ops.append(op(self.third, line[last - 3 + i]))
        return ops
    def arrived(self, l, j):
        for k in range(1, self.ways):
            for i in range(4, 8):
                self.p_copy(l, j, k, i, True).wait_recv()
        self.own_copy(l, j).wait_recv()
    def sent(self, l, j):
        for k in range(1, self.ways):
            self.z_copy(l, j, k).wait_send()
            for i in range(len(self.plane)):
                self.p_copy(l, j, k, i).wait_send()
        self.own_copy(l, j).wait_send()

QB, VB, UB, OB, GAIN, BIAS, DB = 0, 1, 2, 6, 7, 9, 11

class Forward:
    def __init__(self, l, seqs, r):
        self.l, self.seqs, self.r = l, seqs, r
        T = r.x.shape[0]
        self.blocks = [slice(i, i + ROWS) for i in range(0, T, ROWS)]
    def par(self, row):
        return self.r.par[self.l, row:row + 1]
    def project(self, m):
        r, l = self.r, self.l
        acc = nt(r.xr[...], r.w_attn[m].reshape(-1, r.x.shape[1]))
        if m == 0:
            r.q[...] = (acc + self.par(QB)).astype(BF16) * jnp.bfloat16(0.125)
        elif m == 1:
            r.k[...] = acc.astype(BF16)
        else:
            r.v[...] = (acc + self.par(VB)).astype(BF16)
    def attend(self, s, i):
        r, l = self.r, self.l
        start, n = self.seqs[s]
        rows = slice(start, start + n)
        lanes = pl.ds(pl.multiple_of(i * 128, 128), 128)
        kp, qp, vp = r.k[rows, lanes], r.q[rows, lanes], r.v[rows, lanes]
        vt = vp.T
        first = lax.broadcasted_iota(jnp.int32, (n, 128), 1) < HEAD_DIM
        bias = jnp.concatenate([r.mask[rows]] * (n // 128), axis=1)
        out = []
        for h in range(2):
            kh = jnp.where(first if h == 0 else ~first, kp, jnp.zeros_like(kp))
            sc = nt(kh, qp) + bias
            top = jnp.max(sc, axis=0, keepdims=True)
            e = jnp.exp(sc - top)
            tot = jnp.sum(e, axis=0, keepdims=True)
            r.lse[i, h:h + 1, rows] = top + jnp.log(tot)
            ct = nn(vt[h * HEAD_DIM:(h + 1) * HEAD_DIM], e.astype(BF16))
            out.append(ct * (1.0 / tot))
        ct = jnp.concatenate(out, axis=0)
        r.ctx[rows, lanes] = ct.T.astype(BF16)
    def out_norm(self, b):
        r, l = self.r, self.l
        z = r.x[b] + nn(r.ctx[b], r.w_attn[3].reshape(-1, r.x.shape[1])) + self.par(OB)
        n, inv, h = norm_rows(z, self.par(GAIN), self.par(BIAS))
        r.n1[b] = n
        r.r1[b] = jnp.broadcast_to(inv, (ROWS, 128))
        r.hr[b] = h.astype(BF16)
        r.x[b] = h + self.par(DB)
    def ffn(self, c, b, slot):
        r, l = self.r, self.l
        u = nn(r.hr[b], r.w_up[c].reshape(r.x.shape[1], -1)) + r.up_b[l, c]
        a, slope = gelu_both(u)
        a = a.astype(BF16)
        r.a[slot, b] = a
        r.slope[slot, b] = slope.astype(BF16)
        r.x[b] += nn(a, r.w_down[c].reshape(-1, r.x.shape[1]))
    def ffn_norm(self, b):
        r, l = self.r, self.l
        n, inv, y = norm_rows(r.x[b], self.par(GAIN + 1), self.par(BIAS + 1))
        r.n2[b] = n
        r.r2[b] = jnp.broadcast_to(inv, (ROWS, 128))
        r.x[b] = y
        r.xr[b] = y.astype(BF16)

def length(r, ways, s):
    me = lax.axis_index("mp")
    q_slots, p_slots = r.q_lens.shape[0] // ways, r.p_lens.shape[0] // ways
    return r.q_lens[me * q_slots + s] if s < q_slots else r.p_lens[me * p_slots + s - q_slots]


def contrast(r, z, seqs, ways, extra):
    d, me = lax.axis_index("dp"), lax.axis_index("mp")
    rank = d * ways + me
    q_slots, p_slots = r.q_in.shape[0], r.p_in.shape[0]
    width = r.x.shape[1]
    parts = width // 128
    shape = r.emb.shape
    count = 1
    for size in shape[:-2]:
        count *= size
    block = shape[-2]
    flat = r.emb.reshape(count * block, 128)
    invs, sizes = [], []
    lane = lax.broadcasted_iota(jnp.int32, (1, 128), 1)
    for s, (start, n) in enumerate(seqs):
        row = lax.broadcasted_iota(jnp.int32, (n, 128), 0)
        live = jnp.concatenate([row < length(r, ways, s)] * parts, axis=1)
        size = jnp.full((1, 1), length(r, ways, s), jnp.int32).astype(F32)
        pooled = jnp.sum(jnp.where(live, r.x[start:start + n], 0.0), axis=0, keepdims=True) / size
        inv = lax.rsqrt(jnp.sum(pooled * pooled, axis=1, keepdims=True) + 1e-06)
        normed = pooled * inv
        for c in range(parts):
            r.own_rows[s * parts + c:s * parts + c + 1] = normed[:, c * 128:(c + 1) * 128]
        invs.append(inv)
        sizes.append(size)
    at = len(seqs) * parts
    marks = jnp.zeros((1, 128), F32)
    values = [r.positive[j] for j in range(q_slots)] + [r.q_count[rank], r.p_count[rank]]
    for i, value in enumerate(values):
        marks = jnp.where(lane == i, jnp.full((1, 128), value, jnp.int32).astype(F32), marks)
    r.own_rows[at:] = jnp.zeros((block - at, 128), F32)
    r.own_rows[at:at + 1] = marks
    flat[pl.ds(pl.multiple_of(rank * block, 8), block)] = r.own_rows[...]
    bits = []
    bit = lax.axis_size("dp") // 2
    while bit:
        bits.append(bit)
        bit //= 2
    name_of = {1: "core", 2: "x", 4: "y"}
    mine = [(d // b) % 2 for b in bits]
    steps = []
    span = 1
    while span < ways:
        low = me - lax.rem(me, span)
        other = me + span - 2 * span * lax.rem(me // span, 2)
        steps.append((tuple(mine) + (pl.ds(low, span),), tuple(mine) + (pl.ds(other - lax.rem(other, span), span),), {"mp": other}))
        span *= 2
    held = list(mine)
    for i, b in enumerate(bits):
        there = list(held)
        there[i] = 1 - mine[i]
        steps.append((tuple(held), tuple(there), z.peers[name_of.get(b, f"far{b}")]))
        held[i] = slice(None)
    copies = []
    for i, (here, there, peer) in enumerate(steps):
        def move(where):
            return pltpu.make_async_remote_copy(
                src_ref=r.emb.at[where], dst_ref=r.emb.at[where], send_sem=r.e_send.at[i], recv_sem=r.e_recv.at[i],
                device_id=peer, device_id_type=pl.DeviceIdType.MESH)
        copies.append(move(here))
        copies[-1].start()
        move(there).wait_recv()
    def rows(i):
        return flat[pl.ds(i, count, stride=block), :]
    def precise(a, b, dims):
        return lax.dot_general(a, b, (dims, ((), ())), precision=PRECISE_MODE, preferred_element_type=F32)
    q = [[rows(j * parts + c) for c in range(parts)] for j in range(q_slots)]
    p = [[rows((q_slots + i) * parts + c) for c in range(parts)] for i in range(p_slots)]
    marks = rows(at)
    marks_t = marks.T
    down = lax.broadcasted_iota(jnp.int32, (count, count), 0)
    across = lax.broadcasted_iota(jnp.int32, (count, count), 1)
    live_total = jnp.sum(marks[:, q_slots:q_slots + 1], axis=0, keepdims=True)
    scale = float(count * q_slots * seqs[0][1])
    loss = jnp.zeros((1, 1), F32)
    dn = [[jnp.zeros((1, 128), F32) for _ in range(parts)] for _ in seqs]
    for j in range(q_slots):
        sims, masked, is_pos = [], [], []
        for i in range(p_slots):
            s = precise(q[j][0], p[i][0], ((1,), (1,)))
            for c in range(1, parts):
                s = s + precise(q[j][c], p[i][c], ((1,), (1,)))
            s = INV_TEMP * s
            sims.append(s)
            masked.append(jnp.where(marks_t[q_slots + 1:q_slots + 2] > i, s, NEG_FILL))
            is_pos.append(jnp.where((across * p_slots + i).astype(F32) == marks[:, j:j + 1], 1.0, 0.0))
        top = functools.reduce(jnp.maximum, [jnp.max(s, axis=1, keepdims=True) for s in masked])
        expo = [jnp.exp(s - top) for s in masked]
        tot = sum(jnp.sum(e, axis=1, keepdims=True) for e in expo)
        pos = sum(jnp.sum(m * s, axis=1, keepdims=True) for m, s in zip(is_pos, sims))
        live = jnp.where(marks[:, q_slots:q_slots + 1] > j, 1.0, 0.0)
        loss = loss + jnp.sum(live * (top + jnp.log(tot) - pos), axis=0, keepdims=True)
        for i in range(p_slots):
            ds = (scale * live / live_total) * (expo[i] / tot - is_pos[i])
            row = jnp.sum(jnp.where(down == rank, ds, 0.0), axis=0, keepdims=True)
            row = jnp.broadcast_to(row, (8, count))
            col = jnp.sum(jnp.where(across == rank, ds, 0.0), axis=1, keepdims=True)
            for c in range(parts):
                dn[j][c] = dn[j][c] + INV_TEMP * precise(row, p[i][c], ((1,), (0,)))[0:1]
                dn[q_slots + i][c] = dn[q_slots + i][c] + INV_TEMP * jnp.sum(col * q[j][c], axis=0, keepdims=True)
    r.loss[...] = jnp.broadcast_to(loss / live_total, r.loss.shape)
    r.token[...] = jnp.zeros(r.token.shape, F32)
    for s in range(len(seqs)):
        normed = [r.own_rows[s * parts + c:s * parts + c + 1] for c in range(parts)]
        along = sum(jnp.sum(a * b, axis=1, keepdims=True) for a, b in zip(normed, dn[s]))
        for c in range(parts):
            r.token[s:s + 1, c * 128:(c + 1) * 128] = invs[s] * (dn[s][c] - normed[c] * along) / sizes[s]
    for copy in copies:
        copy.wait_send()


def forward_kernel(seqs, layers, ways, names, *refs):
    r = Refs(**dict(zip(names, refs)))
    z = Weights(r, ways, layers)
    width = r.x.shape[1]
    zpeers = []
    for k in range(1, ways):
        zpeers.append(f"z{k}")
        z.peers[f"z{k}"] = {"mp": lax.rem(lax.axis_index("mp") + k, ways)}
    part = z.part
    def build(l):
        for m in range(3):
            r.pack[l, m * part:(m + 1) * part] = r.qkv_w[l, m]
        r.pack[l, 3 * part:] = r.out_w[l]
    build(0)
    r.tiny[0] = r.tiny_in[...]
    extra = far_peers()
    z.peers.update(extra)
    greet(["core", "x", "y"] + zpeers + list(extra), z.peers)
    def tiny_copy(k):
        return z.remote(r.tiny.at[0], r.tiny.at[k], r.t_send, r.t_recv, k - 1, f"z{k}")
    z.z_copy(0, 0, 1).start()
    for k in range(1, ways):
        tiny_copy(k).start()
    for l in range(1, layers):
        build(l)
    for l in range(layers):
        for j in range(3):
            z.own_copy(l, j).start()
    for s, (start, n) in enumerate(seqs):
        row = lax.broadcasted_iota(jnp.int32, (n, 128), 0)
        r.mask[start:start + n] = jnp.where(row < length(r, ways, s), 0.0, NEG_FILL)
    at = 0
    for ref in (r.q_in, r.p_in):
        for i in range(ref.shape[0]):
            r.xr[at:at + ref.shape[1]] = ref[i]
            r.x[at:at + ref.shape[1]] = ref[i].astype(F32)
            at += ref.shape[1]
    out_b, down_b = r.out_b_in[...].astype(F32), r.down_b_in[...].astype(F32)
    for l in range(layers):
        r.par[l, OB:OB + 1] = out_b[l:l + 1]
        r.par[l, DB:DB + 1] = down_b[l:l + 1]
        r.par[l, GAIN:GAIN + 2] = r.gain_in[l].astype(F32)
        r.par[l, BIAS:BIAS + 2] = r.bias_in[l].astype(F32)
    z.first(0, 0, 1)
    z.z_copy(0, 1, 1).start()
    z.z_copy(0, 2, 1).start()
    z.first(0, 0, 2)
    z.second(0, 0, 1)
    z.first(0, 1, 1)
    z.second(0, 0, 2)
    z.third(0, 0, 1)
    z.first(0, 0, 3)
    z.second(0, 1, 1)
    z.third(0, 0, 2)
    z.first(0, 1, 2)
    z.second(0, 0, 3)
    z.third(0, 1, 1)
    for k in range(1, ways):
        tiny_copy(k).wait_recv()
    for l in range(layers):
        for i in range(2):
            row = r.tiny[0, 2 * l + i:2 * l + i + 1].astype(F32)
            for k in range(1, ways):
                row = row + pltpu.roll(r.tiny[k, 2 * l + i:2 * l + i + 1].astype(F32), k * part, 1)
            r.par[l, i:i + 1] = row
        for k in range(ways):
            r.up_b[l, k] = r.tiny[k, 2 * layers + l:2 * layers + l + 1].astype(F32)
    z.first(0, 2, 1)
    z.second(0, 1, 2)
    z.third(0, 0, 3)
    kept = ("xr", "q", "k", "v", "ctx", "lse", "n1", "r1", "hr", "n2", "r2")
    def keep(l, name):
        return pltpu.make_async_copy(getattr(r, name), getattr(r, name + "_out").at[l], r.k_sem.at[l * len(kept) + kept.index(name)])
    bufs = [r.w_attn, r.w_up, r.w_down]
    def load(l, j):
        return pltpu.make_async_copy(r.w.at[3 * l + j], bufs[j], r.w_sem.at[3 * l + j])
    def save(l, c, j):
        src, dst = ((r.a, r.a_out), (r.slope, r.slope_out))[j]
        return pltpu.make_async_copy(src.at[lax.rem(c, 2)], dst.at[l, c], r.s_sem.at[(l * ways + c) * 2 + j])
    z.arrived(0, 0)
    load(0, 0).start()
    pairs = width // 128
    def layer(l, _):
        f = Forward(l, seqs, r)
        more = l + 1 < layers
        early = z.tick(l, 1) + z.tick(l, 2)
        def up_here():
            z.arrived(l, 1)
            load(l, 1).start()
        early.insert(13, up_here)
        late = z.tick(l, 3)
        def run(ops, n):
            for _ in range(min(n, len(ops))):
                ops.pop(0)()
        keep(l, "xr").start()
        load(l, 0).wait()
        for m in range(3):
            f.project(m)
            keep(l, "qkv"[m]).start()
            run(early, 1)
        def pair(i, _):
            for s in range(len(seqs)):
                f.attend(s, i)
            for at in range(pairs):
                @pl.when(i == at)
                def _():
                    run(early, 2)
            return 0
        lax.fori_loop(0, pairs, pair, 0)
        keep(l, "ctx").start()
        keep(l, "lse").start()
        for b in f.blocks:
            f.out_norm(b)
            run(early, 1)
        for name in ("n1", "r1", "hr"):
            keep(l, name).start()
        run(early, len(early))
        z.arrived(l, 2)
        load(l, 2).start()
        load(l, 1).wait()
        load(l, 2).wait()
        def chunk(c, _):
            @pl.when(c >= 2)
            def _():
                for j in range(2):
                    save(l, c - 2, j).wait()
            for b in f.blocks:
                f.ffn(c, b, lax.rem(c, 2))
            for j in range(2):
                save(l, c, j).start()
            for at in range(ways):
                @pl.when(c == at)
                def _():
                    run(late, 3)
            return 0
        lax.fori_loop(0, ways, chunk, 0)
        for c in range(ways - 2, ways):
            for j in range(2):
                save(l, c, j).wait()
        @pl.when(more)
        def _():
            z.arrived(l + 1, 0)
            load(l + 1, 0).start()
        for name in kept[:-2]:
            keep(l, name).wait()
        @pl.when(l > 0)
        def _():
            for name in kept[-2:]:
                keep(l - 1, name).wait()
        for b in f.blocks:
            f.ffn_norm(b)
        for name in kept[-2:]:
            keep(l, name).start()
        return 0
    lax.fori_loop(0, layers, layer, 0)
    contrast(r, z, seqs, ways, extra)
    def finish(l, _):
        for j in range(3):
            z.sent(l, j)
        return 0
    lax.fori_loop(0, layers, finish, 0)
    for k in range(1, ways):
        tiny_copy(k).wait_send()
    for name in kept[-2:]:
        keep(layers - 1, name).wait()

def forward(query_states, passage_states, qkv_w, out_w, up_w, down_w, q_lens, p_lens, targets, tiny, shared, seqs, ways, collective_id):
    D = query_states.shape[-1]
    T = sum(n for _, n in seqs)
    L = qkv_w.shape[0]
    R = up_w.shape[-1]
    G = 3 * L
    V = pl.BlockSpec(memory_space=pltpu.VMEM)
    S = pl.BlockSpec(memory_space=pltpu.SMEM)
    heads = D // HEAD_DIM
    ins = dict(q_lens=(q_lens, S), p_lens=(p_lens, S), q_in=(query_states, V), p_in=(passage_states, V), qkv_w=(qkv_w, V), out_w=(out_w, V),
               up_w=(up_w, ANY), down_w=(down_w, ANY), tiny_in=(tiny, V))
    for name, value in zip(("out_b_in", "gain_in", "bias_in", "down_b_in"), shared):
        ins[name] = (value, V)
    for name, value in zip(("positive", "q_count", "p_count"), targets):
        ins[name] = (value, S)
    states = dict(xr=((T, D), BF16), q=((T, D), BF16), k=((T, D), BF16), v=((T, D), BF16), ctx=((T, D), BF16),
                  lse=((heads // 2, 8, T), F32), n1=((T, D), F32), r1=((T, 128), F32), hr=((T, D), BF16), n2=((T, D), F32), r2=((T, 128), F32))
    outs = dict(loss=((8, 128), F32, V), token=((-(-len(seqs) // 8) * 8, D), F32, V))
    for name, (shape, kind) in states.items():
        outs[name + "_out"] = ((L, *shape), kind, ANY)
    outs.update(a_out=((L, ways, T, R), BF16, ANY), slope_out=((L, ways, T, R), BF16, ANY), w=((G, ways, 4, R // 4, D), BF16, ANY))
    VM, DMA = pltpu.VMEM, pltpu.SemaphoreType.DMA
    waves = G * (ways - 1)
    scratch = {name: VM(shape, kind) for name, (shape, kind) in states.items()}
    nbits = 0
    while 1 << nbits < lax.axis_size("dp"):
        nbits += 1
    block = -(-(len(seqs) * (D // 128) + 1) // 8) * 8
    scratch.update(
        x=VM((T, D), F32), emb=VM((2,) * nbits + (ways, block, 128), F32), own_rows=VM((block, 128), F32),
        e_send=DMA((nbits + ways,)), e_recv=DMA((nbits + ways,)))
    scratch.update(
        mask=VM((T, 128), F32), par=VM((L, 16, D), F32), up_b=VM((L, ways, 1, R), F32), pack=VM((L, R, D), BF16), tiny=VM((ways, 16, D), BF16),
        a=VM((2, T, R), BF16), slope=VM((2, T, R), BF16),
        w_attn=VM((4, ways, R // 4, D), BF16), w_up=VM((ways, 4, R // 4, D), BF16), w_down=VM((ways, 4, R // 4, D), BF16),
        w_sem=DMA((G,)), s_sem=DMA((L * ways * 2,)), k_sem=DMA((L * 11,)), z_send=DMA((waves,)), z_recv=DMA((waves,)),
        p_send=DMA((waves * 8,)), p_recv=DMA((waves * 8,)), own_send=DMA((G,)), own_recv=DMA((G,)),
        t_send=DMA((ways - 1,)), t_recv=DMA((ways - 1,)))
    names = tuple(ins) + tuple(outs) + tuple(scratch)
    res = pl.pallas_call(
        functools.partial(forward_kernel, seqs, L, ways, names),
        out_shape=[jax.ShapeDtypeStruct(s, d) for s, d, _ in outs.values()],
        in_specs=[s for _, s in ins.values()],
        out_specs=[s for _, _, s in outs.values()],
        scratch_shapes=list(scratch.values()),
        compiler_params=pltpu.CompilerParams(collective_id=collective_id, has_side_effects=True, vmem_limit_bytes=62 << 20),
        name="forward_layers",
    )(*[v for v, _ in ins.values()])
    return {name.removesuffix("_out") if name[:-4] in states else name: value for name, value in zip(outs, res)}


def add_low(a, b):
    return a + b


class Reduce:
    def __init__(self, r, ways, layers):
        self.r, self.ways, self.layers = r, ways, layers
        self.core, self.px, self.py, self.peers = place()
        for k in range(1, ways):
            self.peers[f"z{k}"] = {"mp": lax.rem(lax.axis_index("mp") + k, ways)}
        self.extra = far_peers()
        self.peers.update(self.extra)
        core, px, py = self.core, self.px, self.py
        self.me = spot(core, px, py)
        sx, sy, sd = spot(core, 1 - px, py), spot(core, px, 1 - py), spot(core, 1 - px, 1 - py)
        self.plane = [
            ("x", self.me, sx, None), ("y", self.me, sy, None), ("y", sx, sd, 0), ("x", sy, sd, 1),
            ("core", self.me, spot(1 - core, px, py), None), ("core", sx, spot(1 - core, 1 - px, py), None),
            ("core", sy, spot(1 - core, px, 1 - py), None), ("core", sd, spot(1 - core, 1 - px, 1 - py), None),
        ]
        self.per = 8 + ways - 1 + len(self.extra)
    def remote(self, src, dst, sems, index, peer):
        return pltpu.make_async_remote_copy(
            src_ref=src, dst_ref=dst, send_sem=sems[0].at[index], recv_sem=sems[1].at[index],
            device_id=self.peers[peer], device_id_type=pl.DeviceIdType.MESH)
    def step(self, src, dst, t, j, i, peer):
        return self.remote(src, dst, (self.r.r_send, self.r.r_recv), (3 * t + j) * self.per + i, peer)
    def share(self, t, j, c, i):
        ref = (self.r.g_down, self.r.g_up, self.r.g_attn)[j].at[self.layers - 1 - t]
        return ref.at[2 * c + i] if j == 2 else ref.at[i, pl.ds(2 * c, 2)]
    def place_of(self, ref, j, i):
        return ref.at[:, i] if j == 2 else ref.at[i]
    def pieces(self, j):
        return range(2 if j == 2 else self.ways)
    def load(self, t, j, i):
        return pltpu.make_async_copy(self.share(t, j, self.core, i), self.place_of(self.r.own.at[j], j, i), self.r.l_sem.at[(3 * t + j) * 4 + i])
    def core_copy(self, t, j, i):
        return self.step(self.share(t, j, 1 - self.core, i), self.place_of(self.r.got.at[3 * t + j], j, i), t, j, i, "core")
    def fetch(self, t, j):
        return pltpu.make_async_copy(self.r.got.at[3 * t + j], self.r.got_v, self.r.f_sem.at[3 * t + j])
    def a1(self, t, j):
        return self.step(self.r.own.at[j, :, :, 1 - self.px, 0], self.r.got_a.at[3 * t + j], t, j, 4, "x")
    def b1(self, t, j):
        return self.step(self.r.own.at[j, :, 1 - self.py, :, 1], self.r.got_b.at[3 * t + j], t, j, 5, "y")
    def a2(self, t, j):
        return self.step(self.r.got_a.at[3 * t + j, :, 1 - self.py], self.r.got_c.at[3 * t + j], t, j, 6, "y")
    def b2(self, t, j):
        return self.step(self.r.got_b.at[3 * t + j, :, 1 - self.px], self.r.got_d.at[3 * t + j], t, j, 7, "x")
    def zc(self, t, j, s):
        return self.step(self.r.zout.at[3 * t + j, s - 1], self.r.zin.at[3 * t + j, s - 1], t, j, 7 + s, "z1")
    def slot(self, i):
        return self.ways - 1 if i == 0 else i - 1
    def fc(self, t, j, i, name):
        return self.step(self.r.zout.at[3 * t + j, self.slot(i)], self.r.far.at[3 * t + j, i], t, j, 7 + self.ways + i, name)
    def pc(self, t, j, i, received=False):
        peer, sent, got, h = self.plane[i]
        dst = self.r.reduced.at[3 * t + j, got if received else sent]
        src = self.r.zout.at[3 * t + j, self.slot(len(self.extra))] if i in (0, 1, 4) and not received else dst
        if h is not None:
            src, dst = src.at[h], dst.at[h]
        return self.remote(src, dst, (self.r.g_send, self.r.g_recv), (3 * t + j) * 8 + i, peer)
    def mine(self, t, j):
        return pltpu.make_async_copy(self.r.zout.at[3 * t + j, self.slot(len(self.extra))], self.r.reduced.at[3 * t + j, self.me], self.r.m_sem.at[3 * t + j])
    def s0(self, t, j, i):
        self.core_copy(t, j, i).start()
        self.load(t, j, i).start()
    def s1(self, t, j):
        r = self.r
        for i in self.pieces(j):
            self.core_copy(t, j, i).wait_recv()
        self.fetch(t, j).start()
        for i in self.pieces(j):
            self.load(t, j, i).wait()
        self.fetch(t, j).wait()
        def body(k, _):
            for y in range(2):
                r.own[j, k, y] = add_low(r.own[j, k, y], r.got_v[k, y])
            return 0
        lax.fori_loop(0, self.ways, body, 0)
        self.a1(t, j).start()
        self.b1(t, j).start()
    def s2(self, t, j):
        r, g, px, py = self.r, 3 * t + j, self.px, self.py
        self.a1(t, j).wait_recv()
        def body(k, _):
            for y in range(2):
                r.got_a[g, k, y] = add_low(r.own[j, k, y, px, 0], r.got_a[g, k, y])
            return 0
        lax.fori_loop(0, self.ways, body, 0)
        self.a2(t, j).start()
        self.b1(t, j).wait_recv()
        def body(k, _):
            for x in range(2):
                r.got_b[g, k, x] = add_low(r.own[j, k, py, x, 1], r.got_b[g, k, x])
            return 0
        lax.fori_loop(0, self.ways, body, 0)
        self.b2(t, j).start()
        self.a1(t, j).wait_send()
        self.b1(t, j).wait_send()
    def part(self, g, k):
        r = self.r
        left = add_low(r.got_a[g, k, self.py], r.got_c[g, k])
        right = add_low(r.got_b[g, k, self.px], r.got_d[g, k])
        return left, right
    def s3(self, t, j):
        g = 3 * t + j
        self.a2(t, j).wait_recv()
        self.b2(t, j).wait_recv()
        for h, value in enumerate(self.part(g, 1)):
            self.r.zout[g, 0, h] = value
        self.zc(t, j, 1).start()
    def sz(self, t, j, s):
        r, g = self.r, 3 * t + j
        self.zc(t, j, s).wait_recv()
        for h, value in enumerate(self.part(g, (s + 1) % self.ways)):
            r.zout[g, s, h] = add_low(r.zin[g, s - 1, h], value)
        if s < self.ways - 1:
            self.zc(t, j, s + 1).start()
    def sz1(self, t, j):
        self.sz(t, j, 1)
    def sz2(self, t, j):
        for s in range(2, self.ways - 1):
            self.sz(t, j, s)
    def sp(self, t, j):
        r, g = self.r, 3 * t + j
        self.sz(t, j, self.ways - 1)
        for s in range(1, self.ways):
            self.zc(t, j, s).wait_send()
        for i, name in enumerate(self.extra):
            self.fc(t, j, i, name).start()
            self.fc(t, j, i, name).wait_recv()
            r.zout[g, self.slot(i + 1)] = add_low(r.zout[g, self.slot(i)], r.far[g, i])
        self.mine(t, j).start()
        for i in (0, 1, 4):
            self.pc(t, j, i).start()
    def sq(self, t, j):
        self.pc(t, j, 0, True).wait_recv()
        self.pc(t, j, 2).start()
        self.pc(t, j, 5).start()
        self.pc(t, j, 1, True).wait_recv()
        self.pc(t, j, 3).start()
        self.pc(t, j, 6).start()
    def sr(self, t, j):
        self.pc(t, j, 2, True).wait_recv()
        self.pc(t, j, 3, True).wait_recv()
        self.pc(t, j, 7).start()
    def end(self, t, j):
        for i in range(4, 8):
            self.pc(t, j, i, True).wait_recv()
        self.mine(t, j).wait()
        for i in self.pieces(j):
            self.core_copy(t, j, i).wait_send()
        self.a2(t, j).wait_send()
        self.b2(t, j).wait_send()
        for i, name in enumerate(self.extra):
            self.fc(t, j, i, name).wait_send()
        for i in range(8):
            self.pc(t, j, i).wait_send()


def norm_back(g, n, r, gain):
    gn = g * gain
    return r * (gn - jnp.mean(gn, axis=-1, keepdims=True) - n * jnp.mean(gn * n, axis=-1, keepdims=True))


def total(v):
    return jnp.sum(v, axis=0, keepdims=True)


class Backward:
    def __init__(self, l, seqs, r):
        self.l, self.seqs, self.r = l, seqs, r
        T = r.dy.shape[0]
        self.blocks = [slice(i, i + ROWS) for i in range(0, T, ROWS)]
    def add_row(self, row, value, first):
        r, l = self.r, self.l
        if first:
            r.sums[l, row:row + 1] = value
        else:
            r.sums[l, row:row + 1] += value
    def norm(self, b, which):
        r, l = self.r, self.l
        g = r.dy[b] if which else r.dz[b]
        n, inv = r.n[b], r.inv[b]
        inv = jnp.concatenate([inv] * (n.shape[1] // 128), axis=1)
        dz = norm_back(g, n, inv, r.gain[l, which:which + 1])
        low = dz.astype(BF16)
        r.dz[b] = dz
        r.low[b] = low
        first = b.start == 0
        self.add_row(GAIN + which, total(g * n), first)
        self.add_row(BIAS + which, total(g), first)
        self.add_row(DB if which else OB, total(low.astype(F32)), first)
    def put(self, slot, value):
        stage = self.r.stage
        stage[slot] = value.astype(BF16).reshape(stage.shape[1:])
    def ffn_down(self, slot):
        self.put(0, nn(self.r.low_t[...], self.r.a[slot]))
    def ffn_mid(self, c, b, slot, w):
        r, l = self.r, self.l
        da = nt(r.low[b], r.w[w])
        du = (da * r.slope[slot, b].astype(F32)).astype(BF16)
        r.du[b] = du
        if b.start == 0:
            r.su[l, c] = total(du.astype(F32))
        else:
            r.su[l, c] += total(du.astype(F32))
    def ffn_up(self):
        self.put(1, nn(self.r.hr_t[...], self.r.du[...]))
    def ffn_back(self, b, w):
        r = self.r
        r.dz[b] += nt(r.du[b], r.w[w])
    def context(self, b, w):
        r = self.r
        r.dctx[b] = nt(r.low[b], r.w[w]).astype(BF16)
    def out_grad(self, slot):
        r = self.r
        self.put(slot, nn(r.hc[...].T, r.low[...]))
    def attend(self, s, i):
        r = self.r
        start, n = self.seqs[s]
        rows = slice(start, start + n)
        lanes = pl.ds(pl.multiple_of(i * 128, 128), 128)
        kp, qp, vp, gp = r.k[rows, lanes], r.q[rows, lanes], r.v[rows, lanes], r.dctx[rows, lanes]
        kt = kp.T
        first = lax.broadcasted_iota(jnp.int32, (n, 128), 1) < HEAD_DIM
        bias = jnp.concatenate([r.mask[rows]] * (n // 128), axis=1)
        dv, dk, dq = [], [], []
        for h in range(2):
            keep = first if h == 0 else ~first
            kh = jnp.where(keep, kp, jnp.zeros_like(kp))
            vh = jnp.where(keep, vp, jnp.zeros_like(vp))
            p = jnp.exp(nt(kh, qp) + bias - r.lse[i, h:h + 1, rows])
            dp = nt(vh, gp)
            ds = (p * (dp - jnp.sum(p * dp, axis=0, keepdims=True))).astype(BF16)
            dv.append(nn(p.astype(BF16), gp))
            dk.append(nn(ds, qp))
            dq.append(nn(kt[h * HEAD_DIM:(h + 1) * HEAD_DIM], ds) * 0.125)
        r.dk[rows, lanes] = jnp.where(first, dk[0], dk[1]).astype(BF16)
        r.dv[rows, lanes] = jnp.where(first, dv[0], dv[1]).astype(BF16)
        r.dq[rows, lanes] = jnp.concatenate(dq, axis=0).T.astype(BF16)
    def qkv_grad(self, m, slot):
        r = self.r
        g = (r.dq, r.dk, r.dv)[m][...]
        self.put(slot, nn(g.T, r.du[...]))
        if m != 1:
            self.add_row(QB if m == 0 else VB, total(g.astype(F32)), True)
    def back_in(self, b, m, w):
        r = self.r
        d = nn((r.dq, r.dk, r.dv)[m][b], r.w[w])
        if m == 0:
            r.dy[b] = r.dz[b] + d
        else:
            r.dy[b] += d


def backward_kernel(seqs, layers, ways, names, *refs):
    r = Refs(**dict(zip(names, refs)))
    if r.low_t.shape == r.dy.shape:
        r.dctx, r.dq = r.low_t, r.hr_t
    red = Reduce(r, ways, layers)
    far = list(red.extra)
    greet(["core", "x", "y"] + [f"z{k}" for k in range(1, ways)] + far, red.peers)
    for s, (start, n) in enumerate(seqs):
        row = lax.broadcasted_iota(jnp.int32, (n, 128), 0)
        r.mask[start:start + n] = jnp.where(row < length(r, ways, s), 0.0, NEG_FILL)
    r.gain[...] = r.gain_in[...].astype(F32)
    each = 2 * ways + 4
    heads_order = (3, 0, 1, 2)
    def wload(t, local, group, block):
        return pltpu.make_async_copy(r.w_in.at[group, block], r.w.at[lax.rem(local, 4)], r.w_sem.at[t * each + local])
    def ffn_w(t, c, half):
        return wload(t, 2 * c + half, 3 * (layers - 1 - t) + 2 - half, c)
    def attn_w(t, i):
        return wload(t, 2 * ways + i, 3 * (layers - 1 - t), heads_order[i])
    items = ("n2", "r2", "hr", "n1", "r1", "ctx", "q", "k", "v", "lse", "xr")
    dst = dict(n2=r.n, n1=r.n, r2=r.inv, r1=r.inv, hr=r.hc, ctx=r.hc, q=r.q, k=r.k, v=r.v, lse=r.lse, xr=r.du)
    src = {name: getattr(r, name + "_in") for name in items}
    def load(l, name):
        return pltpu.make_async_copy(src[name].at[l], dst[name], r.i_sem.at[l * len(items) + items.index(name)])
    def aload(l, c, j):
        return pltpu.make_async_copy((r.a_in, r.slope_in)[j].at[l, c], (r.a, r.slope)[j].at[lax.rem(c, 2)], r.a_sem.at[(l * ways + c) * 2 + j])
    def ffn_save(l, c, j):
        return pltpu.make_async_copy(r.stage.at[j], (r.g_down, r.g_up)[j].at[l, c], r.o_sem.at[l * each + 2 * c + j])
    def attn_save(l, m, slot):
        return pltpu.make_async_copy(r.stage.at[slot], r.g_attn.at[l, m], r.o_sem.at[l * each + 2 * ways + m])
    top = layers - 1
    for c in range(2):
        for half in range(2):
            ffn_w(0, c, half).start()
    for name in ("n2", "r2", "hr"):
        load(top, name).start()
    for c in range(2):
        for j in range(2):
            aload(top, c, j).start()
    for name in ("q", "k", "v", "lse"):
        load(top, name).start()
    for s, (start, n) in enumerate(seqs):
        row = lax.broadcasted_iota(jnp.int32, (n, r.dy.shape[1]), 0)
        r.dy[start:start + n] = jnp.where(row < length(r, ways, s), r.token[s:s + 1], 0.0)
    pairs = r.q.shape[1] // 128

    def layer(t, _):
        l = layers - 1 - t
        f = Backward(l, seqs, r)
        after, more = t > 0, t + 1 < layers
        def old(kind, j):
            def go():
                @pl.when(after)
                def _():
                    kind(t - 1, j)
            return go
        def new(kind, j):
            return lambda: kind(t, j)
        def run(ops, n=1):
            for _ in range(min(n, len(ops))):
                ops.pop(0)()
        def again(*nm):
            @pl.when(more)
            def _():
                for x in nm:
                    load(l - 1, x).start()
        ops = [old(*x) for x in (
            (red.s2, 1), (red.sz1, 0), (red.s1, 2), (red.sz2, 0), (red.s3, 1), (red.sp, 0), (red.sz1, 1), (red.sq, 0), (red.s2, 2),
            (red.sz2, 1), (red.sr, 0), (red.s3, 2), (red.sp, 1), (red.sq, 1), (red.sr, 1))]
        load(l, "n2").wait()
        load(l, "r2").wait()
        for b in f.blocks:
            f.norm(b, 1)
            run(ops)
        load(l, "n1").start()
        load(l, "r1").start()
        r.low_t[...] = r.low[...].T
        load(l, "hr").wait()
        r.hr_t[...] = r.hc[...].T
        load(l, "ctx").start()
        def chunk(c, _):
            slot = lax.rem(c, 2)
            w = 2 * slot
            aload(l, c, 0).wait()
            @pl.when(c > 0)
            def _():
                ffn_save(l, c - 1, 0).wait()
                red.s0(t, 0, c - 1)
            f.ffn_down(slot)
            ffn_save(l, c, 0).start()
            aload(l, c, 1).wait()
            ffn_w(t, c, 0).wait()
            for b in f.blocks:
                f.ffn_mid(c, b, slot, w)
            for half in range(2):
                if half == 1:
                    @pl.when(c > 0)
                    def _():
                        ffn_save(l, c - 1, 1).wait()
                        red.s0(t, 1, c - 1)
                    f.ffn_up()
                    ffn_save(l, c, 1).start()
                    ffn_w(t, c, 1).wait()
                    for b in f.blocks:
                        f.ffn_back(b, w + 1)
                @pl.when(c + 2 < ways)
                def _():
                    ffn_w(t, c + 2, half).start()
                for late in range(2):
                    @pl.when(c == ways - 2 + late)
                    def _():
                        attn_w(t, 2 * late + half).start()
                if half == 0:
                    over = (c + 2) // ways
                    @pl.when(l - over >= 0)
                    def _():
                        for j in range(2):
                            aload(l - over, c + 2 - over * ways, j).start()
            for at in range(ways):
                @pl.when(c == at)
                def _():
                    run(ops, 3)
            return 0
        lax.fori_loop(0, ways, chunk, 0)
        load(l, "xr").start()
        ops = [new(red.s1, 0), new(red.s1, 1), old(red.sz1, 2), old(red.sz2, 2), old(red.sp, 2), new(red.s2, 0), old(red.sq, 2), new(red.s3, 0), old(red.sr, 2)]
        for j in range(2):
            ffn_save(l, ways - 1, j).wait()
            red.s0(t, j, ways - 1)
        load(l, "n1").wait()
        load(l, "r1").wait()
        for b in f.blocks:
            f.norm(b, 0)
        again("n2", "r2")
        run(ops)
        attn_w(t, 0).wait()
        for b in f.blocks:
            f.context(b, 0)
        @pl.when(more)
        def _():
            ffn_w(t + 1, 0, 0).start()
        run(ops)
        load(l, "ctx").wait()
        f.out_grad(0)
        attn_save(l, 3, 0).start()
        again("hr")
        for nm in ("q", "k", "v", "lse"):
            load(l, nm).wait()
        def pair(i, _):
            for s in range(len(seqs)):
                f.attend(s, i)
            for at in (0, 2, 4):
                @pl.when(i == at)
                def _():
                    run(ops)
            return 0
        lax.fori_loop(0, pairs, pair, 0)
        again("q", "k", "v", "lse")
        load(l, "xr").wait()
        for m in range(3):
            slot = (m + 1) % 2
            if m == 1:
                attn_save(l, 3, 0).wait()
            if m == 2:
                attn_save(l, 0, 1).wait()
            f.qkv_grad(m, slot)
            attn_save(l, m, slot).start()
            run(ops)
        run(ops, len(ops))
        attn_save(l, 1, 0).wait()
        attn_save(l, 2, 1).wait()
        for i in red.pieces(2):
            red.s0(t, 2, i)
        for m in range(3):
            attn_w(t, m + 1).wait()
            for b in f.blocks:
                f.back_in(b, m, m + 1)
            @pl.when(more)
            def _():
                ffn_w(t + 1, (m + 1) // 2, (m + 1) % 2).start()
        return 0
    lax.fori_loop(0, layers, layer, 0)

    names_dp = ["core", "x", "y"] + far
    for l in range(layers):
        r.small[0, l] = r.sums[l]
        for c in range(ways):
            r.small[0, l, UB + c:UB + c + 1] = r.su[l, c]
    def sd(i):
        return red.remote(r.small.at[i], r.small_in.at[i], (r.v_send, r.v_recv), i, names_dp[i])
    def sm(k):
        n = len(names_dp)
        return red.remote(r.small.at[n], r.small_in.at[n + k - 1], (r.v_send, r.v_recv), n + k - 1, f"z{k}")
    def small_step(i):
        def go():
            if i > 0:
                sd(i - 1).wait_recv()
                r.small[i] = r.small[i - 1] + r.small_in[i - 1]
            if i < len(names_dp):
                sd(i).start()
            else:
                for k in range(1, ways):
                    sm(k).start()
        return go
    def small_end():
        n = len(names_dp)
        for k in range(1, ways):
            sm(k).wait_recv()
        v = [r.small.at[n]] + [r.small_in.at[n + k - 1] for k in range(1, ways)]
        for l in range(layers):
            part = v[0].shape[-1] // ways
            even, odd = v[0][l], v[1][l]
            for k in range(2, ways):
                if k % 2:
                    odd = odd + v[k][l]
                else:
                    even = even + v[k][l]
            r.small_out[l] = even + odd
            split, up = None, None
            for k in range(ways):
                back = (ways - k) % ways
                row = v[k][l, QB:VB + 1]
                if back:
                    row = pltpu.roll(row, (ways - back) * part, 1)
                split = row if split is None else split + row
                one = v[k][l, UB + back:UB + back + 1]
                up = one if up is None else up + one
            r.small_out[l, QB:VB + 1] = split
            r.small_out[l, UB:UB + 1] = up
    t = layers - 1
    a, b, c = 0, 1, 2
    tail = [(red.s2, b), (red.sz1, a), (red.s1, c), (red.sz2, a), (red.s3, b), (red.sp, a), (red.sz1, b), (red.s2, c), (red.sq, a), (red.sz2, b),
            (red.s3, c), (red.sr, a), (red.sp, b), (red.sz1, c), (red.sq, b), (red.sz2, c), (red.sr, b), (red.sp, c), (red.sq, c), (red.sr, c)]
    smalls = [small_step(i) for i in range(len(names_dp) + 1)]
    for i, (kind, j) in enumerate(tail):
        kind(t, j)
        if smalls and i % 2 == 0:
            smalls.pop(0)()
    for go in smalls:
        go()
    small_end()
    def finish(t, _):
        for j in range(3):
            red.end(t, j)
        return 0
    lax.fori_loop(0, layers, finish, 0)
    for i in range(len(names_dp)):
        sd(i).wait_send()
    for k in range(1, ways):
        sm(k).wait_send()


def backward(saved, w, q_lens, p_lens, gain, seqs, collective_id):
    T, D = saved["q"].shape[1:]
    G, ways, R, _ = w.shape
    L = G // 3
    V = pl.BlockSpec(memory_space=pltpu.VMEM)
    S = pl.BlockSpec(memory_space=pltpu.SMEM)
    ins = dict(q_lens=(q_lens, S), p_lens=(p_lens, S), token=(saved["token"], V), w_in=(w, ANY), gain_in=(gain, V))
    for n in ("n2", "r2", "hr", "n1", "r1", "ctx", "q", "k", "v", "lse", "xr"):
        ins[n + "_in"] = (saved[n], ANY)
    ins["a_in"] = (saved["a_out"], ANY)
    ins["slope_in"] = (saved["slope_out"], ANY)
    half = R // 16
    block = (2, 2, half, D)
    outs = dict(
        dy=((T, D), F32, V), small_out=((L, 16, D), F32, V), reduced=((G, 8, 2, half, D), BF16, ANY),
        g_down=((L, ways, 4, *block), BF16, ANY), g_up=((L, ways, 4, *block), BF16, ANY), g_attn=((L, 4, ways, *block), BF16, ANY),
        got=((G, ways, 2, *block), BF16, ANY))
    H = saved["lse"].shape[1]
    nfar = 0
    while 8 << nfar < lax.axis_size("dp"):
        nfar += 1
    VM, DMA = pltpu.VMEM, pltpu.SemaphoreType.DMA
    per = 8 + ways - 1 + nfar
    steps = 3 + nfar
    each = 2 * ways + 4
    scratch = dict(
        gain=VM(gain.shape, F32), mask=VM((T, 128), F32), n=VM((T, D), F32), inv=VM((T, 128), F32), hc=VM((T, D), BF16), hr_t=VM((D, T), BF16),
        low=VM((T, D), BF16), low_t=VM((D, T), BF16), dz=VM((T, D), F32), du=VM((T, R), BF16),
        a=VM((2, T, R), BF16), slope=VM((2, T, R), BF16), q=VM((T, D), BF16), k=VM((T, D), BF16), v=VM((T, D), BF16),
        lse=VM((H, 8, T), F32), dk=VM((T, D), BF16), dv=VM((T, D), BF16),
        stage=VM((2, 4, *block), BF16), w=VM((4, R, D), BF16), sums=VM((L, 16, D), F32), su=VM((L, ways, 1, R), F32),
        own=VM((3, ways, 2, *block), BF16), got_v=VM((ways, 2, *block), BF16),
        got_a=VM((G, ways, 2, half, D), BF16), got_b=VM((G, ways, 2, half, D), BF16),
        got_c=VM((G, ways, half, D), BF16), got_d=VM((G, ways, half, D), BF16),
        zin=VM((G, ways - 1, 2, half, D), BF16), zout=VM((G, ways, 2, half, D), BF16),
        small=VM((steps + 1, L, 16, D), F32), small_in=VM((steps + ways - 1, L, 16, D), F32),
        w_sem=DMA((L * each,)), i_sem=DMA((L * 11,)), a_sem=DMA((L * ways * 2,)), o_sem=DMA((L * each,)),
        l_sem=DMA((G * 4,)), f_sem=DMA((G,)), m_sem=DMA((G,)), r_send=DMA((G * per,)), r_recv=DMA((G * per,)),
        g_send=DMA((G * 8,)), g_recv=DMA((G * 8,)), v_send=DMA((steps + ways - 1,)), v_recv=DMA((steps + ways - 1,)))
    if T != D:
        scratch["dctx"] = VM((T, D), BF16)
        scratch["dq"] = VM((T, D), BF16)
    if nfar:
        scratch["far"] = VM((G, nfar, 2, half, D), BF16)
    names = tuple(ins) + tuple(outs) + tuple(scratch)
    res = pl.pallas_call(
        functools.partial(backward_kernel, seqs, L, ways, names),
        out_shape=[jax.ShapeDtypeStruct(s, d) for s, d, _ in outs.values()],
        in_specs=[s for _, s in ins.values()],
        out_specs=[s for _, _, s in outs.values()],
        scratch_shapes=list(scratch.values()),
        compiler_params=pltpu.CompilerParams(collective_id=collective_id, has_side_effects=True, vmem_limit_bytes=255 << 18),
        name="backward_layers",
    )(*[v for v, _ in ins.values()])
    return dict(zip(outs, res))


def finish_kernel(reduced, dy, small, qkv, out, up, down, q_grad, p_grad, qv_bias, out_bias, gain, bias, up_bias, down_bias):
    part = out.shape[1]
    attn = reduced[2].astype(F32)
    qkv[0] = attn[:3 * part]
    out[0] = attn[3 * part:]
    up[0] = reduced[1].astype(F32)
    down[0] = reduced[0].astype(F32).T

    @pl.when(pl.program_id(0) == 0)
    def _():
        rows = q_grad.shape[0]
        q_grad[...] = dy[:rows]
        p_grad[...] = dy[rows:]
        for l in range(small.shape[0]):
            qv_bias[l] = small[l, QB:VB + 1, :part]
            out_bias[l:l + 1] = small[l, OB:OB + 1]
            gain[l] = small[l, GAIN:GAIN + 2]
            bias[l] = small[l, BIAS:BIAS + 2]
            up_bias[l:l + 1] = small[l, UB:UB + 1, :up_bias.shape[1]]
            down_bias[l:l + 1] = small[l, DB:DB + 1]


def finish(reduced, dy, small, layers, part, rows):
    G, R, D = reduced.shape
    T = dy.shape[0]
    per_layer = [(3 * part, D), (part, D), (D, R), (R, D)]
    once = [(rows, D), (T - rows, D), (layers, 2, part), (layers, D), (layers, 2, D), (layers, 2, D), (layers, R), (layers, D)]
    whole = lambda shape: pl.BlockSpec(shape, lambda l: (0,) * len(shape))
    return pl.pallas_call(
        finish_kernel,
        grid=(layers,),
        out_shape=[jax.ShapeDtypeStruct((layers, *s), F32) for s in per_layer] + [jax.ShapeDtypeStruct(s, F32) for s in once],
        in_specs=[pl.BlockSpec((3, R, D), lambda l: (layers - 1 - l, 0, 0)), whole(dy.shape), whole(small.shape)],
        out_specs=[pl.BlockSpec((1, *s), lambda l: (l, 0, 0)) for s in per_layer] + [whole(s) for s in once],
        compiler_params=pltpu.CompilerParams(vmem_limit_bytes=60 << 20),
        name="finish",
    )(reduced, dy, small)


def local(
    query_states,
    passage_states,
    query_lengths,
    passage_lengths,
    query_count,
    passage_count,
    positive,
    query_key_value_matrix,
    qv_bias,
    out_weight,
    out_bias,
    norm_gain,
    norm_bias,
    up_matrix,
    up_bias,
    down_matrix,
    down_bias,
):
    layers = query_key_value_matrix.shape[0]
    width = query_states.shape[-1]
    ways = lax.axis_size("mp")
    q_slots, q_len, _ = query_states.shape
    p_slots, p_len, _ = passage_states.shape
    shapes = ((q_slots, q_len), (p_slots, p_len))
    part = qv_bias.shape[-1]

    hidden = up_bias.shape[-1]
    tiny = jnp.concatenate(
        [
            jnp.pad(qv_bias.reshape(2 * layers, part), ((0, 0), (0, width - part))),
            up_bias,
            jnp.zeros((16 - 3 * layers, width), BF16),
        ]
    )
    seqs, at = [], 0
    for count, length in shapes:
        for _ in range(count):
            seqs.append((at, length))
            at += length
    seqs = tuple(seqs)
    saved = forward(
        query_states, passage_states, jnp.swapaxes(query_key_value_matrix, 2, 3), out_weight, up_matrix, down_matrix,
        query_lengths, passage_lengths, (positive, query_count, passage_count), tiny, (out_bias, norm_gain, norm_bias, down_bias), seqs, ways, 0,
    )
    loss = saved["loss"][0, 0]
    back = backward(
        saved, saved["w"].reshape(3 * layers, 4, -1, width), query_lengths, passage_lengths, norm_gain, seqs, 1
    )
    reduced = back["reduced"].reshape(3 * layers, -1, width)
    qkv_grad, out_grad, up_grad, down_grad, query_grad, passage_grad, qv_b, out_b, gain_g, bias_g, up_b, down_b = finish(
        reduced, back["dy"], back["small_out"], layers, part, q_slots * q_len
    )
    qkv_grad = jnp.swapaxes(qkv_grad.reshape(layers, 3, part, width), 2, 3)
    query_grad = query_grad.reshape(query_states.shape)
    passage_grad = passage_grad.reshape(passage_states.shape)
    return (
        loss, query_grad, passage_grad, qkv_grad, qv_b, out_grad, out_b, gain_g, bias_g, up_grad, up_b, down_grad, down_b
    )


def solution(mesh):
    placed = (
        P(("dp", "mp"), None, None),
        P(("dp", "mp"), None, None),
        P("dp"),
        P("dp"),
        P(),
        P(),
        P(("dp", "mp")),
        P(None, None, None, "mp"),
        P(None, None, "mp"),
        P(None, "mp", None),
        P(),
        P(),
        P(),
        P(None, None, "mp"),
        P(None, "mp"),
        P(None, "mp", None),
        P(),
    )
    return jax.shard_map(
        local,
        mesh=mesh,
        in_specs=placed,
        out_specs=(
            P(),
            P(("dp", "mp"), None, None),
            P(("dp", "mp"), None, None),
            P(None, None, None, "mp"),
            P(None, None, "mp"),
            P(None, "mp", None),
            P(),
            P(),
            P(),
            P(None, None, "mp"),
            P(None, "mp"),
            P(None, "mp", None),
            P(),
        ),
        check_vma=False,
    )
```
